32 devices in a mesh: space: 8 (over y, x, core), freq: 4 (over z).
Axes of the slice: x: 2, y: 2, z: 4, core: 2. Of those that a mesh axis runs over, the one named last changes fastest.
Arguments:
- snapshots: bfloat16 [32768, 1024], P('space', 'freq'), may hold values from -6 to 6
- tail: bfloat16 [32768, 128], P('space'), may hold values from -6 to 6
Outputs:
- gram: float32 [16, 2, 8, 8], P('freq', None, 'space')
- spectrum: float32 [16], P('freq')
The draws below stay inside these ranges and needn't reach their ends.
All inputs are finite; a program needn't handle non-finite values.
Results may differ from the reference program's by a relative error of at most 0.0038.
Values may be sent and summed in bfloat16 or wider, within the bound.
A program may use at most 64 MiB of HBM per device.

```python
import math
import jax
import jax.numpy as jnp
from jax import lax

PTS_DEV = 4096
NFFT = 256
POWER = 4
HALF = 128
POINTS = 32768
NB = 8
NF = 16
SNAPS = 1024
N_SPACE = 8


def steps_of(stream_key, dims, split, least, top_value):
    factor_of = 1.0
    for dim, shards_of in split:
        heights = jax.random.uniform(jax.random.fold_in(jax.random.fold_in(stream_key, 6), dim), (shards_of,), jnp.float32, least / len(split), top_value / len(split))
        factor_of = factor_of * jnp.repeat(jnp.exp(heights), dims[dim] // shards_of).reshape((-1,) + (1,) * (len(dims) - 1 - dim))
    return factor_of


def bell_draw(stream_key, extent, deviation, most, pieces=(), held_as=jnp.bfloat16):
    drawn = jax.random.normal(stream_key, extent, jnp.float32) * deviation
    if len(pieces) > 0:
        drawn = steps_of(stream_key, extent, pieces, -0.22, 0.18) * drawn
    return jnp.clip(drawn, min=-most, max=most).astype(held_as)


def setup_inputs(seed: int = 0) -> dict:
    seeds = jax.random.split(jax.random.key(seed), 3)
    return {
        "snapshots": bell_draw(seeds[0], (POINTS, SNAPS), 1.0, 6.0, ((0, 8), (1, 4))),
        "tail": bell_draw(seeds[1], (POINTS, HALF), 1.0, 6.0, ((0, 8),)),
    }


def build_table(count):
    steps = jnp.arange(NFFT, dtype=jnp.int32)
    freqs = jnp.arange(count, dtype=jnp.int32)
    window = 0.5 - 0.5 * jnp.cos(2.0 * math.pi * steps.astype(jnp.float32) / NFFT)
    phase = 2.0 * math.pi * (steps[:, None] * freqs[None, :] % NFFT).astype(jnp.float32) / NFFT
    table = jnp.concatenate([window[:, None] * jnp.cos(phase), -window[:, None] * jnp.sin(phase)], 1)
    return (table.astype(jnp.bfloat16), jnp.sum(window * window))

def apply_matrix(matrix, vector):
    high = lax.Precision.HIGHEST
    m_real, m_imag = (matrix[:, 0], matrix[:, 1])
    v_real, v_imag = (vector[:, 0], vector[:, 1])
    u_real = jnp.einsum('fjk,fk->fj', m_real, v_real, precision=high) - jnp.einsum('fjk,fk->fj', m_imag, v_imag, precision=high)
    u_imag = jnp.einsum('fjk,fk->fj', m_real, v_imag, precision=high) + jnp.einsum('fjk,fk->fj', m_imag, v_real, precision=high)
    return jnp.stack([u_real, u_imag], 1)

def rescale(product):
    return product / jnp.sqrt(lax.optimization_barrier(jnp.mean(product * product, axis=(1, 2), keepdims=True)) + 1e-06)

def rayleigh(vector, product):
    return lax.optimization_barrier(jnp.mean(vector * product, axis=(1, 2))) / (lax.optimization_barrier(jnp.mean(vector * vector, axis=(1, 2))) + 1e-06)

def reference(snapshots, tail):
    pressure = jnp.concatenate([snapshots, tail], 1)
    table, wsum = build_table(NF)
    table_wide = table.astype(jnp.float32)
    high = lax.Precision.HIGHEST

    def span_gram(total, index):
        rows = lax.dynamic_slice_in_dim(pressure, index * PTS_DEV, PTS_DEV, 0)
        halves = rows.reshape(PTS_DEV, NB + 1, HALF)
        blocks = jnp.concatenate([halves[:, :-1], halves[:, 1:]], 2).astype(jnp.float32)
        coef = jnp.einsum('pbt,tk->bkp', blocks, table_wide, precision=high)
        coef = coef.astype(jnp.bfloat16).astype(jnp.float32).reshape(NB, 2, NF, PTS_DEV)
        big = jnp.einsum('bcfp,gdfp->fcbdg', coef, coef, precision=high)
        return (total + big, None)
    start = jnp.zeros((NF, 2, NB, 2, NB), jnp.float32)
    big, unused = lax.scan(span_gram, start, jnp.arange(N_SPACE, dtype=jnp.int32))
    real = big[:, 0, :, 0, :] + big[:, 1, :, 1, :]
    imag = big[:, 0, :, 1, :] - big[:, 1, :, 0, :]
    gram = jnp.stack([real, imag], 1) / (POINTS * wsum)
    vector = jnp.stack([jnp.ones((NF, NB), jnp.float32), jnp.zeros((NF, NB), jnp.float32)], 1)
    for step in range(POWER):
        vector = rescale(apply_matrix(gram, vector))
    spectrum = rayleigh(vector, apply_matrix(gram, vector))
    return (gram, spectrum)
```

```python
import functools
import math

import jax
import jax.numpy as jnp
import ml_dtypes
import numpy as np
from jax import lax
from jax.experimental import pallas as pl
from jax.experimental.pallas import tpu as pltpu
from jax.sharding import PartitionSpec as P

FREQ_DEV = 4
NFFT = 256
POWER = 4
LANES = 128
SUBS = 2
MESH = pl.DeviceIdType.MESH


def shifted(value, axis, steps):
    count = lax.axis_size(axis)
    initial, last = (max(0, -steps), min(count, count - steps))
    return lax.ppermute(value, axis, [(source, source + steps) for source in range(initial, last)])


def build_table(count):
    steps = jnp.arange(NFFT, dtype=jnp.int32)
    freqs = jnp.arange(count, dtype=jnp.int32)
    window = 0.5 - 0.5 * jnp.cos(2.0 * math.pi * steps.astype(jnp.float32) / NFFT)
    phase = 2.0 * math.pi * (steps[:, None] * freqs[None, :] % NFFT).astype(jnp.float32) / NFFT
    table = jnp.concatenate(
        [window[:, None] * jnp.cos(phase), -window[:, None] * jnp.sin(phase)], 1
    )
    return (table.astype(jnp.bfloat16), jnp.sum(window * window))


def transform(extended, table):
    points, width = extended.shape
    half = NFFT // 2
    count = width // half - 1
    halves = extended.reshape(points, count + 1, half)
    blocks = jnp.concatenate([halves[:, :-1], halves[:, 1:]], 2)
    coef = jnp.einsum("pbt,tk->bkp", blocks, table, preferred_element_type=jnp.float32)
    return coef.reshape(count, 2, table.shape[1] // 2, points).astype(jnp.bfloat16)


def gram_terms(coef, scale):
    big = jnp.einsum("bcfp,gdfp->fcbdg", coef, coef, preferred_element_type=jnp.float32)
    real = big[:, 0, :, 0, :] + big[:, 1, :, 1, :]
    imag = big[:, 0, :, 1, :] - big[:, 1, :, 0, :]
    return jnp.stack([real, imag], 1) * scale


def apply_matrix(matrix, vector):
    high = lax.Precision.HIGHEST
    m_real, m_imag = (matrix[:, 0], matrix[:, 1])
    v_real, v_imag = (vector[:, 0], vector[:, 1])
    u_real = jnp.einsum("fjk,fk->fj", m_real, v_real, precision=high) - jnp.einsum(
        "fjk,fk->fj", m_imag, v_imag, precision=high
    )
    u_imag = jnp.einsum("fjk,fk->fj", m_real, v_imag, precision=high) + jnp.einsum(
        "fjk,fk->fj", m_imag, v_real, precision=high
    )
    return jnp.stack([u_real, u_imag], 1)


def rescale(product):
    return product / jnp.sqrt(jnp.mean(product * product, axis=(1, 2), keepdims=True) + 1e-06)


def rayleigh(vector, product):
    return jnp.mean(vector * product, axis=(1, 2)) / (
        jnp.mean(vector * vector, axis=(1, 2)) + 1e-06
    )


def shards_general(snapshots, tail):
    points = snapshots.shape[0]
    freq_count = lax.axis_size("freq")
    half = NFFT // 2
    table, wsum = build_table(FREQ_DEV * freq_count)
    scale = 1.0 / (points * lax.axis_size("space") * wsum)
    following = shifted(snapshots[:, :half], "freq", -1)
    is_last = lax.axis_index("freq") == freq_count - 1
    following = jnp.where(is_last, tail, following)
    extended = jnp.concatenate([snapshots, following], 1)
    coef = transform(extended, table)
    regrouped = lax.all_to_all(coef, "freq", split_axis=2, concat_axis=0, tiled=True)
    partial_value = gram_terms(regrouped, scale)
    blocks_all = partial_value.shape[2]
    held = blocks_all // lax.axis_size("space")
    vector = jnp.stack(
        [
            jnp.ones((FREQ_DEV, blocks_all), jnp.float32),
            jnp.zeros((FREQ_DEV, blocks_all), jnp.float32),
        ],
        1,
    )
    total = lax.psum(partial_value, "space")
    for step in range(POWER):
        vector = rescale(apply_matrix(total, vector))
    spectrum = rayleigh(vector, apply_matrix(total, vector))
    gram_rows = lax.dynamic_slice_in_dim(total, lax.axis_index("space") * held, held, 2)
    return (gram_rows, spectrum)


def two_pieces(values):
    high = values.astype(ml_dtypes.bfloat16)
    low = (values - high.astype(np.float64)).astype(ml_dtypes.bfloat16)
    return np.concatenate([high, low], 0)


def half_rows(nf):
    steps = np.arange(NFFT // 2)
    phase = 2.0 * np.pi * (np.arange(nf + 1)[:, None] * steps[None, :] % NFFT) / NFFT
    real, imag = np.cos(phase), -np.sin(phase)
    main = np.concatenate([real[:nf], imag[:nf]], 0)
    main[nf] = real[nf]
    return main, imag[nf : nf + 1]


def make_tables(nf, pieces):
    main, extra = half_rows(nf)
    half = NFFT // 2
    width = 2 * nf
    both = np.zeros((2 * width + 2 * pieces, NFFT))
    for h in range(2):
        both[h * width : (h + 1) * width, h * half : (h + 1) * half] = main
        both[2 * width + h :: 2, h * half : (h + 1) * half] = extra
    last = np.zeros((width + 16, half))
    last[:width] = main
    last[width] = extra[0]
    return two_pieces(both), two_pieces(last)


def make_combine(nf, nb, pieces):
    width = 2 * nf
    main_rows = nb * width
    ext_rows = nb * pieces
    combine = np.zeros((2, nf, nb, main_rows + ext_rows + width + 16))

    def columns(m, f, part):
        if f == nf and part == 1:
            if m == nb:
                return [main_rows + ext_rows + width]
            first = main_rows + m // 2 * 2 * pieces + m % 2
            return [first + 2 * q for q in range(pieces)]
        start = main_rows + ext_rows if m == nb else m * width
        if f == nf:
            return [start + nf]
        if part == 1 and f == 0:
            return []
        return [start + part * nf + f]

    for f in range(nf):
        for b in range(nb):
            for m in (b, b + 1):
                second = m - b
                sign = (-1.0) ** f if second else 1.0
                side = 0.25 if second else -0.25
                for part in range(2):
                    for g, weight in ((f, 0.5), (f - 1, side), (f + 1, side)):
                        flip = -1.0 if g < 0 and part == 1 else 1.0
                        for column in columns(m, abs(g), part):
                            combine[part, f, b, column] += sign * flip * weight
    return combine.reshape(2 * nf * nb, -1).astype(ml_dtypes.bfloat16)


def xor_index(index, other, count):
    result = 0
    bit = 1
    while bit < count:
        digit = lax.rem(index // bit, 2)
        result = result + bit * ((1 - digit) if other & bit else digit)
        bit *= 2
    return result


def nt_dot(left, right):
    return lax.dot_general(
        left, right, (((1,), (1,)), ((), ())), preferred_element_type=jnp.float32
    )


def leading_value(g_re, g_im, nb):
    shape = g_re.shape
    row = lax.broadcasted_iota(jnp.int32, shape, 0)
    lane = lax.broadcasted_iota(jnp.int32, shape, 1)
    entries = 2.0 * nb

    def lane_sum(x):
        step = 1
        while step < nb:
            ahead = pltpu.roll(x, LANES - step, 1)
            behind = pltpu.roll(x, step, 1)
            x = x + jnp.where(lane % (2 * step) < step, ahead, behind)
            step *= 2
        return x

    def row_sum(x):
        return jnp.broadcast_to(jnp.sum(x, axis=0, keepdims=True), shape)

    def to_lanes(v_re, v_im):
        return row_sum(g_re * v_re + g_im * v_im), row_sum(g_re * v_im - g_im * v_re)

    def to_rows(v_re, v_im):
        return lane_sum(g_re * v_re - g_im * v_im), lane_sum(g_re * v_im + g_im * v_re)

    v_re, v_im = jnp.ones(shape, jnp.float32), jnp.zeros(shape, jnp.float32)
    for step in range(POWER):
        if step % 2 == 0:
            u_re, u_im = to_lanes(v_re, v_im)
            mean = lane_sum(u_re * u_re + u_im * u_im) / entries
        else:
            u_re, u_im = to_rows(v_re, v_im)
            mean = row_sum(u_re * u_re + u_im * u_im) / entries
        size = jnp.sqrt(mean + 1e-06)
        v_re, v_im = u_re / size, u_im / size
    u_re, u_im = to_lanes(v_re, v_im)
    here = lane % nb == row
    across_re = row_sum(jnp.where(here, v_re, 0.0))
    across_im = row_sum(jnp.where(here, v_im, 0.0))
    top = lane_sum(across_re * u_re + across_im * u_im) / entries
    return top / (row_sum(v_re * v_re + v_im * v_im) / entries + 1e-06)


def kernel(
    zs, ns, nf, nb, scale,
    snap_ref, tail_ref, table_ref, tail_table_ref, combine_ref, out_ref,
    x_buf, tail_buf, table, tail_table, combine,
    send, send_ext, recv, recv_ext, z_part, z_recv, s_recv,
    x_sem, const_sem, send_sem, recv_sem, ext_send_sem, ext_recv_sem,
    z_send_sem, z_recv_sem, s_send_sem, s_recv_sem,
):
    my_s, my_z = lax.axis_index("space"), lax.axis_index("freq")
    quarter = snap_ref.shape[0] // zs
    sub = quarter // SUBS
    width = 2 * nf
    pieces = sub // LANES
    order = list(range(zs // 2, zs)) + list(range(1, zs // 2))
    peers = {k: xor_index(my_z, k, zs) for k in order}
    peers[0] = my_z
    friends = {k: xor_index(my_s, k, ns) for k in range(1, ns)}

    loads = {}
    constants = [
        pltpu.make_async_copy(table_ref, table, const_sem.at[0]),
        pltpu.make_async_copy(tail_table_ref, tail_table, const_sem.at[1]),
        pltpu.make_async_copy(combine_ref, combine, const_sem.at[2]),
        pltpu.make_async_copy(
            tail_ref.at[pl.ds(pl.multiple_of(my_z * quarter, quarter), quarter)],
            tail_buf, const_sem.at[3],
        ),
    ]
    constants[0].start()
    for s in range(SUBS):
        for k in order + [0]:
            first = pl.multiple_of(peers[k] * quarter + s * sub, sub)
            loads[k, s] = pltpu.make_async_copy(
                snap_ref.at[pl.ds(first, sub)], x_buf.at[k, s], x_sem.at[k, s]
            )
            loads[k, s].start()
    for copy in constants[1:]:
        copy.start()

    barrier = pltpu.get_barrier_semaphore()
    for k in order:
        pl.semaphore_signal(barrier, inc=1, device_id=(my_s, peers[k]), device_id_type=MESH)
    for k in range(1, ns):
        pl.semaphore_signal(barrier, inc=1, device_id=(friends[k], my_z), device_id_type=MESH)

    ext_row = lax.broadcasted_iota(jnp.int32, (2 * pieces, LANES), 0) // 2

    def transform(k, s):
        loads[k, s].wait()
        both = nt_dot(table[...], x_buf[k, s])
        rows = both.shape[0] // 2
        both = both[:rows] + both[rows:]
        extra = jnp.zeros((2 * pieces, LANES), jnp.float32)
        for q in range(pieces):
            extra = jnp.where(
                ext_row == q, both[2 * width :, q * LANES : (q + 1) * LANES], extra
            )
        return both[: 2 * width].astype(jnp.bfloat16), extra

    constants[0].wait()
    copies = {}
    for s in range(SUBS):
        for k in order:
            main, extra = transform(k, s)
            send[k, s] = main
            send_ext[k, s] = extra
            if s == 0 and k == order[0]:
                pl.semaphore_wait(barrier, zs - 1 + ns - 1)
            target = (my_s, peers[k])
            copies[k, s] = [
                pltpu.make_async_remote_copy(
                    send_ext.at[k, s], recv_ext.at[my_z, s],
                    ext_send_sem.at[k, s], ext_recv_sem.at[k, s],
                    device_id=target, device_id_type=MESH,
                ),
                pltpu.make_async_remote_copy(
                    send.at[k, s], recv.at[my_z, s],
                    send_sem.at[k, s], recv_sem.at[k, s],
                    device_id=target, device_id_type=MESH,
                ),
            ]
            for copy in copies[k, s]:
                copy.start()
    for s in range(SUBS):
        main, extra = transform(0, s)
        recv[my_z, s] = main
        recv_ext[my_z, s] = extra
    for copy in constants[1:]:
        copy.wait()

    gram = jnp.zeros((width * nb, width * nb), jnp.float32)
    for s in range(SUBS):
        last = nt_dot(tail_table[...], tail_buf[s * sub : (s + 1) * sub])
        rows = last.shape[0] // 2
        last = (last[:rows] + last[rows:]).astype(jnp.bfloat16)
        for k in order:
            for copy in copies[k, s]:
                copy.wait_recv()
        extras = []
        for d in range(zs):
            extra = recv_ext[d, s]
            extras.append(
                jnp.concatenate([jnp.where(ext_row == q, extra, 0.0) for q in range(pieces)], 1)
            )
        stacked = jnp.concatenate(
            [recv[d, s] for d in range(zs)]
            + [jnp.concatenate(extras, 0).astype(jnp.bfloat16), last],
            0,
        )
        coef = jnp.dot(combine[...], stacked, preferred_element_type=jnp.float32)
        coef = coef.astype(jnp.bfloat16)
        gram = gram + nt_dot(coef, coef)

    side = nf * nb
    real = gram[:side, :side] + gram[side:, side:]
    imag = gram[:side, side:] - gram[side:, :side]
    lane_freq = lax.broadcasted_iota(jnp.int32, (nb, side), 1) // nb
    g_re = jnp.zeros((nb, side), jnp.float32)
    g_im = jnp.zeros((nb, side), jnp.float32)
    for f in range(nf):
        g_re = jnp.where(lane_freq == f, real[f * nb : (f + 1) * nb], g_re)
        g_im = jnp.where(lane_freq == f, imag[f * nb : (f + 1) * nb], g_im)
    z_part[0] = g_re * scale
    z_part[1] = g_im * scale

    z_copies = []
    for k in order:
        copy = pltpu.make_async_remote_copy(
            z_part, z_recv.at[k], z_send_sem.at[k], z_recv_sem.at[k],
            device_id=(my_s, peers[k]), device_id_type=MESH,
        )
        copy.start()
        z_copies.append(copy)
    total = z_part[...]
    for k, copy in zip(order, z_copies):
        copy.wait_recv()
        total = total + z_recv[k]
    s_recv[my_s] = total
    s_copies = []
    for k in range(1, ns):
        copy = pltpu.make_async_remote_copy(
            s_recv.at[my_s], s_recv.at[my_s], s_send_sem.at[k], s_recv_sem.at[k],
            device_id=(friends[k], my_z), device_id_type=MESH,
        )
        copy.start()
        s_copies.append(copy)
    for copy in s_copies:
        copy.wait_recv()
    total = s_recv[0]
    for d in range(1, ns):
        total = total + s_recv[d]
    g_re, g_im = total[0], total[1]

    value = leading_value(g_re, g_im, nb)
    row = lax.broadcasted_iota(jnp.int32, (nb, side), 0)
    mine = row == my_s
    row_re = jnp.sum(jnp.where(mine, g_re, 0.0), axis=0, keepdims=True)
    row_im = jnp.sum(jnp.where(mine, g_im, 0.0), axis=0, keepdims=True)
    result = jnp.where(row == 0, row_re, jnp.where(row == 1, row_im, value))
    group = FREQ_DEV * nb
    placed = result
    for z in range(1, zs):
        placed = jnp.where(my_z == z, pltpu.roll(result, LANES - z * group, 1), placed)
    out_ref[...] = placed

    for group_copies in copies.values():
        for copy in group_copies:
            copy.wait_send()
    for copy in z_copies + s_copies:
        copy.wait_send()


def shards_kernel(zs, ns, snapshots, tail):
    points, steps = snapshots.shape
    nf = FREQ_DEV * zs
    nb = 2 * zs
    sub = points // zs // SUBS
    pieces = sub // LANES
    width = 2 * nf
    table, tail_table = make_tables(nf, pieces)
    combine = make_combine(nf, nb, pieces)
    window = 0.5 - 0.5 * np.cos(2.0 * np.pi * np.arange(NFFT) / NFFT)
    scale = float(1.0 / (points * ns * np.sum(window * window)))
    dma = pltpu.SemaphoreType.DMA
    flops = 2 * points * steps * table.shape[0]
    packed = pl.pallas_call(
        functools.partial(kernel, zs, ns, nf, nb, scale),
        out_shape=jax.ShapeDtypeStruct((nb, LANES), jnp.float32),
        in_specs=[pl.BlockSpec(memory_space=pl.ANY)] * 5,
        out_specs=pl.BlockSpec(memory_space=pltpu.VMEM),
        scratch_shapes=[
            pltpu.VMEM((zs, SUBS, sub, steps), jnp.bfloat16),
            pltpu.VMEM((points // zs, tail.shape[1]), jnp.bfloat16),
            pltpu.VMEM(table.shape, jnp.bfloat16),
            pltpu.VMEM(tail_table.shape, jnp.bfloat16),
            pltpu.VMEM(combine.shape, jnp.bfloat16),
            pltpu.VMEM((zs, SUBS, 2 * width, sub), jnp.bfloat16),
            pltpu.VMEM((zs, SUBS, 2 * pieces, LANES), jnp.float32),
            pltpu.VMEM((zs, SUBS, 2 * width, sub), jnp.bfloat16),
            pltpu.VMEM((zs, SUBS, 2 * pieces, LANES), jnp.float32),
            pltpu.VMEM((2, nb, LANES), jnp.float32),
            pltpu.VMEM((zs, 2, nb, LANES), jnp.float32),
            pltpu.VMEM((ns, 2, nb, LANES), jnp.float32),
            dma((zs, SUBS)), dma((4,)),
            dma((zs, SUBS)), dma((zs, SUBS)), dma((zs, SUBS)), dma((zs, SUBS)),
            dma((zs,)), dma((zs,)), dma((ns,)), dma((ns,)),
        ],
        compiler_params=pltpu.CompilerParams(
            collective_id=0, has_side_effects=True, vmem_limit_bytes=32 * 1024 * 1024
        ),
        cost_estimate=pl.CostEstimate(
            flops=flops, bytes_accessed=points * steps * 2, transcendentals=0
        ),
    )(snapshots, tail, jnp.asarray(table), jnp.asarray(tail_table), jnp.asarray(combine))
    group = FREQ_DEV * nb
    rows = packed[:2, :group].reshape(2, FREQ_DEV, 1, nb).transpose(1, 0, 2, 3)
    return rows, packed[2, :group:nb]


def power_of_two(count):
    return count > 1 and count & (count - 1) == 0


def shards(snapshots, tail):
    zs, ns = lax.axis_size("freq"), lax.axis_size("space")
    points, steps = snapshots.shape
    nb = zs * steps // (NFFT // 2)
    packs = FREQ_DEV * zs * nb == LANES and steps == NFFT and nb == ns == 8
    whole = points % (zs * SUBS * LANES * 4) == 0
    if packs and whole and power_of_two(zs) and power_of_two(ns):
        return shards_kernel(zs, ns, snapshots, tail)
    return shards_general(snapshots, tail)


def solution(mesh):
    in_specs = (P("space", "freq"), P("space", None))
    out_specs = (P("freq", None, "space", None), P("freq"))
    return jax.shard_map(shards, mesh=mesh, in_specs=in_specs, out_specs=out_specs, check_vma=False)
```

```python
import functools
import math

import jax
import jax.numpy as jnp
import ml_dtypes
import numpy as np
from jax import lax
from jax.experimental import pallas as pl
from jax.experimental.pallas import tpu as pltpu
from jax.sharding import PartitionSpec as P

FREQ_DEV = 4
NFFT = 256
POWER = 4
LANES = 128
SUBS = 2
MESH = pl.DeviceIdType.MESH


def shifted(value, axis, steps):
    count = lax.axis_size(axis)
    initial, last = (max(0, -steps), min(count, count - steps))
    return lax.ppermute(value, axis, [(source, source + steps) for source in range(initial, last)])


def build_table(count):
    steps = jnp.arange(NFFT, dtype=jnp.int32)
    freqs = jnp.arange(count, dtype=jnp.int32)
    window = 0.5 - 0.5 * jnp.cos(2.0 * math.pi * steps.astype(jnp.float32) / NFFT)
    phase = 2.0 * math.pi * (steps[:, None] * freqs[None, :] % NFFT).astype(jnp.float32) / NFFT
    table = jnp.concatenate(
        [window[:, None] * jnp.cos(phase), -window[:, None] * jnp.sin(phase)], 1
    )
    return (table.astype(jnp.bfloat16), jnp.sum(window * window))


def transform(extended, table):
    points, width = extended.shape
    half = NFFT // 2
    count = width // half - 1
    halves = extended.reshape(points, count + 1, half)
    blocks = jnp.concatenate([halves[:, :-1], halves[:, 1:]], 2)
    coef = jnp.einsum("pbt,tk->bkp", blocks, table, preferred_element_type=jnp.float32)
    return coef.reshape(count, 2, table.shape[1] // 2, points).astype(jnp.bfloat16)


def gram_terms(coef, scale):
    big = jnp.einsum("bcfp,gdfp->fcbdg", coef, coef, preferred_element_type=jnp.float32)
    real = big[:, 0, :, 0, :] + big[:, 1, :, 1, :]
    imag = big[:, 0, :, 1, :] - big[:, 1, :, 0, :]
    return jnp.stack([real, imag], 1) * scale


def apply_matrix(matrix, vector):
    high = lax.Precision.HIGHEST
    m_real, m_imag = (matrix[:, 0], matrix[:, 1])
    v_real, v_imag = (vector[:, 0], vector[:, 1])
    u_real = jnp.einsum("fjk,fk->fj", m_real, v_real, precision=high) - jnp.einsum(
        "fjk,fk->fj", m_imag, v_imag, precision=high
    )
    u_imag = jnp.einsum("fjk,fk->fj", m_real, v_imag, precision=high) + jnp.einsum(
        "fjk,fk->fj", m_imag, v_real, precision=high
    )
    return jnp.stack([u_real, u_imag], 1)


def rescale(product):
    return product / jnp.sqrt(jnp.mean(product * product, axis=(1, 2), keepdims=True) + 1e-06)


def rayleigh(vector, product):
    return jnp.mean(vector * product, axis=(1, 2)) / (
        jnp.mean(vector * vector, axis=(1, 2)) + 1e-06
    )


def shards_general(snapshots, tail):
    points = snapshots.shape[0]
    freq_count = lax.axis_size("freq")
    half = NFFT // 2
    table, wsum = build_table(FREQ_DEV * freq_count)
    scale = 1.0 / (points * lax.axis_size("space") * wsum)
    following = shifted(snapshots[:, :half], "freq", -1)
    is_last = lax.axis_index("freq") == freq_count - 1
    following = jnp.where(is_last, tail, following)
    extended = jnp.concatenate([snapshots, following], 1)
    coef = transform(extended, table)
    regrouped = lax.all_to_all(coef, "freq", split_axis=2, concat_axis=0, tiled=True)
    partial_value = gram_terms(regrouped, scale)
    blocks_all = partial_value.shape[2]
    held = blocks_all // lax.axis_size("space")
    vector = jnp.stack(
        [
            jnp.ones((FREQ_DEV, blocks_all), jnp.float32),
            jnp.zeros((FREQ_DEV, blocks_all), jnp.float32),
        ],
        1,
    )
    total = lax.psum(partial_value, "space")
    for step in range(POWER):
        vector = rescale(apply_matrix(total, vector))
    spectrum = rayleigh(vector, apply_matrix(total, vector))
    gram_rows = lax.dynamic_slice_in_dim(total, lax.axis_index("space") * held, held, 2)
    return (gram_rows, spectrum)


def two_pieces(values):
    high = values.astype(ml_dtypes.bfloat16)
    low = (values - high.astype(np.float64)).astype(ml_dtypes.bfloat16)
    return np.concatenate([high, low], 0)


def half_rows(nf):
    steps = np.arange(NFFT // 2)
    phase = 2.0 * np.pi * (np.arange(nf + 1)[:, None] * steps[None, :] % NFFT) / NFFT
    real, imag = np.cos(phase), -np.sin(phase)
    main = np.concatenate([real[:nf], imag[:nf]], 0)
    main[nf] = real[nf]
    return main, imag[nf : nf + 1]


def make_tables(nf, pieces):
    main, extra = half_rows(nf)
    half = NFFT // 2
    width = 2 * nf
    both = np.zeros((2 * width + 2 * pieces, NFFT))
    for h in range(2):
        both[h * width : (h + 1) * width, h * half : (h + 1) * half] = main
        both[2 * width + h :: 2, h * half : (h + 1) * half] = extra
    last = np.zeros((width + 16, half))
    last[:width] = main
    last[width] = extra[0]
    return two_pieces(both), two_pieces(last)


def make_combine(nf, nb, pieces):
    width = 2 * nf
    main_rows = nb * width
    ext_rows = nb * pieces
    combine = np.zeros((2, nf, nb, main_rows + ext_rows + width + 16))

    def columns(m, f, part):
        if f == nf and part == 1:
            if m == nb:
                return [main_rows + ext_rows + width]
            first = main_rows + m // 2 * 2 * pieces + m % 2
            return [first + 2 * q for q in range(pieces)]
        start = main_rows + ext_rows if m == nb else m * width
        if f == nf:
            return [start + nf]
        if part == 1 and f == 0:
            return []
        return [start + part * nf + f]

    for f in range(nf):
        for b in range(nb):
            for m in (b, b + 1):
                second = m - b
                sign = (-1.0) ** f if second else 1.0
                side = 0.25 if second else -0.25
                for part in range(2):
                    for g, weight in ((f, 0.5), (f - 1, side), (f + 1, side)):
                        flip = -1.0 if g < 0 and part == 1 else 1.0
                        for column in columns(m, abs(g), part):
                            combine[part, f, b, column] += sign * flip * weight
    return combine.reshape(2 * nf * nb, -1).astype(ml_dtypes.bfloat16)


def xor_index(index, other, count):
    result = 0
    bit = 1
    while bit < count:
        digit = lax.rem(index // bit, 2)
        result = result + bit * ((1 - digit) if other & bit else digit)
        bit *= 2
    return result


def nt_dot(left, right):
    return lax.dot_general(
        left, right, (((1,), (1,)), ((), ())), preferred_element_type=jnp.float32
    )


def leading_value(g_re, g_im, nb):
    shape = g_re.shape
    row = lax.broadcasted_iota(jnp.int32, shape, 0)
    lane = lax.broadcasted_iota(jnp.int32, shape, 1)
    entries = 2.0 * nb

    def lane_sum(x):
        step = 1
        while step < nb:
            ahead = pltpu.roll(x, LANES - step, 1)
            behind = pltpu.roll(x, step, 1)
            x = x + jnp.where(lane % (2 * step) < step, ahead, behind)
            step *= 2
        return x

    def row_sum(x):
        return jnp.broadcast_to(jnp.sum(x, axis=0, keepdims=True), shape)

    def to_lanes(v_re, v_im):
        return row_sum(g_re * v_re + g_im * v_im), row_sum(g_re * v_im - g_im * v_re)

    def to_rows(v_re, v_im):
        return lane_sum(g_re * v_re - g_im * v_im), lane_sum(g_re * v_im + g_im * v_re)

    v_re, v_im = jnp.ones(shape, jnp.float32), jnp.zeros(shape, jnp.float32)
    for step in range(POWER):
        if step % 2 == 0:
            u_re, u_im = to_lanes(v_re, v_im)
            size = jnp.sqrt(lane_sum(u_re * u_re + u_im * u_im) / entries + 1e-06)
            v_re, v_im = u_re, u_im
        else:
            u_re, u_im = to_rows(v_re, v_im)
            u_re, u_im = u_re / size, u_im / size
            size = jnp.sqrt(row_sum(u_re * u_re + u_im * u_im) / entries + 1e-06)
            v_re, v_im = u_re / size, u_im / size
    u_re, u_im = to_lanes(v_re, v_im)
    here = lane % nb == row
    across_re = row_sum(jnp.where(here, v_re, 0.0))
    across_im = row_sum(jnp.where(here, v_im, 0.0))
    top = lane_sum(across_re * u_re + across_im * u_im) / entries
    return top / (row_sum(v_re * v_re + v_im * v_im) / entries + 1e-06)


def kernel(
    zs, ns, nf, nb, scale, spans, inner,
    snap_ref, tail_ref, const_ref, gram_ref, value_ref,
    x_buf, tail_buf, const,
    send, send_ext, recv, recv_ext, z_part, z_recv, s_recv,
    x_sem, const_sem, send_sem, recv_sem, ext_send_sem, ext_recv_sem,
    z_send_sem, z_recv_sem, s_send_sem, s_recv_sem,
):
    my_s, my_z = lax.axis_index("space"), lax.axis_index("freq")
    quarter = snap_ref.shape[0] // zs
    sub = quarter // SUBS
    width = 2 * nf
    pieces = sub // LANES
    order = list(range(zs // 2, zs)) + list(range(1, zs // 2))
    peers = {k: xor_index(my_z, k, zs) for k in order}
    peers[0] = my_z
    friends = {k: xor_index(my_s, k, ns) for k in range(1, ns)}

    barrier = pltpu.get_barrier_semaphore()
    for k in order:
        pl.semaphore_signal(barrier, inc=1, device_id=(my_s, peers[k]), device_id_type=MESH)
    for k in range(1, ns):
        pl.semaphore_signal(barrier, inc=1, device_id=(friends[k], my_z), device_id_type=MESH)

    loads = {}
    (t0, t1), (l0, l1), (c0, c1) = spans
    constants = [
        pltpu.make_async_copy(const_ref.at[a:b], const.at[a:b], const_sem.at[i])
        for i, (a, b) in enumerate(spans)
    ] + [
        pltpu.make_async_copy(
            tail_ref.at[pl.ds(pl.multiple_of(my_z * quarter, quarter), quarter)],
            tail_buf, const_sem.at[3],
        ),
    ]
    constants[0].start()
    for s in range(SUBS):
        for k in order + [0]:
            first = pl.multiple_of(peers[k] * quarter + s * sub, sub)
            loads[k, s] = pltpu.make_async_copy(
                snap_ref.at[pl.ds(first, sub)], x_buf.at[k, s], x_sem.at[k, s]
            )
            loads[k, s].start()
    for copy in constants[1:]:
        copy.start()

    ext_row = lax.broadcasted_iota(jnp.int32, (2 * pieces, LANES), 0) // 2

    def transform(k, s):
        loads[k, s].wait()
        both = nt_dot(const[t0:t1, : x_buf.shape[3]], x_buf[k, s])
        rows = both.shape[0] // 2
        both = both[:rows] + both[rows:]
        extra = jnp.zeros((2 * pieces, LANES), jnp.float32)
        for q in range(pieces):
            extra = jnp.where(
                ext_row == q, both[2 * width :, q * LANES : (q + 1) * LANES], extra
            )
        return both[: 2 * width].astype(jnp.bfloat16), extra

    constants[0].wait()
    copies = {}
    for s in range(SUBS):
        for k in order:
            main, extra = transform(k, s)
            send[k, s] = main
            send_ext[k, s] = extra
            if s == 0 and k == order[0]:
                pl.semaphore_wait(barrier, zs - 1 + ns - 1)
            target = (my_s, peers[k])
            copies[k, s] = [
                pltpu.make_async_remote_copy(
                    send_ext.at[k, s], recv_ext.at[my_z, s],
                    ext_send_sem.at[k, s], ext_recv_sem.at[k, s],
                    device_id=target, device_id_type=MESH,
                ),
                pltpu.make_async_remote_copy(
                    send.at[k, s], recv.at[my_z, s],
                    send_sem.at[k, s], recv_sem.at[k, s],
                    device_id=target, device_id_type=MESH,
                ),
            ]
            for copy in copies[k, s]:
                copy.start()
    for s in range(SUBS):
        main, extra = transform(0, s)
        recv[my_z, s] = main
        recv_ext[my_z, s] = extra
    for copy in constants[1:]:
        copy.wait()

    gram = jnp.zeros((width * nb, width * nb), jnp.float32)
    for s in range(SUBS):
        last = nt_dot(const[l0:l1, : tail_buf.shape[1]], tail_buf[s * sub : (s + 1) * sub])
        rows = last.shape[0] // 2
        last = (last[:rows] + last[rows:]).astype(jnp.bfloat16)
        for k in order:
            for copy in copies[k, s]:
                copy.wait_recv()
        extras = []
        for d in range(zs):
            extra = recv_ext[d, s]
            extras.append(
                jnp.concatenate([jnp.where(ext_row == q, extra, 0.0) for q in range(pieces)], 1)
            )
        stacked = jnp.concatenate(
            [recv[d, s] for d in range(zs)]
            + [jnp.concatenate(extras, 0).astype(jnp.bfloat16), last],
            0,
        )
        coef = jnp.dot(const[c0:c1, :inner], stacked, preferred_element_type=jnp.float32)
        coef = coef.astype(jnp.bfloat16)
        gram = gram + nt_dot(coef, coef)

    side = nf * nb
    real = gram[:side, :side] + gram[side:, side:]
    imag = gram[:side, side:] - gram[side:, :side]
    lane_freq = lax.broadcasted_iota(jnp.int32, (nb, side), 1) // nb
    g_re = jnp.zeros((nb, side), jnp.float32)
    g_im = jnp.zeros((nb, side), jnp.float32)
    for f in range(nf):
        g_re = jnp.where(lane_freq == f, real[f * nb : (f + 1) * nb], g_re)
        g_im = jnp.where(lane_freq == f, imag[f * nb : (f + 1) * nb], g_im)
    z_part[0] = g_re * scale
    z_part[1] = g_im * scale

    z_copies = []
    for k in order:
        copy = pltpu.make_async_remote_copy(
            z_part, z_recv.at[k], z_send_sem.at[k], z_recv_sem.at[k],
            device_id=(my_s, peers[k]), device_id_type=MESH,
        )
        copy.start()
        z_copies.append(copy)
    total = z_part[...]
    for k, copy in zip(order, z_copies):
        copy.wait_recv()
        total = total + z_recv[k]
    s_recv[my_s] = total
    s_copies = []
    for k in range(1, ns):
        copy = pltpu.make_async_remote_copy(
            s_recv.at[my_s], s_recv.at[my_s], s_send_sem.at[k], s_recv_sem.at[k],
            device_id=(friends[k], my_z), device_id_type=MESH,
        )
        copy.start()
        s_copies.append(copy)
    for copy in s_copies:
        copy.wait_recv()
    total = s_recv[0]
    for d in range(1, ns):
        total = total + s_recv[d]
    g_re, g_im = total[0], total[1]

    value = leading_value(g_re, g_im, nb)
    row = lax.broadcasted_iota(jnp.int32, (nb, side), 0)
    mine = row == my_s
    row_re = jnp.sum(jnp.where(mine, g_re, 0.0), axis=0, keepdims=True)
    row_im = jnp.sum(jnp.where(mine, g_im, 0.0), axis=0, keepdims=True)
    group = FREQ_DEV * nb
    result = jnp.where(row % 2 == 0, row_re, row_im)
    placed, spread = result, value
    for z in range(1, zs):
        placed = jnp.where(my_z == z, pltpu.roll(result, LANES - z * group, 1), placed)
        spread = jnp.where(my_z == z, pltpu.roll(value, LANES - z * group, 1), spread)
    rows, values = placed, spread
    lane = lax.broadcasted_iota(jnp.int32, (nb, side), 1)
    for f in range(1, FREQ_DEV):
        rows = jnp.where(row // 2 == f, pltpu.roll(placed, LANES - f * nb, 1), rows)
        values = jnp.where(lane == f, pltpu.roll(spread, LANES - f * (nb - 1), 1), values)
    gram_ref[...] = rows
    value_ref[...] = values

    for group_copies in copies.values():
        for copy in group_copies:
            copy.wait_send()
    for copy in z_copies + s_copies:
        copy.wait_send()


def shards_kernel(zs, ns, snapshots, tail):
    points, steps = snapshots.shape
    nf = FREQ_DEV * zs
    nb = 2 * zs
    sub = points // zs // SUBS
    pieces = sub // LANES
    width = 2 * nf
    table, tail_table = make_tables(nf, pieces)
    combine = make_combine(nf, nb, pieces)
    window = 0.5 - 0.5 * np.cos(2.0 * np.pi * np.arange(NFFT) / NFFT)
    scale = float(1.0 / (points * ns * np.sum(window * window)))
    parts = [table, tail_table, combine]
    inner = combine.shape[1]
    padded = -(-inner // LANES) * LANES
    const = np.concatenate([np.pad(p, ((0, 0), (0, padded - p.shape[1]))) for p in parts], 0)
    ends = np.cumsum([p.shape[0] for p in parts]).tolist()
    spans = list(zip([0] + ends[:-1], ends))
    dma = pltpu.SemaphoreType.DMA
    flops = 2 * points * steps * table.shape[0]
    gram, values = pl.pallas_call(
        functools.partial(kernel, zs, ns, nf, nb, scale, spans, inner),
        out_shape=[jax.ShapeDtypeStruct((nb, LANES), jnp.float32)] * 2,
        in_specs=[pl.BlockSpec(memory_space=pltpu.HBM)] * 3,
        out_specs=[pl.BlockSpec(memory_space=pltpu.VMEM)] * 2,
        scratch_shapes=[
            pltpu.VMEM((zs, SUBS, sub, steps), jnp.bfloat16),
            pltpu.VMEM((points // zs, tail.shape[1]), jnp.bfloat16),
            pltpu.VMEM(const.shape, jnp.bfloat16),
            pltpu.VMEM((zs, SUBS, 2 * width, sub), jnp.bfloat16),
            pltpu.VMEM((zs, SUBS, 2 * pieces, LANES), jnp.float32),
            pltpu.VMEM((zs, SUBS, 2 * width, sub), jnp.bfloat16),
            pltpu.VMEM((zs, SUBS, 2 * pieces, LANES), jnp.float32),
            pltpu.VMEM((2, nb, LANES), jnp.float32),
            pltpu.VMEM((zs, 2, nb, LANES), jnp.float32),
            pltpu.VMEM((ns, 2, nb, LANES), jnp.float32),
            dma((zs, SUBS)), dma((4,)),
            dma((zs, SUBS)), dma((zs, SUBS)), dma((zs, SUBS)), dma((zs, SUBS)),
            dma((zs,)), dma((zs,)), dma((ns,)), dma((ns,)),
        ],
        compiler_params=pltpu.CompilerParams(
            collective_id=0, has_side_effects=True, vmem_limit_bytes=56 * 1024 * 1024
        ),
        cost_estimate=pl.CostEstimate(
            flops=flops, bytes_accessed=points * steps * 2, transcendentals=0
        ),
    )(snapshots, tail, jnp.asarray(const))
    return gram[:, :nb].reshape(FREQ_DEV, 2, 1, nb), values[0, :FREQ_DEV]


def power_of_two(count):
    return count > 1 and count & (count - 1) == 0


def shards(snapshots, tail):
    zs, ns = lax.axis_size("freq"), lax.axis_size("space")
    points, steps = snapshots.shape
    nb = zs * steps // (NFFT // 2)
    packs = FREQ_DEV * zs * nb == LANES and steps == NFFT and nb == ns == 8
    whole = points % (zs * SUBS * LANES * 4) == 0
    if packs and whole and power_of_two(zs) and power_of_two(ns):
        return shards_kernel(zs, ns, snapshots, tail)
    return shards_general(snapshots, tail)


def solution(mesh):
    in_specs = (P("space", "freq"), P("space", None))
    out_specs = (P("freq", None, "space", None), P("freq"))
    return jax.shard_map(shards, mesh=mesh, in_specs=in_specs, out_specs=out_specs, check_vma=False)
```

```python
import functools
import math

import jax
import jax.numpy as jnp
import ml_dtypes
import numpy as np
from jax import lax
from jax.experimental import pallas as pl
from jax.experimental.pallas import tpu as pltpu
from jax.sharding import PartitionSpec as P

FREQ_DEV = 4
NFFT = 256
POWER = 4
LANES = 128
SUBS = 4
MESH = pl.DeviceIdType.MESH


def shifted(value, axis, steps):
    count = lax.axis_size(axis)
    initial, last = (max(0, -steps), min(count, count - steps))
    return lax.ppermute(value, axis, [(source, source + steps) for source in range(initial, last)])


def build_table(count):
    steps = jnp.arange(NFFT, dtype=jnp.int32)
    freqs = jnp.arange(count, dtype=jnp.int32)
    window = 0.5 - 0.5 * jnp.cos(2.0 * math.pi * steps.astype(jnp.float32) / NFFT)
    phase = 2.0 * math.pi * (steps[:, None] * freqs[None, :] % NFFT).astype(jnp.float32) / NFFT
    table = jnp.concatenate(
        [window[:, None] * jnp.cos(phase), -window[:, None] * jnp.sin(phase)], 1
    )
    return (table.astype(jnp.bfloat16), jnp.sum(window * window))


def transform(extended, table):
    points, width = extended.shape
    half = NFFT // 2
    count = width // half - 1
    halves = extended.reshape(points, count + 1, half)
    blocks = jnp.concatenate([halves[:, :-1], halves[:, 1:]], 2)
    coef = jnp.einsum("pbt,tk->bkp", blocks, table, preferred_element_type=jnp.float32)
    return coef.reshape(count, 2, table.shape[1] // 2, points).astype(jnp.bfloat16)


def gram_terms(coef, scale):
    big = jnp.einsum("bcfp,gdfp->fcbdg", coef, coef, preferred_element_type=jnp.float32)
    real = big[:, 0, :, 0, :] + big[:, 1, :, 1, :]
    imag = big[:, 0, :, 1, :] - big[:, 1, :, 0, :]
    return jnp.stack([real, imag], 1) * scale


def apply_matrix(matrix, vector):
    high = lax.Precision.HIGHEST
    m_real, m_imag = (matrix[:, 0], matrix[:, 1])
    v_real, v_imag = (vector[:, 0], vector[:, 1])
    u_real = jnp.einsum("fjk,fk->fj", m_real, v_real, precision=high) - jnp.einsum(
        "fjk,fk->fj", m_imag, v_imag, precision=high
    )
    u_imag = jnp.einsum("fjk,fk->fj", m_real, v_imag, precision=high) + jnp.einsum(
        "fjk,fk->fj", m_imag, v_real, precision=high
    )
    return jnp.stack([u_real, u_imag], 1)


def rescale(product):
    return product / jnp.sqrt(jnp.mean(product * product, axis=(1, 2), keepdims=True) + 1e-06)


def rayleigh(vector, product):
    return jnp.mean(vector * product, axis=(1, 2)) / (
        jnp.mean(vector * vector, axis=(1, 2)) + 1e-06
    )


def shards_general(snapshots, tail):
    points = snapshots.shape[0]
    freq_count = lax.axis_size("freq")
    half = NFFT // 2
    table, wsum = build_table(FREQ_DEV * freq_count)
    scale = 1.0 / (points * lax.axis_size("space") * wsum)
    following = shifted(snapshots[:, :half], "freq", -1)
    is_last = lax.axis_index("freq") == freq_count - 1
    following = jnp.where(is_last, tail, following)
    extended = jnp.concatenate([snapshots, following], 1)
    coef = transform(extended, table)
    regrouped = lax.all_to_all(coef, "freq", split_axis=2, concat_axis=0, tiled=True)
    partial_value = gram_terms(regrouped, scale)
    blocks_all = partial_value.shape[2]
    held = blocks_all // lax.axis_size("space")
    vector = jnp.stack(
        [
            jnp.ones((FREQ_DEV, blocks_all), jnp.float32),
            jnp.zeros((FREQ_DEV, blocks_all), jnp.float32),
        ],
        1,
    )
    total = lax.psum(partial_value, "space")
    for step in range(POWER):
        vector = rescale(apply_matrix(total, vector))
    spectrum = rayleigh(vector, apply_matrix(total, vector))
    gram_rows = lax.dynamic_slice_in_dim(total, lax.axis_index("space") * held, held, 2)
    return (gram_rows, spectrum)


def two_pieces(values):
    high = values.astype(ml_dtypes.bfloat16)
    low = (values - high.astype(np.float64)).astype(ml_dtypes.bfloat16)
    return np.concatenate([high, low], 0)


def half_rows(nf):
    steps = np.arange(NFFT // 2)
    phase = 2.0 * np.pi * (np.arange(nf + 1)[:, None] * steps[None, :] % NFFT) / NFFT
    real, imag = np.cos(phase), -np.sin(phase)
    main = np.concatenate([real[:nf], imag[:nf]], 0)
    main[nf] = real[nf]
    return main, imag[nf : nf + 1]


def make_tables(nf, pieces):
    main, extra = half_rows(nf)
    half = NFFT // 2
    width = 2 * nf
    both = np.zeros((2 * width + max(2 * pieces, 8), NFFT))
    for h in range(2):
        both[h * width : (h + 1) * width, h * half : (h + 1) * half] = main
        both[2 * width + h : 2 * width + 2 * pieces : 2, h * half : (h + 1) * half] = extra
    last = np.zeros((width + 16, half))
    last[:width] = main
    last[width] = extra[0]
    return two_pieces(both), two_pieces(last)


def make_combine(nf, nb, pieces):
    width = 2 * nf
    main_rows = nb * width
    ext_rows = nb * pieces
    combine = np.zeros((2, nf, nb, main_rows + ext_rows + width + 16))

    def columns(m, f, part):
        if f == nf and part == 1:
            if m == nb:
                return [main_rows + ext_rows + width]
            first = main_rows + m // 2 * 2 * pieces + m % 2
            return [first + 2 * q for q in range(pieces)]
        start = main_rows + ext_rows if m == nb else m * width
        if f == nf:
            return [start + nf]
        if part == 1 and f == 0:
            return []
        return [start + part * nf + f]

    for f in range(nf):
        for b in range(nb):
            for m in (b, b + 1):
                second = m - b
                sign = (-1.0) ** f if second else 1.0
                side = 0.25 if second else -0.25
                for part in range(2):
                    for g, weight in ((f, 0.5), (f - 1, side), (f + 1, side)):
                        flip = -1.0 if g < 0 and part == 1 else 1.0
                        for column in columns(m, abs(g), part):
                            combine[part, f, b, column] += sign * flip * weight
    return combine.reshape(2 * nf * nb, -1).astype(ml_dtypes.bfloat16)


def xor_index(index, other, count):
    result = 0
    bit = 1
    while bit < count:
        digit = lax.rem(index // bit, 2)
        result = result + bit * ((1 - digit) if other & bit else digit)
        bit *= 2
    return result


def nt_dot(left, right):
    return lax.dot_general(
        left, right, (((1,), (1,)), ((), ())), preferred_element_type=jnp.float32
    )


def leading_value(g_re, g_im, nb):
    shape = g_re.shape
    row = lax.broadcasted_iota(jnp.int32, shape, 0)
    lane = lax.broadcasted_iota(jnp.int32, shape, 1)
    entries = 2.0 * nb

    def lane_sum(x):
        step = 1
        while step < nb:
            ahead = pltpu.roll(x, LANES - step, 1)
            behind = pltpu.roll(x, step, 1)
            x = x + jnp.where(lane % (2 * step) < step, ahead, behind)
            step *= 2
        return x

    def row_sum(x):
        return jnp.broadcast_to(jnp.sum(x, axis=0, keepdims=True), shape)

    def to_lanes(v_re, v_im):
        return row_sum(g_re * v_re + g_im * v_im), row_sum(g_re * v_im - g_im * v_re)

    def to_rows(v_re, v_im):
        return lane_sum(g_re * v_re - g_im * v_im), lane_sum(g_re * v_im + g_im * v_re)

    v_re, v_im = jnp.ones(shape, jnp.float32), jnp.zeros(shape, jnp.float32)
    for step in range(POWER):
        if step % 2 == 0:
            u_re, u_im = to_lanes(v_re, v_im)
            size = jnp.sqrt(lane_sum(u_re * u_re + u_im * u_im) / entries + 1e-06)
            v_re, v_im = u_re, u_im
        else:
            u_re, u_im = to_rows(v_re, v_im)
            u_re, u_im = u_re / size, u_im / size
            size = jnp.sqrt(row_sum(u_re * u_re + u_im * u_im) / entries + 1e-06)
            v_re, v_im = u_re / size, u_im / size
    u_re, u_im = to_lanes(v_re, v_im)
    here = lane % nb == row
    across_re = row_sum(jnp.where(here, v_re, 0.0))
    across_im = row_sum(jnp.where(here, v_im, 0.0))
    top = lane_sum(across_re * u_re + across_im * u_im) / entries
    return top / (row_sum(v_re * v_re + v_im * v_im) / entries + 1e-06)


def kernel(
    zs, ns, nf, nb, scale, spans, inner,
    snap_ref, tail_ref, const_ref, gram_ref, value_ref,
    x_buf, tail_buf, last_buf, const,
    send, send_ext, recv, recv_ext, z_part, z_recv, s_recv,
    x_sem, const_sem, send_sem, recv_sem, ext_send_sem, ext_recv_sem,
    z_send_sem, z_recv_sem, s_send_sem, s_recv_sem,
):
    my_s, my_z = lax.axis_index("space"), lax.axis_index("freq")
    quarter = snap_ref.shape[0] // zs
    sub = quarter // SUBS
    width = 2 * nf
    pieces = sub // LANES
    order = list(range(zs // 2, zs)) + list(range(1, zs // 2))
    peers = {k: xor_index(my_z, k, zs) for k in order}
    peers[0] = my_z
    friends = {k: xor_index(my_s, k, ns) for k in range(1, ns)}

    barrier = pltpu.get_barrier_semaphore()
    for k in order:
        pl.semaphore_signal(barrier, inc=1, device_id=(my_s, peers[k]), device_id_type=MESH)
    for k in range(1, ns):
        pl.semaphore_signal(barrier, inc=1, device_id=(friends[k], my_z), device_id_type=MESH)

    loads = {}
    (t0, t1), (l0, l1), (c0, c1) = spans
    constants = [
        pltpu.make_async_copy(const_ref.at[a:b], const.at[a:b], const_sem.at[i])
        for i, (a, b) in enumerate(spans)
    ] + [
        pltpu.make_async_copy(
            tail_ref.at[pl.ds(pl.multiple_of(my_z * quarter, quarter), quarter)],
            tail_buf, const_sem.at[3],
        ),
    ]
    constants[0].start()
    for s in range(SUBS):
        for k in order + [0]:
            first = pl.multiple_of(peers[k] * quarter + s * sub, sub)
            loads[k, s] = pltpu.make_async_copy(
                snap_ref.at[pl.ds(first, sub)], x_buf.at[k, s], x_sem.at[k, s]
            )
            loads[k, s].start()
    for copy in constants[1:]:
        copy.start()

    ext_row = lax.broadcasted_iota(jnp.int32, (2 * pieces, LANES), 0) // 2

    def transform(k, s):
        loads[k, s].wait()
        both = nt_dot(const[t0:t1, : x_buf.shape[3]], x_buf[k, s])
        rows = both.shape[0] // 2
        both = both[:rows] + both[rows:]
        extra = jnp.zeros((2 * pieces, LANES), jnp.float32)
        for q in range(pieces):
            extra = jnp.where(
                ext_row == q, both[2 * width : 2 * width + 2 * pieces, q * LANES : (q + 1) * LANES], extra
            )
        return both[: 2 * width].astype(jnp.bfloat16), extra

    constants[0].wait()
    copies = {}
    for s in range(SUBS):
        for k in order:
            main, extra = transform(k, s)
            send[k, s] = main
            send_ext[k, s] = extra
            if s == 0 and k == order[0]:
                pl.semaphore_wait(barrier, zs - 1 + ns - 1)
            target = (my_s, peers[k])
            copies[k, s] = [
                pltpu.make_async_remote_copy(
                    send_ext.at[k, s], recv_ext.at[my_z, s],
                    ext_send_sem.at[k, s], ext_recv_sem.at[k, s],
                    device_id=target, device_id_type=MESH,
                ),
                pltpu.make_async_remote_copy(
                    send.at[k, s], recv.at[my_z, s],
                    send_sem.at[k, s], recv_sem.at[k, s],
                    device_id=target, device_id_type=MESH,
                ),
            ]
            for copy in copies[k, s]:
                copy.start()
    for s in range(SUBS):
        main, extra = transform(0, s)
        recv[my_z, s] = main
        recv_ext[my_z, s] = extra
    for copy in constants[1:]:
        copy.wait()
    for s in range(SUBS):
        last = nt_dot(const[l0:l1, : tail_buf.shape[1]], tail_buf[s * sub : (s + 1) * sub])
        rows = last.shape[0] // 2
        last_buf[s] = (last[:rows] + last[rows:]).astype(jnp.bfloat16)

    gram = jnp.zeros((width * nb, width * nb), jnp.float32)
    for s in range(SUBS):
        for k in order:
            for copy in copies[k, s]:
                copy.wait_recv()
        extras = []
        for d in range(zs):
            extra = recv_ext[d, s]
            extras.append(
                jnp.concatenate([jnp.where(ext_row == q, extra, 0.0) for q in range(pieces)], 1)
            )
        stacked = jnp.concatenate(
            [recv[d, s] for d in range(zs)]
            + [jnp.concatenate(extras, 0).astype(jnp.bfloat16), last_buf[s]],
            0,
        )
        coef = jnp.dot(const[c0:c1, :inner], stacked, preferred_element_type=jnp.float32)
        coef = coef.astype(jnp.bfloat16)
        gram = gram + nt_dot(coef, coef)

    side = nf * nb
    real = gram[:side, :side] + gram[side:, side:]
    imag = gram[:side, side:] - gram[side:, :side]
    lane_freq = lax.broadcasted_iota(jnp.int32, (nb, side), 1) // nb
    g_re = jnp.zeros((nb, side), jnp.float32)
    g_im = jnp.zeros((nb, side), jnp.float32)
    for f in range(nf):
        g_re = jnp.where(lane_freq == f, real[f * nb : (f + 1) * nb], g_re)
        g_im = jnp.where(lane_freq == f, imag[f * nb : (f + 1) * nb], g_im)
    z_part[0] = g_re * scale
    z_part[1] = g_im * scale

    z_copies = []
    for k in order:
        copy = pltpu.make_async_remote_copy(
            z_part, z_recv.at[k], z_send_sem.at[k], z_recv_sem.at[k],
            device_id=(my_s, peers[k]), device_id_type=MESH,
        )
        copy.start()
        z_copies.append(copy)
    total = z_part[...]
    for k, copy in zip(order, z_copies):
        copy.wait_recv()
        total = total + z_recv[k]
    s_recv[my_s] = total
    s_copies = []
    for k in range(1, ns):
        copy = pltpu.make_async_remote_copy(
            s_recv.at[my_s], s_recv.at[my_s], s_send_sem.at[k], s_recv_sem.at[k],
            device_id=(friends[k], my_z), device_id_type=MESH,
        )
        copy.start()
        s_copies.append(copy)
    for copy in s_copies:
        copy.wait_recv()
    total = s_recv[0]
    for d in range(1, ns):
        total = total + s_recv[d]
    g_re, g_im = total[0], total[1]

    value = leading_value(g_re, g_im, nb)
    row = lax.broadcasted_iota(jnp.int32, (nb, side), 0)
    mine = row == my_s
    row_re = jnp.sum(jnp.where(mine, g_re, 0.0), axis=0, keepdims=True)
    row_im = jnp.sum(jnp.where(mine, g_im, 0.0), axis=0, keepdims=True)
    group = FREQ_DEV * nb
    result = jnp.where(row % 2 == 0, row_re, row_im)
    placed, spread = result, value
    for z in range(1, zs):
        placed = jnp.where(my_z == z, pltpu.roll(result, LANES - z * group, 1), placed)
        spread = jnp.where(my_z == z, pltpu.roll(value, LANES - z * group, 1), spread)
    rows, values = placed, spread
    lane = lax.broadcasted_iota(jnp.int32, (nb, side), 1)
    for f in range(1, FREQ_DEV):
        rows = jnp.where(row // 2 == f, pltpu.roll(placed, LANES - f * nb, 1), rows)
        values = jnp.where(lane == f, pltpu.roll(spread, LANES - f * (nb - 1), 1), values)
    gram_ref[...] = rows
    value_ref[...] = values

    for group_copies in copies.values():
        for copy in group_copies:
            copy.wait_send()
    for copy in z_copies + s_copies:
        copy.wait_send()


def shards_kernel(zs, ns, snapshots, tail):
    points, steps = snapshots.shape
    nf = FREQ_DEV * zs
    nb = 2 * zs
    sub = points // zs // SUBS
    pieces = sub // LANES
    width = 2 * nf
    table, tail_table = make_tables(nf, pieces)
    combine = make_combine(nf, nb, pieces)
    window = 0.5 - 0.5 * np.cos(2.0 * np.pi * np.arange(NFFT) / NFFT)
    scale = float(1.0 / (points * ns * np.sum(window * window)))
    parts = [table, tail_table, combine]
    inner = combine.shape[1]
    padded = -(-inner // LANES) * LANES
    const = np.concatenate([np.pad(p, ((0, 0), (0, padded - p.shape[1]))) for p in parts], 0)
    ends = np.cumsum([p.shape[0] for p in parts]).tolist()
    spans = list(zip([0] + ends[:-1], ends))
    dma = pltpu.SemaphoreType.DMA
    flops = 2 * points * steps * table.shape[0]
    gram, values = pl.pallas_call(
        functools.partial(kernel, zs, ns, nf, nb, scale, spans, inner),
        out_shape=[jax.ShapeDtypeStruct((nb, LANES), jnp.float32)] * 2,
        in_specs=[pl.BlockSpec(memory_space=pltpu.HBM)] * 3,
        out_specs=[pl.BlockSpec(memory_space=pltpu.VMEM)] * 2,
        scratch_shapes=[
            pltpu.VMEM((zs, SUBS, sub, steps), jnp.bfloat16),
            pltpu.VMEM((points // zs, tail.shape[1]), jnp.bfloat16),
            pltpu.VMEM((SUBS, tail_table.shape[0] // 2, sub), jnp.bfloat16),
            pltpu.VMEM(const.shape, jnp.bfloat16),
            pltpu.VMEM((zs, SUBS, 2 * width, sub), jnp.bfloat16),
            pltpu.VMEM((zs, SUBS, 2 * pieces, LANES), jnp.float32),
            pltpu.VMEM((zs, SUBS, 2 * width, sub), jnp.bfloat16),
            pltpu.VMEM((zs, SUBS, 2 * pieces, LANES), jnp.float32),
            pltpu.VMEM((2, nb, LANES), jnp.float32),
            pltpu.VMEM((zs, 2, nb, LANES), jnp.float32),
            pltpu.VMEM((ns, 2, nb, LANES), jnp.float32),
            dma((zs, SUBS)), dma((4,)),
            dma((zs, SUBS)), dma((zs, SUBS)), dma((zs, SUBS)), dma((zs, SUBS)),
            dma((zs,)), dma((zs,)), dma((ns,)), dma((ns,)),
        ],
        compiler_params=pltpu.CompilerParams(
            collective_id=0, has_side_effects=True, vmem_limit_bytes=55040 * 1024
        ),
        cost_estimate=pl.CostEstimate(
            flops=flops, bytes_accessed=points * steps * 2, transcendentals=0
        ),
    )(snapshots, tail, jnp.asarray(const))
    return gram[:, :nb].reshape(FREQ_DEV, 2, 1, nb), values[0, :FREQ_DEV]


def power_of_two(count):
    return count > 1 and count & (count - 1) == 0


def shards(snapshots, tail):
    zs, ns = lax.axis_size("freq"), lax.axis_size("space")
    points, steps = snapshots.shape
    nb = zs * steps // (NFFT // 2)
    packs = FREQ_DEV * zs * nb == LANES and steps == NFFT and nb == ns == 8
    whole = points % (zs * SUBS * LANES) == 0
    if packs and whole and power_of_two(zs) and power_of_two(ns):
        return shards_kernel(zs, ns, snapshots, tail)
    return shards_general(snapshots, tail)


def solution(mesh):
    in_specs = (P("space", "freq"), P("space", None))
    out_specs = (P("freq", None, "space", None), P("freq"))
    return jax.shard_map(shards, mesh=mesh, in_specs=in_specs, out_specs=out_specs, check_vma=False)
```

```python
import functools
import math

import jax
import jax.numpy as jnp
import ml_dtypes
import numpy as np
from jax import lax
from jax.experimental import pallas as pl
from jax.experimental.pallas import tpu as pltpu
from jax.sharding import PartitionSpec as P

FREQ_DEV = 4
NFFT = 256
POWER = 4
LANES = 128
SUBS = 4
MESH = pl.DeviceIdType.MESH


def shifted(value, axis, steps):
    count = lax.axis_size(axis)
    initial, last = (max(0, -steps), min(count, count - steps))
    return lax.ppermute(value, axis, [(source, source + steps) for source in range(initial, last)])


def build_table(count):
    steps = jnp.arange(NFFT, dtype=jnp.int32)
    freqs = jnp.arange(count, dtype=jnp.int32)
    window = 0.5 - 0.5 * jnp.cos(2.0 * math.pi * steps.astype(jnp.float32) / NFFT)
    phase = 2.0 * math.pi * (steps[:, None] * freqs[None, :] % NFFT).astype(jnp.float32) / NFFT
    table = jnp.concatenate(
        [window[:, None] * jnp.cos(phase), -window[:, None] * jnp.sin(phase)], 1
    )
    return (table.astype(jnp.bfloat16), jnp.sum(window * window))


def transform(extended, table):
    points, width = extended.shape
    half = NFFT // 2
    count = width // half - 1
    halves = extended.reshape(points, count + 1, half)
    blocks = jnp.concatenate([halves[:, :-1], halves[:, 1:]], 2)
    coef = jnp.einsum("pbt,tk->bkp", blocks, table, preferred_element_type=jnp.float32)
    return coef.reshape(count, 2, table.shape[1] // 2, points).astype(jnp.bfloat16)


def gram_terms(coef, scale):
    big = jnp.einsum("bcfp,gdfp->fcbdg", coef, coef, preferred_element_type=jnp.float32)
    real = big[:, 0, :, 0, :] + big[:, 1, :, 1, :]
    imag = big[:, 0, :, 1, :] - big[:, 1, :, 0, :]
    return jnp.stack([real, imag], 1) * scale


def apply_matrix(matrix, vector):
    high = lax.Precision.HIGHEST
    m_real, m_imag = (matrix[:, 0], matrix[:, 1])
    v_real, v_imag = (vector[:, 0], vector[:, 1])
    u_real = jnp.einsum("fjk,fk->fj", m_real, v_real, precision=high) - jnp.einsum(
        "fjk,fk->fj", m_imag, v_imag, precision=high
    )
    u_imag = jnp.einsum("fjk,fk->fj", m_real, v_imag, precision=high) + jnp.einsum(
        "fjk,fk->fj", m_imag, v_real, precision=high
    )
    return jnp.stack([u_real, u_imag], 1)


def rescale(product):
    return product / jnp.sqrt(jnp.mean(product * product, axis=(1, 2), keepdims=True) + 1e-06)


def rayleigh(vector, product):
    return jnp.mean(vector * product, axis=(1, 2)) / (
        jnp.mean(vector * vector, axis=(1, 2)) + 1e-06
    )


def shards_general(snapshots, tail):
    points = snapshots.shape[0]
    freq_count = lax.axis_size("freq")
    half = NFFT // 2
    table, wsum = build_table(FREQ_DEV * freq_count)
    scale = 1.0 / (points * lax.axis_size("space") * wsum)
    following = shifted(snapshots[:, :half], "freq", -1)
    is_last = lax.axis_index("freq") == freq_count - 1
    following = jnp.where(is_last, tail, following)
    extended = jnp.concatenate([snapshots, following], 1)
    coef = transform(extended, table)
    regrouped = lax.all_to_all(coef, "freq", split_axis=2, concat_axis=0, tiled=True)
    partial_value = gram_terms(regrouped, scale)
    blocks_all = partial_value.shape[2]
    held = blocks_all // lax.axis_size("space")
    vector = jnp.stack(
        [
            jnp.ones((FREQ_DEV, blocks_all), jnp.float32),
            jnp.zeros((FREQ_DEV, blocks_all), jnp.float32),
        ],
        1,
    )
    total = lax.psum(partial_value, "space")
    for step in range(POWER):
        vector = rescale(apply_matrix(total, vector))
    spectrum = rayleigh(vector, apply_matrix(total, vector))
    gram_rows = lax.dynamic_slice_in_dim(total, lax.axis_index("space") * held, held, 2)
    return (gram_rows, spectrum)


def two_pieces(values):
    high = values.astype(ml_dtypes.bfloat16)
    low = (values - high.astype(np.float64)).astype(ml_dtypes.bfloat16)
    return np.concatenate([high, low], 0)


def half_rows(nf):
    steps = np.arange(NFFT // 2)
    phase = 2.0 * np.pi * (np.arange(nf + 1)[:, None] * steps[None, :] % NFFT) / NFFT
    real, imag = np.cos(phase), -np.sin(phase)
    main = np.concatenate([real[:nf], imag[:nf]], 0)
    main[nf] = real[nf]
    return main, imag[nf : nf + 1]


def make_tables(nf, pieces):
    main, extra = half_rows(nf)
    half = NFFT // 2
    width = 2 * nf
    both = np.zeros((2 * width + max(2 * pieces, 8), NFFT))
    for h in range(2):
        both[h * width : (h + 1) * width, h * half : (h + 1) * half] = main
        both[2 * width + h : 2 * width + 2 * pieces : 2, h * half : (h + 1) * half] = extra
    last = np.zeros((width + 16, half))
    last[:width] = main
    last[width] = extra[0]
    return two_pieces(both), two_pieces(last)


def make_combine(nf, nb, pieces):
    width = 2 * nf
    main_rows = nb * width
    ext_rows = nb * pieces
    combine = np.zeros((2, nf, nb, main_rows + ext_rows + width + 16))

    def columns(m, f, part):
        if f == nf and part == 1:
            if m == nb:
                return [main_rows + ext_rows + width]
            first = main_rows + m // 2 * 2 * pieces + m % 2
            return [first + 2 * q for q in range(pieces)]
        start = main_rows + ext_rows if m == nb else m * width
        if f == nf:
            return [start + nf]
        if part == 1 and f == 0:
            return []
        return [start + part * nf + f]

    for f in range(nf):
        for b in range(nb):
            for m in (b, b + 1):
                second = m - b
                sign = (-1.0) ** f if second else 1.0
                side = 0.25 if second else -0.25
                for part in range(2):
                    for g, weight in ((f, 0.5), (f - 1, side), (f + 1, side)):
                        flip = -1.0 if g < 0 and part == 1 else 1.0
                        for column in columns(m, abs(g), part):
                            combine[part, f, b, column] += sign * flip * weight
    return combine.reshape(2 * nf * nb, -1).astype(ml_dtypes.bfloat16)


def xor_index(index, other, count):
    result = 0
    bit = 1
    while bit < count:
        digit = lax.rem(index // bit, 2)
        result = result + bit * ((1 - digit) if other & bit else digit)
        bit *= 2
    return result


def nt_dot(left, right):
    return lax.dot_general(
        left, right, (((1,), (1,)), ((), ())), preferred_element_type=jnp.float32
    )


def leading_value(g_re, g_im, nb):
    shape = g_re.shape
    row = lax.broadcasted_iota(jnp.int32, shape, 0)
    lane = lax.broadcasted_iota(jnp.int32, shape, 1)
    entries = 2.0 * nb

    def lane_sum(x):
        step = 1
        while step < nb:
            ahead = pltpu.roll(x, LANES - step, 1)
            behind = pltpu.roll(x, step, 1)
            x = x + jnp.where(lane % (2 * step) < step, ahead, behind)
            step *= 2
        return x

    def row_sum(x):
        return jnp.broadcast_to(jnp.sum(x, axis=0, keepdims=True), shape)

    def to_lanes(v_re, v_im):
        return row_sum(g_re * v_re + g_im * v_im), row_sum(g_re * v_im - g_im * v_re)

    def to_rows(v_re, v_im):
        return lane_sum(g_re * v_re - g_im * v_im), lane_sum(g_re * v_im + g_im * v_re)

    v_re, v_im = jnp.ones(shape, jnp.float32), jnp.zeros(shape, jnp.float32)
    for step in range(POWER):
        if step % 2 == 0:
            u_re, u_im = to_lanes(v_re, v_im)
            scale = lax.rsqrt(lane_sum(u_re * u_re + u_im * u_im) / entries + 1e-06)
            v_re, v_im = u_re, u_im
        else:
            u_re, u_im = to_rows(v_re, v_im)
            u_re, u_im = u_re * scale, u_im * scale
            scale = lax.rsqrt(row_sum(u_re * u_re + u_im * u_im) / entries + 1e-06)
            v_re, v_im = u_re * scale, u_im * scale
    u_re, u_im = to_lanes(v_re, v_im)
    here = lane % nb == row
    across_re = row_sum(jnp.where(here, v_re, 0.0))
    across_im = row_sum(jnp.where(here, v_im, 0.0))
    top = lane_sum(across_re * u_re + across_im * u_im) / entries
    return top / (row_sum(v_re * v_re + v_im * v_im) / entries + 1e-06)


def kernel(
    zs, ns, nf, nb, scale, spans, inner,
    snap_ref, tail_ref, const_ref, gram_ref, value_ref,
    x_buf, tail_buf, last_buf, const,
    send, send_ext, recv, recv_ext, z_part, z_recv, s_recv,
    x_sem, const_sem, send_sem, recv_sem, ext_send_sem, ext_recv_sem,
    z_send_sem, z_recv_sem, s_send_sem, s_recv_sem,
):
    my_s, my_z = lax.axis_index("space"), lax.axis_index("freq")
    quarter = snap_ref.shape[0] // zs
    sub = quarter // SUBS
    width = 2 * nf
    pieces = sub // LANES
    far = list(range(zs // 2, zs))
    near = list(range(1, zs // 2))
    beside = lax.rem((my_z + zs // 4) // (zs // 2), 2)
    order = list(range(1, zs))
    steps = {0: 0}
    peers = {0: my_z}
    for i, (inner_k, outer_k) in enumerate(zip(near + far, far + near), 1):
        steps[i] = beside * inner_k + (1 - beside) * outer_k
        peers[i] = beside * xor_index(my_z, inner_k, zs) + (1 - beside) * xor_index(
            my_z, outer_k, zs
        )
    friends = {k: xor_index(my_s, k, ns) for k in range(1, ns)}

    barrier = pltpu.get_barrier_semaphore()
    for k in order:
        pl.semaphore_signal(barrier, inc=1, device_id=(my_s, peers[k]), device_id_type=MESH)
    for k in range(1, ns):
        pl.semaphore_signal(barrier, inc=1, device_id=(friends[k], my_z), device_id_type=MESH)

    loads = {}
    (t0, t1), (l0, l1), (c0, c1) = spans
    constants = [
        pltpu.make_async_copy(const_ref.at[a:b], const.at[a:b], const_sem.at[i])
        for i, (a, b) in enumerate(spans)
    ] + [
        pltpu.make_async_copy(
            tail_ref.at[pl.ds(pl.multiple_of(my_z * quarter, quarter), quarter)],
            tail_buf, const_sem.at[3],
        ),
    ]
    constants[0].start()
    for s in range(SUBS):
        for k in order + [0]:
            first = pl.multiple_of(peers[k] * quarter + s * sub, sub)
            loads[k, s] = pltpu.make_async_copy(
                snap_ref.at[pl.ds(first, sub)], x_buf.at[k, s], x_sem.at[k, s]
            )
            loads[k, s].start()
    for copy in constants[1:]:
        copy.start()

    ext_row = lax.broadcasted_iota(jnp.int32, (2 * pieces, LANES), 0) // 2

    def transform(k, s):
        loads[k, s].wait()
        both = nt_dot(const[t0:t1, : x_buf.shape[3]], x_buf[k, s])
        rows = both.shape[0] // 2
        both = both[:rows] + both[rows:]
        extra = jnp.zeros((2 * pieces, LANES), jnp.float32)
        for q in range(pieces):
            extra = jnp.where(
                ext_row == q, both[2 * width : 2 * width + 2 * pieces, q * LANES : (q + 1) * LANES], extra
            )
        return both[: 2 * width].astype(jnp.bfloat16), extra

    constants[0].wait()
    copies = {}
    for s in range(SUBS):
        for k in order:
            main, extra = transform(k, s)
            send[k, s] = main
            send_ext[k, s] = extra
            if s == 0 and k == order[0]:
                pl.semaphore_wait(barrier, zs - 1 + ns - 1)
            target = (my_s, peers[k])
            copies[k, s] = [
                pltpu.make_async_remote_copy(
                    send_ext.at[k, s], recv_ext.at[my_z, s],
                    ext_send_sem.at[k, s], ext_recv_sem.at[steps[k], s],
                    device_id=target, device_id_type=MESH,
                ),
                pltpu.make_async_remote_copy(
                    send.at[k, s], recv.at[my_z, s],
                    send_sem.at[k, s], recv_sem.at[steps[k], s],
                    device_id=target, device_id_type=MESH,
                ),
            ]
            for copy in copies[k, s]:
                copy.start()
    for s in range(SUBS):
        main, extra = transform(0, s)
        recv[my_z, s] = main
        recv_ext[my_z, s] = extra
    for copy in constants[1:]:
        copy.wait()
    for s in range(SUBS):
        last = nt_dot(const[l0:l1, : tail_buf.shape[1]], tail_buf[s * sub : (s + 1) * sub])
        rows = last.shape[0] // 2
        last_buf[s] = (last[:rows] + last[rows:]).astype(jnp.bfloat16)

    gram = jnp.zeros((width * nb, width * nb), jnp.float32)
    for s in range(SUBS):
        for k in order:
            for copy in copies[k, s]:
                copy.wait_recv()
        extras = []
        for d in range(zs):
            extra = recv_ext[d, s]
            extras.append(
                jnp.concatenate([jnp.where(ext_row == q, extra, 0.0) for q in range(pieces)], 1)
            )
        stacked = jnp.concatenate(
            [recv[d, s] for d in range(zs)]
            + [jnp.concatenate(extras, 0).astype(jnp.bfloat16), last_buf[s]],
            0,
        )
        coef = jnp.dot(const[c0:c1, :inner], stacked, preferred_element_type=jnp.float32)
        coef = coef.astype(jnp.bfloat16)
        gram = gram + nt_dot(coef, coef)

    side = nf * nb
    real = gram[:side, :side] + gram[side:, side:]
    imag = gram[:side, side:] - gram[side:, :side]
    lane_freq = lax.broadcasted_iota(jnp.int32, (nb, side), 1) // nb
    g_re = jnp.zeros((nb, side), jnp.float32)
    g_im = jnp.zeros((nb, side), jnp.float32)
    for f in range(nf):
        g_re = jnp.where(lane_freq == f, real[f * nb : (f + 1) * nb], g_re)
        g_im = jnp.where(lane_freq == f, imag[f * nb : (f + 1) * nb], g_im)
    z_part[0] = g_re * scale
    z_part[1] = g_im * scale

    z_copies = []
    for k in order:
        copy = pltpu.make_async_remote_copy(
            z_part, z_recv.at[steps[k]], z_send_sem.at[k], z_recv_sem.at[steps[k]],
            device_id=(my_s, peers[k]), device_id_type=MESH,
        )
        copy.start()
        z_copies.append(copy)
    for copy in z_copies:
        copy.wait_recv()
    total = z_part[...]
    for k in order:
        total = total + z_recv[k]
    s_recv[my_s] = total
    s_copies = []
    for k in range(1, ns):
        copy = pltpu.make_async_remote_copy(
            s_recv.at[my_s], s_recv.at[my_s], s_send_sem.at[k], s_recv_sem.at[k],
            device_id=(friends[k], my_z), device_id_type=MESH,
        )
        copy.start()
        s_copies.append(copy)
    for copy in s_copies:
        copy.wait_recv()
    total = s_recv[0]
    for d in range(1, ns):
        total = total + s_recv[d]
    g_re, g_im = total[0], total[1]

    value = leading_value(g_re, g_im, nb)
    row = lax.broadcasted_iota(jnp.int32, (nb, side), 0)
    mine = row == my_s
    row_re = jnp.sum(jnp.where(mine, g_re, 0.0), axis=0, keepdims=True)
    row_im = jnp.sum(jnp.where(mine, g_im, 0.0), axis=0, keepdims=True)
    group = FREQ_DEV * nb
    result = jnp.where(row % 2 == 0, row_re, row_im)
    placed, spread = result, value
    for z in range(1, zs):
        placed = jnp.where(my_z == z, pltpu.roll(result, LANES - z * group, 1), placed)
        spread = jnp.where(my_z == z, pltpu.roll(value, LANES - z * group, 1), spread)
    rows, values = placed, spread
    lane = lax.broadcasted_iota(jnp.int32, (nb, side), 1)
    for f in range(1, FREQ_DEV):
        rows = jnp.where(row // 2 == f, pltpu.roll(placed, LANES - f * nb, 1), rows)
        values = jnp.where(lane == f, pltpu.roll(spread, LANES - f * (nb - 1), 1), values)
    gram_ref[...] = rows
    value_ref[...] = values

    for group_copies in copies.values():
        for copy in group_copies:
            copy.wait_send()
    for copy in z_copies + s_copies:
        copy.wait_send()


def shards_kernel(zs, ns, snapshots, tail):
    points, steps = snapshots.shape
    nf = FREQ_DEV * zs
    nb = 2 * zs
    sub = points // zs // SUBS
    pieces = sub // LANES
    width = 2 * nf
    table, tail_table = make_tables(nf, pieces)
    combine = make_combine(nf, nb, pieces)
    window = 0.5 - 0.5 * np.cos(2.0 * np.pi * np.arange(NFFT) / NFFT)
    scale = float(1.0 / (points * ns * np.sum(window * window)))
    parts = [table, tail_table, combine]
    inner = combine.shape[1]
    padded = -(-inner // LANES) * LANES
    const = np.concatenate([np.pad(p, ((0, 0), (0, padded - p.shape[1]))) for p in parts], 0)
    ends = np.cumsum([p.shape[0] for p in parts]).tolist()
    spans = list(zip([0] + ends[:-1], ends))
    dma = pltpu.SemaphoreType.DMA
    flops = 2 * points * steps * table.shape[0]
    gram, values = pl.pallas_call(
        functools.partial(kernel, zs, ns, nf, nb, scale, spans, inner),
        out_shape=[jax.ShapeDtypeStruct((nb, LANES), jnp.float32)] * 2,
        in_specs=[pl.BlockSpec(memory_space=pltpu.HBM)] * 3,
        out_specs=[pl.BlockSpec(memory_space=pltpu.VMEM)] * 2,
        scratch_shapes=[
            pltpu.VMEM((zs, SUBS, sub, steps), jnp.bfloat16),
            pltpu.VMEM((points // zs, tail.shape[1]), jnp.bfloat16),
            pltpu.VMEM((SUBS, tail_table.shape[0] // 2, sub), jnp.bfloat16),
            pltpu.VMEM(const.shape, jnp.bfloat16),
            pltpu.VMEM((zs, SUBS, 2 * width, sub), jnp.bfloat16),
            pltpu.VMEM((zs, SUBS, 2 * pieces, LANES), jnp.float32),
            pltpu.VMEM((zs, SUBS, 2 * width, sub), jnp.bfloat16),
            pltpu.VMEM((zs, SUBS, 2 * pieces, LANES), jnp.float32),
            pltpu.VMEM((2, nb, LANES), jnp.float32),
            pltpu.VMEM((zs, 2, nb, LANES), jnp.float32),
            pltpu.VMEM((ns, 2, nb, LANES), jnp.float32),
            dma((zs, SUBS)), dma((4,)),
            dma((zs, SUBS)), dma((zs, SUBS)), dma((zs, SUBS)), dma((zs, SUBS)),
            dma((zs,)), dma((zs,)), dma((ns,)), dma((ns,)),
        ],
        compiler_params=pltpu.CompilerParams(
            collective_id=0, has_side_effects=True, vmem_limit_bytes=55040 * 1024
        ),
        cost_estimate=pl.CostEstimate(
            flops=flops, bytes_accessed=points * steps * 2, transcendentals=0
        ),
    )(snapshots, tail, jnp.asarray(const))
    return gram[:, :nb].reshape(FREQ_DEV, 2, 1, nb), values[0, :FREQ_DEV]


def power_of_two(count):
    return count > 1 and count & (count - 1) == 0


def shards(snapshots, tail):
    zs, ns = lax.axis_size("freq"), lax.axis_size("space")
    points, steps = snapshots.shape
    nb = zs * steps // (NFFT // 2)
    packs = FREQ_DEV * zs * nb == LANES and steps == NFFT and nb == ns == 8
    whole = points % (zs * SUBS * LANES) == 0
    if packs and whole and power_of_two(zs) and power_of_two(ns):
        return shards_kernel(zs, ns, snapshots, tail)
    return shards_general(snapshots, tail)


def solution(mesh):
    in_specs = (P("space", "freq"), P("space", None))
    out_specs = (P("freq", None, "space", None), P("freq"))
    return jax.shard_map(shards, mesh=mesh, in_specs=in_specs, out_specs=out_specs, check_vma=False)
```

```python
import functools
import math

import jax
import jax.numpy as jnp
import ml_dtypes
import numpy as np
from jax import lax
from jax.experimental import pallas as pl
from jax.experimental.pallas import tpu as pltpu
from jax.sharding import PartitionSpec as P

FREQ_DEV = 4
NFFT = 256
POWER = 4
LANES = 128
SUBS = 4
MESH = pl.DeviceIdType.MESH


def shifted(value, axis, steps):
    count = lax.axis_size(axis)
    initial, last = (max(0, -steps), min(count, count - steps))
    return lax.ppermute(value, axis, [(source, source + steps) for source in range(initial, last)])


def build_table(count):
    steps = jnp.arange(NFFT, dtype=jnp.int32)
    freqs = jnp.arange(count, dtype=jnp.int32)
    window = 0.5 - 0.5 * jnp.cos(2.0 * math.pi * steps.astype(jnp.float32) / NFFT)
    phase = 2.0 * math.pi * (steps[:, None] * freqs[None, :] % NFFT).astype(jnp.float32) / NFFT
    table = jnp.concatenate(
        [window[:, None] * jnp.cos(phase), -window[:, None] * jnp.sin(phase)], 1
    )
    return (table.astype(jnp.bfloat16), jnp.sum(window * window))


def transform(extended, table):
    points, width = extended.shape
    half = NFFT // 2
    count = width // half - 1
    halves = extended.reshape(points, count + 1, half)
    blocks = jnp.concatenate([halves[:, :-1], halves[:, 1:]], 2)
    coef = jnp.einsum("pbt,tk->bkp", blocks, table, preferred_element_type=jnp.float32)
    return coef.reshape(count, 2, table.shape[1] // 2, points).astype(jnp.bfloat16)


def gram_terms(coef, scale):
    big = jnp.einsum("bcfp,gdfp->fcbdg", coef, coef, preferred_element_type=jnp.float32)
    real = big[:, 0, :, 0, :] + big[:, 1, :, 1, :]
    imag = big[:, 0, :, 1, :] - big[:, 1, :, 0, :]
    return jnp.stack([real, imag], 1) * scale


def apply_matrix(matrix, vector):
    high = lax.Precision.HIGHEST
    m_real, m_imag = (matrix[:, 0], matrix[:, 1])
    v_real, v_imag = (vector[:, 0], vector[:, 1])
    u_real = jnp.einsum("fjk,fk->fj", m_real, v_real, precision=high) - jnp.einsum(
        "fjk,fk->fj", m_imag, v_imag, precision=high
    )
    u_imag = jnp.einsum("fjk,fk->fj", m_real, v_imag, precision=high) + jnp.einsum(
        "fjk,fk->fj", m_imag, v_real, precision=high
    )
    return jnp.stack([u_real, u_imag], 1)


def rescale(product):
    return product / jnp.sqrt(jnp.mean(product * product, axis=(1, 2), keepdims=True) + 1e-06)


def rayleigh(vector, product):
    return jnp.mean(vector * product, axis=(1, 2)) / (
        jnp.mean(vector * vector, axis=(1, 2)) + 1e-06
    )


def shards_general(snapshots, tail):
    points = snapshots.shape[0]
    freq_count = lax.axis_size("freq")
    half = NFFT // 2
    table, wsum = build_table(FREQ_DEV * freq_count)
    scale = 1.0 / (points * lax.axis_size("space") * wsum)
    following = shifted(snapshots[:, :half], "freq", -1)
    is_last = lax.axis_index("freq") == freq_count - 1
    following = jnp.where(is_last, tail, following)
    extended = jnp.concatenate([snapshots, following], 1)
    coef = transform(extended, table)
    regrouped = lax.all_to_all(coef, "freq", split_axis=2, concat_axis=0, tiled=True)
    partial_value = gram_terms(regrouped, scale)
    blocks_all = partial_value.shape[2]
    held = blocks_all // lax.axis_size("space")
    vector = jnp.stack(
        [
            jnp.ones((FREQ_DEV, blocks_all), jnp.float32),
            jnp.zeros((FREQ_DEV, blocks_all), jnp.float32),
        ],
        1,
    )
    total = lax.psum(partial_value, "space")
    for step in range(POWER):
        vector = rescale(apply_matrix(total, vector))
    spectrum = rayleigh(vector, apply_matrix(total, vector))
    gram_rows = lax.dynamic_slice_in_dim(total, lax.axis_index("space") * held, held, 2)
    return (gram_rows, spectrum)


def two_pieces(values):
    high = values.astype(ml_dtypes.bfloat16)
    low = (values - high.astype(np.float64)).astype(ml_dtypes.bfloat16)
    return np.concatenate([high, low], 0)


def half_rows(nf):
    steps = np.arange(NFFT // 2)
    phase = 2.0 * np.pi * (np.arange(nf + 1)[:, None] * steps[None, :] % NFFT) / NFFT
    real, imag = np.cos(phase), -np.sin(phase)
    main = np.concatenate([real[:nf], imag[:nf]], 0)
    main[nf] = real[nf]
    return main, imag[nf : nf + 1]


def make_tables(nf, pieces):
    main, extra = half_rows(nf)
    half = NFFT // 2
    width = 2 * nf
    both = np.zeros((2 * width + max(2 * pieces, 8), NFFT))
    for h in range(2):
        both[h * width : (h + 1) * width, h * half : (h + 1) * half] = main
        both[2 * width + h : 2 * width + 2 * pieces : 2, h * half : (h + 1) * half] = extra
    last = np.zeros((width + 16, half))
    last[:width] = main
    last[width] = extra[0]
    return two_pieces(both), two_pieces(last)


def make_combine(nf, nb, pieces):
    width = 2 * nf
    main_rows = nb * width
    ext_rows = nb * pieces
    combine = np.zeros((2, nf, nb, main_rows + ext_rows + width + 16))

    def columns(m, f, part):
        if f == nf and part == 1:
            if m == nb:
                return [main_rows + ext_rows + width]
            first = main_rows + m // 2 * 2 * pieces + m % 2
            return [first + 2 * q for q in range(pieces)]
        start = main_rows + ext_rows if m == nb else m * width
        if f == nf:
            return [start + nf]
        if part == 1 and f == 0:
            return []
        return [start + part * nf + f]

    for f in range(nf):
        for b in range(nb):
            for m in (b, b + 1):
                second = m - b
                sign = (-1.0) ** f if second else 1.0
                side = 0.25 if second else -0.25
                for part in range(2):
                    for g, weight in ((f, 0.5), (f - 1, side), (f + 1, side)):
                        flip = -1.0 if g < 0 and part == 1 else 1.0
                        for column in columns(m, abs(g), part):
                            combine[part, f, b, column] += sign * flip * weight
    return combine.reshape(2 * nf * nb, -1).astype(ml_dtypes.bfloat16)


def xor_index(index, other, count):
    result = 0
    bit = 1
    while bit < count:
        left, right = lax.rem(index // bit, 2), lax.rem(other // bit, 2)
        result = result + bit * (left + right - 2 * left * right)
        bit *= 2
    return result


def nt_dot(left, right):
    return lax.dot_general(
        left, right, (((1,), (1,)), ((), ())), preferred_element_type=jnp.float32
    )


def leading_value(g_re, g_im, nb):
    shape = g_re.shape
    row = lax.broadcasted_iota(jnp.int32, shape, 0)
    lane = lax.broadcasted_iota(jnp.int32, shape, 1)
    entries = 2.0 * nb

    def lane_sum(x):
        step = 1
        while step < nb:
            ahead = pltpu.roll(x, LANES - step, 1)
            behind = pltpu.roll(x, step, 1)
            x = x + jnp.where(lane % (2 * step) < step, ahead, behind)
            step *= 2
        return x

    def row_sum(x):
        return jnp.broadcast_to(jnp.sum(x, axis=0, keepdims=True), shape)

    def to_lanes(v_re, v_im):
        return row_sum(g_re * v_re + g_im * v_im), row_sum(g_re * v_im - g_im * v_re)

    def to_rows(v_re, v_im):
        return lane_sum(g_re * v_re - g_im * v_im), lane_sum(g_re * v_im + g_im * v_re)

    v_re, v_im = jnp.ones(shape, jnp.float32), jnp.zeros(shape, jnp.float32)
    for step in range(POWER):
        if step % 2 == 0:
            u_re, u_im = to_lanes(v_re, v_im)
            scale = lax.rsqrt(lane_sum(u_re * u_re + u_im * u_im) / entries + 1e-06)
            v_re, v_im = u_re, u_im
        else:
            u_re, u_im = to_rows(v_re, v_im)
            u_re, u_im = u_re * scale, u_im * scale
            scale = lax.rsqrt(row_sum(u_re * u_re + u_im * u_im) / entries + 1e-06)
            v_re, v_im = u_re * scale, u_im * scale
    u_re, u_im = to_lanes(v_re, v_im)
    here = lane % nb == row
    across_re = row_sum(jnp.where(here, v_re, 0.0))
    across_im = row_sum(jnp.where(here, v_im, 0.0))
    top = lane_sum(across_re * u_re + across_im * u_im) / entries
    return top / (row_sum(v_re * v_re + v_im * v_im) / entries + 1e-06)


def kernel(
    zs, ns, nf, nb, scale, spans, inner,
    snap_ref, tail_ref, const_ref, gram_ref, value_ref,
    x_buf, tail_buf, last_buf, gram_buf, const,
    send, send_ext, recv, recv_ext, z_part, z_recv, s_recv,
    x_sem, const_sem, send_sem, recv_sem, ext_send_sem, ext_recv_sem,
    z_send_sem, z_recv_sem, s_send_sem, s_recv_sem,
):
    my_s, my_z = lax.axis_index("space"), lax.axis_index("freq")
    quarter = snap_ref.shape[0] // zs
    sub = quarter // SUBS
    width = 2 * nf
    pieces = sub // LANES

    def peer(k):
        return xor_index(my_z, k, zs)

    def friend(k):
        return xor_index(my_s, k, ns)

    barrier = pltpu.get_barrier_semaphore()

    def greet_peer(k, carry):
        pl.semaphore_signal(barrier, inc=1, device_id=(my_s, peer(k)), device_id_type=MESH)
        return carry

    def greet_friend(k, carry):
        pl.semaphore_signal(barrier, inc=1, device_id=(friend(k), my_z), device_id_type=MESH)
        return carry

    lax.fori_loop(1, zs, greet_peer, 0)
    lax.fori_loop(1, ns, greet_friend, 0)

    (t0, t1), (l0, l1), (c0, c1) = spans
    constants = [
        pltpu.make_async_copy(const_ref.at[a:b], const.at[a:b], const_sem.at[i])
        for i, (a, b) in enumerate(spans)
    ] + [
        pltpu.make_async_copy(
            tail_ref.at[pl.ds(pl.multiple_of(my_z * quarter, quarter), quarter)],
            tail_buf, const_sem.at[3],
        ),
    ]

    def place(t):
        return lax.rem(t + zs // 2, zs), t // zs

    def load(t):
        k, s = place(t)
        first = pl.multiple_of(peer(k) * quarter + s * sub, sub)
        return pltpu.make_async_copy(
            snap_ref.at[pl.ds(first, sub)], x_buf.at[k, s], x_sem.at[k, s]
        )

    def send_copies(k, s):
        target = (my_s, peer(k))
        return [
            pltpu.make_async_remote_copy(
                send_ext.at[k, s], recv_ext.at[my_z, s],
                ext_send_sem.at[k, s], ext_recv_sem.at[k, s],
                device_id=target, device_id_type=MESH,
            ),
            pltpu.make_async_remote_copy(
                send.at[k, s], recv.at[my_z, s],
                send_sem.at[k, s], recv_sem.at[k, s],
                device_id=target, device_id_type=MESH,
            ),
        ]

    def start_load(t, carry):
        load(t).start()
        return carry

    constants[0].start()
    lax.fori_loop(0, zs * SUBS, start_load, 0)
    for copy in constants[1:]:
        copy.start()
    ext_row = lax.broadcasted_iota(jnp.int32, (2 * pieces, LANES), 0) // 2
    constants[0].wait()
    pl.semaphore_wait(barrier, zs - 1 + ns - 1)

    def transform(t, carry):
        k, s = place(t)
        load(t).wait()
        both = nt_dot(const[t0:t1, : x_buf.shape[3]], x_buf[k, s])
        rows = both.shape[0] // 2
        both = both[:rows] + both[rows:]
        extra = jnp.zeros((2 * pieces, LANES), jnp.float32)
        for q in range(pieces):
            extra = jnp.where(
                ext_row == q,
                both[2 * width : 2 * width + 2 * pieces, q * LANES : (q + 1) * LANES],
                extra,
            )
        main = both[: 2 * width].astype(jnp.bfloat16)

        @pl.when(k == 0)
        def _():
            recv[my_z, s] = main
            recv_ext[my_z, s] = extra

        @pl.when(k > 0)
        def _():
            send[k, s] = main
            send_ext[k, s] = extra
            for copy in send_copies(k, s):
                copy.start()

        return carry

    lax.fori_loop(0, zs * SUBS, transform, 0)

    for copy in constants[1:]:
        copy.wait()

    def transform_tail(s, carry):
        points = tail_buf[pl.ds(pl.multiple_of(s * sub, sub), sub)]
        last = nt_dot(const[l0:l1, : tail_buf.shape[1]], points)
        rows = last.shape[0] // 2
        last_buf[s] = (last[:rows] + last[rows:]).astype(jnp.bfloat16)
        return carry

    lax.fori_loop(0, SUBS, transform_tail, 0)
    gram_buf[...] = jnp.zeros(gram_buf.shape, jnp.float32)

    def combine(s, carry):
        for k in range(1, zs):
            for copy in send_copies(k, s):
                copy.wait_recv()
        extras = []
        for d in range(zs):
            extra = recv_ext[d, s]
            extras.append(
                jnp.concatenate([jnp.where(ext_row == q, extra, 0.0) for q in range(pieces)], 1)
            )
        stacked = jnp.concatenate(
            [recv[d, s] for d in range(zs)]
            + [jnp.concatenate(extras, 0).astype(jnp.bfloat16), last_buf[s]],
            0,
        )
        coef = jnp.dot(const[c0:c1, :inner], stacked, preferred_element_type=jnp.float32)
        coef = coef.astype(jnp.bfloat16)
        gram_buf[...] += nt_dot(coef, coef)
        return carry

    lax.fori_loop(0, SUBS, combine, 0)

    side = nf * nb
    real = gram_buf[:side, :side] + gram_buf[side:, side:]
    imag = gram_buf[:side, side:] - gram_buf[side:, :side]
    lane_freq = lax.broadcasted_iota(jnp.int32, (nb, side), 1) // nb
    g_re = jnp.zeros((nb, side), jnp.float32)
    g_im = jnp.zeros((nb, side), jnp.float32)
    for f in range(nf):
        g_re = jnp.where(lane_freq == f, real[f * nb : (f + 1) * nb], g_re)
        g_im = jnp.where(lane_freq == f, imag[f * nb : (f + 1) * nb], g_im)
    z_part[0] = g_re * scale
    z_part[1] = g_im * scale

    def z_copy(k):
        return pltpu.make_async_remote_copy(
            z_part, z_recv.at[k], z_send_sem.at[k], z_recv_sem.at[k],
            device_id=(my_s, peer(k)), device_id_type=MESH,
        )

    def s_copy(k):
        return pltpu.make_async_remote_copy(
            s_recv.at[my_s], s_recv.at[my_s], s_send_sem.at[k], s_recv_sem.at[k],
            device_id=(friend(k), my_z), device_id_type=MESH,
        )

    def run(first, last, action):
        def body(k, carry):
            action(k)
            return carry

        lax.fori_loop(first, last, body, 0)

    run(1, zs, lambda k: z_copy(k).start())
    run(1, zs, lambda k: z_copy(k).wait_recv())
    total = z_part[...]
    for k in range(1, zs):
        total = total + z_recv[k]
    s_recv[my_s] = total
    run(1, ns, lambda k: s_copy(k).start())
    run(1, ns, lambda k: s_copy(k).wait_recv())
    total = s_recv[0]
    for d in range(1, ns):
        total = total + s_recv[d]
    g_re, g_im = total[0], total[1]

    value = leading_value(g_re, g_im, nb)
    row = lax.broadcasted_iota(jnp.int32, (nb, side), 0)
    mine = row == my_s
    row_re = jnp.sum(jnp.where(mine, g_re, 0.0), axis=0, keepdims=True)
    row_im = jnp.sum(jnp.where(mine, g_im, 0.0), axis=0, keepdims=True)
    group = FREQ_DEV * nb
    result = jnp.where(row % 2 == 0, row_re, row_im)
    placed, spread = result, value
    for z in range(1, zs):
        placed = jnp.where(my_z == z, pltpu.roll(result, LANES - z * group, 1), placed)
        spread = jnp.where(my_z == z, pltpu.roll(value, LANES - z * group, 1), spread)
    rows, values = placed, spread
    lane = lax.broadcasted_iota(jnp.int32, (nb, side), 1)
    for f in range(1, FREQ_DEV):
        rows = jnp.where(row // 2 == f, pltpu.roll(placed, LANES - f * nb, 1), rows)
        values = jnp.where(lane == f, pltpu.roll(spread, LANES - f * (nb - 1), 1), values)
    gram_ref[...] = rows
    value_ref[...] = values

    def finish(k):
        for s in range(SUBS):
            for copy in send_copies(k, s):
                copy.wait_send()
        z_copy(k).wait_send()

    run(1, zs, finish)
    run(1, ns, lambda k: s_copy(k).wait_send())


def shards_kernel(zs, ns, snapshots, tail):
    points, steps = snapshots.shape
    nf = FREQ_DEV * zs
    nb = 2 * zs
    sub = points // zs // SUBS
    pieces = sub // LANES
    width = 2 * nf
    table, tail_table = make_tables(nf, pieces)
    combine = make_combine(nf, nb, pieces)
    window = 0.5 - 0.5 * np.cos(2.0 * np.pi * np.arange(NFFT) / NFFT)
    scale = float(1.0 / (points * ns * np.sum(window * window)))
    parts = [table, tail_table, combine]
    inner = combine.shape[1]
    padded = -(-inner // LANES) * LANES
    const = np.concatenate([np.pad(p, ((0, 0), (0, padded - p.shape[1]))) for p in parts], 0)
    ends = np.cumsum([p.shape[0] for p in parts]).tolist()
    spans = list(zip([0] + ends[:-1], ends))
    dma = pltpu.SemaphoreType.DMA
    flops = 2 * points * steps * table.shape[0]
    gram, values = pl.pallas_call(
        functools.partial(kernel, zs, ns, nf, nb, scale, spans, inner),
        out_shape=[jax.ShapeDtypeStruct((nb, LANES), jnp.float32)] * 2,
        in_specs=[pl.BlockSpec(memory_space=pltpu.HBM)] * 3,
        out_specs=[pl.BlockSpec(memory_space=pltpu.VMEM)] * 2,
        scratch_shapes=[
            pltpu.VMEM((zs, SUBS, sub, steps), jnp.bfloat16),
            pltpu.VMEM((points // zs, tail.shape[1]), jnp.bfloat16),
            pltpu.VMEM((SUBS, tail_table.shape[0] // 2, sub), jnp.bfloat16),
            pltpu.VMEM((width * nb, width * nb), jnp.float32),
            pltpu.VMEM(const.shape, jnp.bfloat16),
            pltpu.VMEM((zs, SUBS, 2 * width, sub), jnp.bfloat16),
            pltpu.VMEM((zs, SUBS, 2 * pieces, LANES), jnp.float32),
            pltpu.VMEM((zs, SUBS, 2 * width, sub), jnp.bfloat16),
            pltpu.VMEM((zs, SUBS, 2 * pieces, LANES), jnp.float32),
            pltpu.VMEM((2, nb, LANES), jnp.float32),
            pltpu.VMEM((zs, 2, nb, LANES), jnp.float32),
            pltpu.VMEM((ns, 2, nb, LANES), jnp.float32),
            dma((zs, SUBS)), dma((4,)),
            dma((zs, SUBS)), dma((zs, SUBS)), dma((zs, SUBS)), dma((zs, SUBS)),
            dma((zs,)), dma((zs,)), dma((ns,)), dma((ns,)),
        ],
        compiler_params=pltpu.CompilerParams(
            collective_id=0, has_side_effects=True, vmem_limit_bytes=55040 * 1024
        ),
        cost_estimate=pl.CostEstimate(
            flops=flops, bytes_accessed=points * steps * 2, transcendentals=0
        ),
    )(snapshots, tail, jnp.asarray(const))
    return gram[:, :nb].reshape(FREQ_DEV, 2, 1, nb), values[0, :FREQ_DEV]


def power_of_two(count):
    return count > 1 and count & (count - 1) == 0


def shards(snapshots, tail):
    zs, ns = lax.axis_size("freq"), lax.axis_size("space")
    points, steps = snapshots.shape
    nb = zs * steps // (NFFT // 2)
    packs = FREQ_DEV * zs * nb == LANES and steps == NFFT and nb == ns == 8
    whole = points % (zs * SUBS * LANES) == 0
    if packs and whole and power_of_two(zs) and power_of_two(ns):
        return shards_kernel(zs, ns, snapshots, tail)
    return shards_general(snapshots, tail)


def solution(mesh):
    in_specs = (P("space", "freq"), P("space", None))
    out_specs = (P("freq", None, "space", None), P("freq"))
    return jax.shard_map(shards, mesh=mesh, in_specs=in_specs, out_specs=out_specs, check_vma=False)
```

```python
import functools
import math

import jax
import jax.numpy as jnp
import ml_dtypes
import numpy as np
from jax import lax
from jax.experimental import pallas as pl
from jax.experimental.pallas import tpu as pltpu
from jax.sharding import PartitionSpec as P

FREQ_DEV = 4
NFFT = 256
POWER = 4
LANES = 128
SUBS = 4
MESH = pl.DeviceIdType.MESH


def shifted(value, axis, steps):
    count = lax.axis_size(axis)
    initial, last = (max(0, -steps), min(count, count - steps))
    return lax.ppermute(value, axis, [(source, source + steps) for source in range(initial, last)])


def build_table(count):
    steps = jnp.arange(NFFT, dtype=jnp.int32)
    freqs = jnp.arange(count, dtype=jnp.int32)
    window = 0.5 - 0.5 * jnp.cos(2.0 * math.pi * steps.astype(jnp.float32) / NFFT)
    phase = 2.0 * math.pi * (steps[:, None] * freqs[None, :] % NFFT).astype(jnp.float32) / NFFT
    table = jnp.concatenate(
        [window[:, None] * jnp.cos(phase), -window[:, None] * jnp.sin(phase)], 1
    )
    return (table.astype(jnp.bfloat16), jnp.sum(window * window))


def transform(extended, table):
    points, width = extended.shape
    half = NFFT // 2
    count = width // half - 1
    halves = extended.reshape(points, count + 1, half)
    blocks = jnp.concatenate([halves[:, :-1], halves[:, 1:]], 2)
    coef = jnp.einsum("pbt,tk->bkp", blocks, table, preferred_element_type=jnp.float32)
    return coef.reshape(count, 2, table.shape[1] // 2, points).astype(jnp.bfloat16)


def gram_terms(coef, scale):
    big = jnp.einsum("bcfp,gdfp->fcbdg", coef, coef, preferred_element_type=jnp.float32)
    real = big[:, 0, :, 0, :] + big[:, 1, :, 1, :]
    imag = big[:, 0, :, 1, :] - big[:, 1, :, 0, :]
    return jnp.stack([real, imag], 1) * scale


def apply_matrix(matrix, vector):
    high = lax.Precision.HIGHEST
    m_real, m_imag = (matrix[:, 0], matrix[:, 1])
    v_real, v_imag = (vector[:, 0], vector[:, 1])
    u_real = jnp.einsum("fjk,fk->fj", m_real, v_real, precision=high) - jnp.einsum(
        "fjk,fk->fj", m_imag, v_imag, precision=high
    )
    u_imag = jnp.einsum("fjk,fk->fj", m_real, v_imag, precision=high) + jnp.einsum(
        "fjk,fk->fj", m_imag, v_real, precision=high
    )
    return jnp.stack([u_real, u_imag], 1)


def rescale(product):
    return product / jnp.sqrt(jnp.mean(product * product, axis=(1, 2), keepdims=True) + 1e-06)


def rayleigh(vector, product):
    return jnp.mean(vector * product, axis=(1, 2)) / (
        jnp.mean(vector * vector, axis=(1, 2)) + 1e-06
    )


def shards_general(snapshots, tail):
    points = snapshots.shape[0]
    freq_count = lax.axis_size("freq")
    half = NFFT // 2
    table, wsum = build_table(FREQ_DEV * freq_count)
    scale = 1.0 / (points * lax.axis_size("space") * wsum)
    following = shifted(snapshots[:, :half], "freq", -1)
    is_last = lax.axis_index("freq") == freq_count - 1
    following = jnp.where(is_last, tail, following)
    extended = jnp.concatenate([snapshots, following], 1)
    coef = transform(extended, table)
    regrouped = lax.all_to_all(coef, "freq", split_axis=2, concat_axis=0, tiled=True)
    partial_value = gram_terms(regrouped, scale)
    blocks_all = partial_value.shape[2]
    held = blocks_all // lax.axis_size("space")
    vector = jnp.stack(
        [
            jnp.ones((FREQ_DEV, blocks_all), jnp.float32),
            jnp.zeros((FREQ_DEV, blocks_all), jnp.float32),
        ],
        1,
    )
    total = lax.psum(partial_value, "space")
    for step in range(POWER):
        vector = rescale(apply_matrix(total, vector))
    spectrum = rayleigh(vector, apply_matrix(total, vector))
    gram_rows = lax.dynamic_slice_in_dim(total, lax.axis_index("space") * held, held, 2)
    return (gram_rows, spectrum)


def two_pieces(values):
    high = values.astype(ml_dtypes.bfloat16)
    low = (values - high.astype(np.float64)).astype(ml_dtypes.bfloat16)
    return np.concatenate([high, low], 0)


def half_rows(nf):
    steps = np.arange(NFFT // 2)
    phase = 2.0 * np.pi * (np.arange(nf + 1)[:, None] * steps[None, :] % NFFT) / NFFT
    real, imag = np.cos(phase), -np.sin(phase)
    main = np.concatenate([real[:nf], imag[:nf]], 0)
    main[nf] = real[nf]
    return main, imag[nf : nf + 1]


def make_tables(nf, pieces):
    main, extra = half_rows(nf)
    half = NFFT // 2
    width = 2 * nf
    both = np.zeros((2 * width, NFFT))
    extras = np.zeros((2 * pieces, NFFT))
    for h in range(2):
        both[h * width : (h + 1) * width, h * half : (h + 1) * half] = main
        extras[h::2, h * half : (h + 1) * half] = extra
    last = np.zeros((width + 16, half))
    last[:width] = main
    last[width] = extra[0]
    return two_pieces(both), two_pieces(extras), two_pieces(last)


def make_combine(nf, nb, pieces):
    width = 2 * nf
    main_rows = nb * width
    ext_rows = nb * pieces
    combine = np.zeros((2, nf, nb, main_rows + ext_rows + width + 16))

    def columns(m, f, part):
        if f == nf and part == 1:
            if m == nb:
                return [main_rows + ext_rows + width]
            first = main_rows + m // 2 * 2 * pieces + m % 2
            return [first + 2 * q for q in range(pieces)]
        start = main_rows + ext_rows if m == nb else m * width
        if f == nf:
            return [start + nf]
        if part == 1 and f == 0:
            return []
        return [start + part * nf + f]

    for f in range(nf):
        for b in range(nb):
            for m in (b, b + 1):
                second = m - b
                sign = (-1.0) ** f if second else 1.0
                side = 0.25 if second else -0.25
                for part in range(2):
                    for g, weight in ((f, 0.5), (f - 1, side), (f + 1, side)):
                        flip = -1.0 if g < 0 and part == 1 else 1.0
                        for column in columns(m, abs(g), part):
                            combine[part, f, b, column] += sign * flip * weight
    return combine.reshape(2 * nf * nb, -1).astype(ml_dtypes.bfloat16)


def xor_index(index, other, count):
    result = 0
    bit = 1
    while bit < count:
        digit = lax.rem(index // bit, 2)
        result = result + bit * ((1 - digit) if other & bit else digit)
        bit *= 2
    return result


def nt_dot(left, right):
    return lax.dot_general(
        left, right, (((1,), (1,)), ((), ())), preferred_element_type=jnp.float32
    )


def leading_value(g_re, g_im, nb):
    shape = g_re.shape
    row = lax.broadcasted_iota(jnp.int32, shape, 0)
    lane = lax.broadcasted_iota(jnp.int32, shape, 1)
    entries = 2.0 * nb

    def lane_sum(x):
        step = 1
        while step < nb:
            ahead = pltpu.roll(x, LANES - step, 1)
            behind = pltpu.roll(x, step, 1)
            x = x + jnp.where(lane % (2 * step) < step, ahead, behind)
            step *= 2
        return x

    def row_sum(x):
        return jnp.broadcast_to(jnp.sum(x, axis=0, keepdims=True), shape)

    def to_lanes(v_re, v_im):
        return row_sum(g_re * v_re + g_im * v_im), row_sum(g_re * v_im - g_im * v_re)

    def to_rows(v_re, v_im):
        return lane_sum(g_re * v_re - g_im * v_im), lane_sum(g_re * v_im + g_im * v_re)

    v_re, v_im = jnp.ones(shape, jnp.float32), jnp.zeros(shape, jnp.float32)
    for step in range(POWER):
        if step % 2 == 0:
            u_re, u_im = to_lanes(v_re, v_im)
            scale = lax.rsqrt(lane_sum(u_re * u_re + u_im * u_im) / entries + 1e-06)
            v_re, v_im = u_re, u_im
        else:
            u_re, u_im = to_rows(v_re, v_im)
            u_re, u_im = u_re * scale, u_im * scale
            scale = lax.rsqrt(row_sum(u_re * u_re + u_im * u_im) / entries + 1e-06)
            v_re, v_im = u_re * scale, u_im * scale
    u_re, u_im = to_lanes(v_re, v_im)
    here = lane % nb == row
    across_re = row_sum(jnp.where(here, v_re, 0.0))
    across_im = row_sum(jnp.where(here, v_im, 0.0))
    top = lane_sum(across_re * u_re + across_im * u_im) / entries
    return top / (row_sum(v_re * v_re + v_im * v_im) / entries + 1e-06)


def kernel(
    zs, ns, nf, nb, scale, spans, inner,
    snap_ref, tail_ref, const_ref, gram_ref, value_ref,
    x_buf, tail_buf, last_buf, const,
    send, send_ext, recv, recv_ext, z_part, z_recv, s_recv,
    x_sem, const_sem, send_sem, recv_sem, ext_send_sem, ext_recv_sem,
    z_send_sem, z_recv_sem, s_send_sem, s_recv_sem,
):
    my_s, my_z = lax.axis_index("space"), lax.axis_index("freq")
    quarter = snap_ref.shape[0] // zs
    sub = quarter // SUBS
    width = 2 * nf
    pieces = quarter // LANES
    here = sub // LANES
    order = list(range(zs // 2, zs)) + list(range(1, zs // 2))
    peers = {k: xor_index(my_z, k, zs) for k in order}
    peers[0] = my_z
    friends = {k: xor_index(my_s, k, ns) for k in range(1, ns)}

    barrier = pltpu.get_barrier_semaphore()
    for k in order:
        pl.semaphore_signal(barrier, inc=1, device_id=(my_s, peers[k]), device_id_type=MESH)
    for k in range(1, ns):
        pl.semaphore_signal(barrier, inc=1, device_id=(friends[k], my_z), device_id_type=MESH)

    loads = {}
    (t0, _), (e0, e1), (l0, l1), (c0, c1) = spans
    constants = [
        pltpu.make_async_copy(const_ref.at[a:b], const.at[a:b], const_sem.at[i])
        for i, (a, b) in enumerate([(t0, e1), (l0, l1), (c0, c1)])
    ] + [
        pltpu.make_async_copy(
            tail_ref.at[pl.ds(pl.multiple_of(my_z * quarter, quarter), quarter)],
            tail_buf, const_sem.at[3],
        ),
    ]
    constants[0].start()
    for s in range(SUBS):
        for k in order + [0]:
            first = pl.multiple_of(peers[k] * quarter + s * sub, sub)
            loads[k, s] = pltpu.make_async_copy(
                snap_ref.at[pl.ds(first, sub)], x_buf.at[k, s], x_sem.at[k, s]
            )
    for k in order:
        loads[k, 0].start()

    ext_row = lax.broadcasted_iota(jnp.int32, (2 * pieces, LANES), 0) // 2

    def folded(x):
        rows = x.shape[0] // 2
        return x[:rows] + x[rows:]

    def transform(k, s):
        return folded(nt_dot(const[t0:e0, : x_buf.shape[3]], x_buf[k, s])).astype(jnp.bfloat16)

    def extras_of(k):
        whole = x_buf[k].reshape(quarter, x_buf.shape[3])
        rows = folded(nt_dot(const[e0:e1, : x_buf.shape[3]], whole))
        extra = jnp.zeros((2 * pieces, LANES), jnp.float32)
        for q in range(pieces):
            extra = jnp.where(ext_row == q, rows[:, q * LANES : (q + 1) * LANES], extra)
        return extra.astype(jnp.bfloat16)

    def started(source, target, send_sems, recv_sems, k):
        copy = pltpu.make_async_remote_copy(
            source, target, send_sems, recv_sems,
            device_id=(my_s, peers[k]), device_id_type=MESH,
        )
        copy.start()
        return copy

    constants[0].wait()
    copies = {}
    for s in range(SUBS):
        for k in order:
            if s < 2:
                loads[k, s].wait()
            send[k, s] = transform(k, s)
            if s == 0 and k == order[0]:
                pl.semaphore_wait(barrier, zs - 1 + ns - 1)
            copies[k, s] = started(
                send.at[k, s], recv.at[my_z, s], send_sem.at[k, s], recv_sem.at[k, s], k
            )
            if s == 0 and k == order[0]:
                for later in range(1, SUBS):
                    for i in order:
                        loads[i, later].start()
                for i in range(SUBS):
                    loads[0, i].start()
                for copy in constants[1:]:
                    copy.start()
        if s == 1:
            for k in order:
                for later in range(2, SUBS):
                    loads[k, later].wait()
                send_ext[k] = extras_of(k)
                copies[k, "ext"] = started(
                    send_ext.at[k], recv_ext.at[my_z], ext_send_sem.at[k], ext_recv_sem.at[k], k
                )
    for s in range(SUBS):
        loads[0, s].wait()
        recv[my_z, s] = transform(0, s)
    recv_ext[my_z] = extras_of(0)
    for copy in constants[1:]:
        copy.wait()
    for s in range(SUBS):
        last = nt_dot(const[l0:l1, : tail_buf.shape[1]], tail_buf[s * sub : (s + 1) * sub])
        rows = last.shape[0] // 2
        last_buf[s] = (last[:rows] + last[rows:]).astype(jnp.bfloat16)

    gram = jnp.zeros((width * nb, width * nb), jnp.float32)
    for s in range(SUBS):
        for k in order:
            copies[k, s].wait_recv()
            if s == 0:
                copies[k, "ext"].wait_recv()
        extras = []
        for d in range(zs):
            extra = recv_ext[d]
            extras.append(
                jnp.concatenate(
                    [
                        jnp.where(ext_row == s * here + q, extra, jnp.zeros_like(extra))
                        for q in range(here)
                    ],
                    1,
                )
            )
        stacked = jnp.concatenate(
            [recv[d, s] for d in range(zs)]
            + extras + [last_buf[s]],
            0,
        )
        coef = jnp.dot(const[c0:c1, :inner], stacked, preferred_element_type=jnp.float32)
        coef = coef.astype(jnp.bfloat16)
        gram = gram + nt_dot(coef, coef)

    side = nf * nb
    real = gram[:side, :side] + gram[side:, side:]
    imag = gram[:side, side:] - gram[side:, :side]
    lane_freq = lax.broadcasted_iota(jnp.int32, (nb, side), 1) // nb
    g_re = jnp.zeros((nb, side), jnp.float32)
    g_im = jnp.zeros((nb, side), jnp.float32)
    for f in range(nf):
        g_re = jnp.where(lane_freq == f, real[f * nb : (f + 1) * nb], g_re)
        g_im = jnp.where(lane_freq == f, imag[f * nb : (f + 1) * nb], g_im)
    group = FREQ_DEV * nb
    lane = lax.broadcasted_iota(jnp.int32, (nb, side), 1)
    packed = []
    for z in range(zs):
        re = pltpu.roll(g_re, (LANES - z * group) % LANES, 1) if z else g_re
        im = pltpu.roll(g_im, (LANES + group - z * group) % LANES, 1) if z != 1 else g_im
        packed.append(jnp.where(lane < group, re, jnp.where(lane < 2 * group, im, 0.0)) * scale)
        z_part[z] = packed[z]

    z_copies = []
    for k in order:
        copy = pltpu.make_async_remote_copy(
            z_part.at[peers[k]], z_recv.at[k], z_send_sem.at[k], z_recv_sem.at[k],
            device_id=(my_s, peers[k]), device_id_type=MESH,
        )
        copy.start()
        z_copies.append(copy)
    total = z_part[my_z]
    for k, copy in zip(order, z_copies):
        copy.wait_recv()
        total = total + z_recv[k]
    s_recv[my_s] = total
    s_copies = []
    for k in range(1, ns):
        copy = pltpu.make_async_remote_copy(
            s_recv.at[my_s], s_recv.at[my_s], s_send_sem.at[k], s_recv_sem.at[k],
            device_id=(friends[k], my_z), device_id_type=MESH,
        )
        copy.start()
        s_copies.append(copy)
    for copy in s_copies:
        copy.wait_recv()
    total = s_recv[0]
    for d in range(1, ns):
        total = total + s_recv[d]
    g_re = jnp.where(lane < group, total, 0.0)
    g_im = jnp.where(lane < group, pltpu.roll(total, LANES - group, 1), 0.0)

    value = leading_value(g_re, g_im, nb)
    row = lax.broadcasted_iota(jnp.int32, (nb, side), 0)
    mine = row == my_s
    row_re = jnp.sum(jnp.where(mine, g_re, 0.0), axis=0, keepdims=True)
    row_im = jnp.sum(jnp.where(mine, g_im, 0.0), axis=0, keepdims=True)
    result = jnp.where(row % 2 == 0, row_re, row_im)
    rows, values = result, value
    for f in range(1, FREQ_DEV):
        rows = jnp.where(row // 2 == f, pltpu.roll(result, LANES - f * nb, 1), rows)
        values = jnp.where(lane == f, pltpu.roll(value, LANES - f * (nb - 1), 1), values)
    gram_ref[...] = rows
    value_ref[...] = values

    for copy in copies.values():
        copy.wait_send()
    for copy in z_copies + s_copies:
        copy.wait_send()


def shards_kernel(zs, ns, snapshots, tail):
    points, steps = snapshots.shape
    nf = FREQ_DEV * zs
    nb = 2 * zs
    sub = points // zs // SUBS
    pieces = points // zs // LANES
    width = 2 * nf
    table, ext_table, tail_table = make_tables(nf, pieces)
    combine = make_combine(nf, nb, pieces)
    window = 0.5 - 0.5 * np.cos(2.0 * np.pi * np.arange(NFFT) / NFFT)
    scale = float(1.0 / (points * ns * np.sum(window * window)))
    parts = [table, ext_table, tail_table, combine]
    inner = combine.shape[1]
    padded = -(-inner // LANES) * LANES
    const = np.concatenate([np.pad(p, ((0, 0), (0, padded - p.shape[1]))) for p in parts], 0)
    ends = np.cumsum([p.shape[0] for p in parts]).tolist()
    spans = list(zip([0] + ends[:-1], ends))
    dma = pltpu.SemaphoreType.DMA
    flops = 2 * points * steps * table.shape[0]
    gram, values = pl.pallas_call(
        functools.partial(kernel, zs, ns, nf, nb, scale, spans, inner),
        out_shape=[jax.ShapeDtypeStruct((nb, LANES), jnp.float32)] * 2,
        in_specs=[pl.BlockSpec(memory_space=pltpu.HBM)] * 3,
        out_specs=[pl.BlockSpec(memory_space=pltpu.VMEM)] * 2,
        scratch_shapes=[
            pltpu.VMEM((zs, SUBS, sub, steps), jnp.bfloat16),
            pltpu.VMEM((points // zs, tail.shape[1]), jnp.bfloat16),
            pltpu.VMEM((SUBS, tail_table.shape[0] // 2, sub), jnp.bfloat16),
            pltpu.VMEM(const.shape, jnp.bfloat16),
            pltpu.VMEM((zs, SUBS, 2 * width, sub), jnp.bfloat16),
            pltpu.VMEM((zs, 2 * pieces, LANES), jnp.bfloat16),
            pltpu.VMEM((zs, SUBS, 2 * width, sub), jnp.bfloat16),
            pltpu.VMEM((zs, 2 * pieces, LANES), jnp.bfloat16),
            pltpu.VMEM((zs, nb, LANES), jnp.float32),
            pltpu.VMEM((zs, nb, LANES), jnp.float32),
            pltpu.VMEM((ns, nb, LANES), jnp.float32),
            dma((zs, SUBS)), dma((4,)),
            dma((zs, SUBS)), dma((zs, SUBS)), dma((zs,)), dma((zs,)),
            dma((zs,)), dma((zs,)), dma((ns,)), dma((ns,)),
        ],
        compiler_params=pltpu.CompilerParams(
            collective_id=0, has_side_effects=True, vmem_limit_bytes=55040 * 1024
        ),
        cost_estimate=pl.CostEstimate(
            flops=flops, bytes_accessed=points * steps * 2, transcendentals=0
        ),
    )(snapshots, tail, jnp.asarray(const))
    return gram[:, :nb].reshape(FREQ_DEV, 2, 1, nb), values[0, :FREQ_DEV]


def power_of_two(count):
    return count > 1 and count & (count - 1) == 0


def shards(snapshots, tail):
    zs, ns = lax.axis_size("freq"), lax.axis_size("space")
    points, steps = snapshots.shape
    nb = zs * steps // (NFFT // 2)
    packs = FREQ_DEV * zs * nb == LANES and steps == NFFT and nb == ns == 8
    whole = points % (zs * SUBS * LANES) == 0
    if packs and whole and power_of_two(zs) and power_of_two(ns):
        return shards_kernel(zs, ns, snapshots, tail)
    return shards_general(snapshots, tail)


def solution(mesh):
    in_specs = (P("space", "freq"), P("space", None))
    out_specs = (P("freq", None, "space", None), P("freq"))
    return jax.shard_map(shards, mesh=mesh, in_specs=in_specs, out_specs=out_specs, check_vma=False)
```

```python
import functools
import math

import jax
import jax.numpy as jnp
import ml_dtypes
import numpy as np
from jax import lax
from jax.experimental import pallas as pl
from jax.experimental.pallas import tpu as pltpu
from jax.sharding import PartitionSpec as P

FREQ_DEV = 4
NFFT = 256
POWER = 4
LANES = 128
SUBS = 4
MESH = pl.DeviceIdType.MESH


def shifted(value, axis, steps):
    count = lax.axis_size(axis)
    initial, last = (max(0, -steps), min(count, count - steps))
    return lax.ppermute(value, axis, [(source, source + steps) for source in range(initial, last)])


def build_table(count):
    steps = jnp.arange(NFFT, dtype=jnp.int32)
    freqs = jnp.arange(count, dtype=jnp.int32)
    window = 0.5 - 0.5 * jnp.cos(2.0 * math.pi * steps.astype(jnp.float32) / NFFT)
    phase = 2.0 * math.pi * (steps[:, None] * freqs[None, :] % NFFT).astype(jnp.float32) / NFFT
    table = jnp.concatenate(
        [window[:, None] * jnp.cos(phase), -window[:, None] * jnp.sin(phase)], 1
    )
    return (table.astype(jnp.bfloat16), jnp.sum(window * window))


def transform(extended, table):
    points, width = extended.shape
    half = NFFT // 2
    count = width // half - 1
    halves = extended.reshape(points, count + 1, half)
    blocks = jnp.concatenate([halves[:, :-1], halves[:, 1:]], 2)
    coef = jnp.einsum("pbt,tk->bkp", blocks, table, preferred_element_type=jnp.float32)
    return coef.reshape(count, 2, table.shape[1] // 2, points).astype(jnp.bfloat16)


def gram_terms(coef, scale):
    big = jnp.einsum("bcfp,gdfp->fcbdg", coef, coef, preferred_element_type=jnp.float32)
    real = big[:, 0, :, 0, :] + big[:, 1, :, 1, :]
    imag = big[:, 0, :, 1, :] - big[:, 1, :, 0, :]
    return jnp.stack([real, imag], 1) * scale


def apply_matrix(matrix, vector):
    high = lax.Precision.HIGHEST
    m_real, m_imag = (matrix[:, 0], matrix[:, 1])
    v_real, v_imag = (vector[:, 0], vector[:, 1])
    u_real = jnp.einsum("fjk,fk->fj", m_real, v_real, precision=high) - jnp.einsum(
        "fjk,fk->fj", m_imag, v_imag, precision=high
    )
    u_imag = jnp.einsum("fjk,fk->fj", m_real, v_imag, precision=high) + jnp.einsum(
        "fjk,fk->fj", m_imag, v_real, precision=high
    )
    return jnp.stack([u_real, u_imag], 1)


def rescale(product):
    return product / jnp.sqrt(jnp.mean(product * product, axis=(1, 2), keepdims=True) + 1e-06)


def rayleigh(vector, product):
    return jnp.mean(vector * product, axis=(1, 2)) / (
        jnp.mean(vector * vector, axis=(1, 2)) + 1e-06
    )


def shards_general(snapshots, tail):
    points = snapshots.shape[0]
    freq_count = lax.axis_size("freq")
    half = NFFT // 2
    table, wsum = build_table(FREQ_DEV * freq_count)
    scale = 1.0 / (points * lax.axis_size("space") * wsum)
    following = shifted(snapshots[:, :half], "freq", -1)
    is_last = lax.axis_index("freq") == freq_count - 1
    following = jnp.where(is_last, tail, following)
    extended = jnp.concatenate([snapshots, following], 1)
    coef = transform(extended, table)
    regrouped = lax.all_to_all(coef, "freq", split_axis=2, concat_axis=0, tiled=True)
    partial_value = gram_terms(regrouped, scale)
    blocks_all = partial_value.shape[2]
    held = blocks_all // lax.axis_size("space")
    vector = jnp.stack(
        [
            jnp.ones((FREQ_DEV, blocks_all), jnp.float32),
            jnp.zeros((FREQ_DEV, blocks_all), jnp.float32),
        ],
        1,
    )
    total = lax.psum(partial_value, "space")
    for step in range(POWER):
        vector = rescale(apply_matrix(total, vector))
    spectrum = rayleigh(vector, apply_matrix(total, vector))
    gram_rows = lax.dynamic_slice_in_dim(total, lax.axis_index("space") * held, held, 2)
    return (gram_rows, spectrum)


def two_pieces(values):
    high = values.astype(ml_dtypes.bfloat16)
    low = (values - high.astype(np.float64)).astype(ml_dtypes.bfloat16)
    return np.concatenate([high, low], 0)


def half_rows(nf):
    steps = np.arange(NFFT // 2)
    phase = 2.0 * np.pi * (np.arange(nf + 1)[:, None] * steps[None, :] % NFFT) / NFFT
    real, imag = np.cos(phase), -np.sin(phase)
    main = np.concatenate([real[:nf], imag[:nf]], 0)
    main[nf] = real[nf]
    return main, imag[nf : nf + 1]


def make_tables(nf, pieces):
    main, extra = half_rows(nf)
    half = NFFT // 2
    width = 2 * nf
    both = np.zeros((2 * width, NFFT))
    extras = np.zeros((2 * pieces, NFFT))
    for h in range(2):
        both[h * width : (h + 1) * width, h * half : (h + 1) * half] = main
        extras[h::2, h * half : (h + 1) * half] = extra
    last = np.zeros((width + 16, half))
    last[:width] = main
    last[width] = extra[0]
    return two_pieces(np.concatenate([both, extras], 0)), two_pieces(last)


def make_combine(nf, nb, pieces):
    width = 2 * nf
    main_rows = nb * width
    ext_rows = nb * pieces
    combine = np.zeros((2, nf, nb, main_rows + ext_rows + width + 16))

    def columns(m, f, part):
        if f == nf and part == 1:
            if m == nb:
                return [main_rows + ext_rows + width]
            first = main_rows + m // 2 * 2 * pieces + m % 2
            return [first + 2 * q for q in range(pieces)]
        start = main_rows + ext_rows if m == nb else m * width
        if f == nf:
            return [start + nf]
        if part == 1 and f == 0:
            return []
        return [start + part * nf + f]

    for f in range(nf):
        for b in range(nb):
            for m in (b, b + 1):
                second = m - b
                sign = (-1.0) ** f if second else 1.0
                side = 0.25 if second else -0.25
                for part in range(2):
                    for g, weight in ((f, 0.5), (f - 1, side), (f + 1, side)):
                        flip = -1.0 if g < 0 and part == 1 else 1.0
                        for column in columns(m, abs(g), part):
                            combine[part, f, b, column] += sign * flip * weight
    return combine.reshape(2 * nf * nb, -1).astype(ml_dtypes.bfloat16)


def xor_index(index, other, count):
    result = 0
    bit = 1
    while bit < count:
        digit = lax.rem(index // bit, 2)
        result = result + bit * ((1 - digit) if other & bit else digit)
        bit *= 2
    return result


def nt_dot(left, right):
    return lax.dot_general(
        left, right, (((1,), (1,)), ((), ())), preferred_element_type=jnp.float32
    )


def leading_value(g_re, g_im, nb):
    shape = g_re.shape
    row = lax.broadcasted_iota(jnp.int32, shape, 0)
    lane = lax.broadcasted_iota(jnp.int32, shape, 1)
    entries = 2.0 * nb

    def lane_sum(x):
        step = 1
        while step < nb:
            ahead = pltpu.roll(x, LANES - step, 1)
            behind = pltpu.roll(x, step, 1)
            x = x + jnp.where(lane % (2 * step) < step, ahead, behind)
            step *= 2
        return x

    def row_sum(x):
        return jnp.broadcast_to(jnp.sum(x, axis=0, keepdims=True), shape)

    def to_lanes(v_re, v_im):
        return row_sum(g_re * v_re + g_im * v_im), row_sum(g_re * v_im - g_im * v_re)

    def to_rows(v_re, v_im):
        return lane_sum(g_re * v_re - g_im * v_im), lane_sum(g_re * v_im + g_im * v_re)

    v_re, v_im = jnp.ones(shape, jnp.float32), jnp.zeros(shape, jnp.float32)
    for step in range(POWER):
        if step % 2 == 0:
            u_re, u_im = to_lanes(v_re, v_im)
            scale = lax.rsqrt(lane_sum(u_re * u_re + u_im * u_im) / entries + 1e-06)
            v_re, v_im = u_re, u_im
        else:
            u_re, u_im = to_rows(v_re, v_im)
            u_re, u_im = u_re * scale, u_im * scale
            scale = lax.rsqrt(row_sum(u_re * u_re + u_im * u_im) / entries + 1e-06)
            v_re, v_im = u_re * scale, u_im * scale
    u_re, u_im = to_lanes(v_re, v_im)
    here = lane % nb == row
    across_re = row_sum(jnp.where(here, v_re, 0.0))
    across_im = row_sum(jnp.where(here, v_im, 0.0))
    top = lane_sum(across_re * u_re + across_im * u_im) / entries
    return top / (row_sum(v_re * v_re + v_im * v_im) / entries + 1e-06)


def kernel(
    zs, ns, nf, nb, scale, spans, inner,
    snap_ref, tail_ref, const_ref, gram_ref, value_ref,
    x_buf, tail_buf, last_buf, const,
    send, send_ext, recv, recv_ext, z_part, z_recv, s_recv,
    x_sem, const_sem, send_sem, recv_sem, ext_send_sem, ext_recv_sem,
    z_send_sem, z_recv_sem, s_send_sem, s_recv_sem,
):
    my_s, my_z = lax.axis_index("space"), lax.axis_index("freq")
    quarter = snap_ref.shape[0] // zs
    sub = quarter // SUBS
    width = 2 * nf
    pieces = quarter // LANES
    here = sub // LANES
    order = list(range(zs // 2, zs)) + list(range(1, zs // 2))
    peers = {k: xor_index(my_z, k, zs) for k in order}
    peers[0] = my_z
    friends = {k: xor_index(my_s, k, ns) for k in range(1, ns)}

    barrier = pltpu.get_barrier_semaphore()
    for k in order:
        pl.semaphore_signal(barrier, inc=1, device_id=(my_s, peers[k]), device_id_type=MESH)
    for k in range(1, ns):
        pl.semaphore_signal(barrier, inc=1, device_id=(friends[k], my_z), device_id_type=MESH)

    loads = {}
    (t0, t1), (l0, l1), (c0, c1) = spans
    constants = [
        pltpu.make_async_copy(const_ref.at[a:b], const.at[a:b], const_sem.at[i])
        for i, (a, b) in enumerate(spans)
    ] + [
        pltpu.make_async_copy(
            tail_ref.at[pl.ds(pl.multiple_of(my_z * quarter, quarter), quarter)],
            tail_buf, const_sem.at[3],
        ),
    ]
    constants[0].start()
    for s in range(SUBS):
        for k in order + [0]:
            first = pl.multiple_of(peers[k] * quarter + s * sub, sub)
            loads[k, s] = pltpu.make_async_copy(
                snap_ref.at[pl.ds(first, sub)], x_buf.at[k, s], x_sem.at[k, s]
            )
    for k in order:
        loads[k, 0].start()

    ext_row = lax.broadcasted_iota(jnp.int32, (2 * pieces, LANES), 0) // 2

    def folded(x):
        rows = x.shape[0] // 2
        return x[:rows] + x[rows:]

    def transform(k, s):
        loads[k, s].wait()
        both = folded(nt_dot(const[t0:t1, : x_buf.shape[3]], x_buf[k, s]))
        for q in range(here):
            extras[k] = jnp.where(
                ext_row == s * here + q,
                both[2 * width :, q * LANES : (q + 1) * LANES],
                extras[k],
            )
        return both[: 2 * width].astype(jnp.bfloat16)

    def started(source, target, send_sems, recv_sems, k):
        copy = pltpu.make_async_remote_copy(
            source, target, send_sems, recv_sems,
            device_id=(my_s, peers[k]), device_id_type=MESH,
        )
        copy.start()
        return copy

    constants[0].wait()
    copies = {}
    extras = {k: jnp.zeros((2 * pieces, LANES), jnp.float32) for k in [0] + order}

    def send_main(k, s):
        copies[k, s] = started(
            send.at[k, s], recv.at[my_z, s], send_sem.at[k, s], recv_sem.at[k, s], k
        )

    for s in range(SUBS - 1):
        for k in order:
            send[k, s] = transform(k, s)
            if s == 0 and k == order[0]:
                pl.semaphore_wait(barrier, zs - 1 + ns - 1)
            send_main(k, s)
            if s == 0 and k == order[0]:
                for later in range(1, SUBS):
                    for i in order:
                        loads[i, later].start()
                for i in range(SUBS):
                    loads[0, i].start()
                for copy in constants[1:]:
                    copy.start()
    for k in order:
        send[k, SUBS - 1] = transform(k, SUBS - 1)
        send_ext[k] = extras[k].astype(jnp.bfloat16)
        copies[k, "ext"] = started(
            send_ext.at[k], recv_ext.at[my_z], ext_send_sem.at[k], ext_recv_sem.at[k], k
        )
    for k in order:
        send_main(k, SUBS - 1)
    for s in range(SUBS):
        recv[my_z, s] = transform(0, s)
    recv_ext[my_z] = extras[0].astype(jnp.bfloat16)
    for copy in constants[1:]:
        copy.wait()
    for s in range(SUBS):
        last = nt_dot(const[l0:l1, : tail_buf.shape[1]], tail_buf[s * sub : (s + 1) * sub])
        rows = last.shape[0] // 2
        last_buf[s] = (last[:rows] + last[rows:]).astype(jnp.bfloat16)

    gram = jnp.zeros((width * nb, width * nb), jnp.float32)
    for s in range(SUBS):
        for k in order:
            copies[k, s].wait_recv()
            if s == 0:
                copies[k, "ext"].wait_recv()
        spread = []
        for d in range(zs):
            extra = recv_ext[d]
            spread.append(
                jnp.concatenate(
                    [
                        jnp.where(ext_row == s * here + q, extra, jnp.zeros_like(extra))
                        for q in range(here)
                    ],
                    1,
                )
            )
        stacked = jnp.concatenate(
            [recv[d, s] for d in range(zs)]
            + spread + [last_buf[s]],
            0,
        )
        coef = jnp.dot(const[c0:c1, :inner], stacked, preferred_element_type=jnp.float32)
        coef = coef.astype(jnp.bfloat16)
        gram = gram + nt_dot(coef, coef)

    side = nf * nb
    real = gram[:side, :side] + gram[side:, side:]
    imag = gram[:side, side:] - gram[side:, :side]
    lane_freq = lax.broadcasted_iota(jnp.int32, (nb, side), 1) // nb
    g_re = jnp.zeros((nb, side), jnp.float32)
    g_im = jnp.zeros((nb, side), jnp.float32)
    for f in range(nf):
        g_re = jnp.where(lane_freq == f, real[f * nb : (f + 1) * nb], g_re)
        g_im = jnp.where(lane_freq == f, imag[f * nb : (f + 1) * nb], g_im)
    group = FREQ_DEV * nb
    lane = lax.broadcasted_iota(jnp.int32, (nb, side), 1)
    packed = []
    for z in range(zs):
        re = pltpu.roll(g_re, (LANES - z * group) % LANES, 1) if z else g_re
        im = pltpu.roll(g_im, (LANES + group - z * group) % LANES, 1) if z != 1 else g_im
        packed.append(jnp.where(lane < group, re, jnp.where(lane < 2 * group, im, 0.0)) * scale)
        z_part[z] = packed[z]

    z_copies = []
    for k in order:
        copy = pltpu.make_async_remote_copy(
            z_part.at[peers[k]], z_recv.at[k], z_send_sem.at[k], z_recv_sem.at[k],
            device_id=(my_s, peers[k]), device_id_type=MESH,
        )
        copy.start()
        z_copies.append(copy)
    total = z_part[my_z]
    for k, copy in zip(order, z_copies):
        copy.wait_recv()
        total = total + z_recv[k]
    s_recv[my_s] = total
    s_copies = []
    for k in range(1, ns):
        copy = pltpu.make_async_remote_copy(
            s_recv.at[my_s], s_recv.at[my_s], s_send_sem.at[k], s_recv_sem.at[k],
            device_id=(friends[k], my_z), device_id_type=MESH,
        )
        copy.start()
        s_copies.append(copy)
    for copy in s_copies:
        copy.wait_recv()
    total = s_recv[0]
    for d in range(1, ns):
        total = total + s_recv[d]
    g_re = jnp.where(lane < group, total, 0.0)
    g_im = jnp.where(lane < group, pltpu.roll(total, LANES - group, 1), 0.0)

    value = leading_value(g_re, g_im, nb)
    row = lax.broadcasted_iota(jnp.int32, (nb, side), 0)
    mine = row == my_s
    row_re = jnp.sum(jnp.where(mine, g_re, 0.0), axis=0, keepdims=True)
    row_im = jnp.sum(jnp.where(mine, g_im, 0.0), axis=0, keepdims=True)
    result = jnp.where(row % 2 == 0, row_re, row_im)
    rows, values = result, value
    for f in range(1, FREQ_DEV):
        rows = jnp.where(row // 2 == f, pltpu.roll(result, LANES - f * nb, 1), rows)
        values = jnp.where(lane == f, pltpu.roll(value, LANES - f * (nb - 1), 1), values)
    gram_ref[...] = rows
    value_ref[...] = values

    for copy in copies.values():
        copy.wait_send()
    for copy in z_copies + s_copies:
        copy.wait_send()


def shards_kernel(zs, ns, snapshots, tail):
    points, steps = snapshots.shape
    nf = FREQ_DEV * zs
    nb = 2 * zs
    sub = points // zs // SUBS
    pieces = points // zs // LANES
    width = 2 * nf
    table, tail_table = make_tables(nf, pieces)
    combine = make_combine(nf, nb, pieces)
    window = 0.5 - 0.5 * np.cos(2.0 * np.pi * np.arange(NFFT) / NFFT)
    scale = float(1.0 / (points * ns * np.sum(window * window)))
    parts = [table, tail_table, combine]
    inner = combine.shape[1]
    padded = -(-inner // LANES) * LANES
    const = np.concatenate([np.pad(p, ((0, 0), (0, padded - p.shape[1]))) for p in parts], 0)
    ends = np.cumsum([p.shape[0] for p in parts]).tolist()
    spans = list(zip([0] + ends[:-1], ends))
    dma = pltpu.SemaphoreType.DMA
    flops = 2 * points * steps * table.shape[0]
    gram, values = pl.pallas_call(
        functools.partial(kernel, zs, ns, nf, nb, scale, spans, inner),
        out_shape=[jax.ShapeDtypeStruct((nb, LANES), jnp.float32)] * 2,
        in_specs=[pl.BlockSpec(memory_space=pltpu.HBM)] * 3,
        out_specs=[pl.BlockSpec(memory_space=pltpu.VMEM)] * 2,
        scratch_shapes=[
            pltpu.VMEM((zs, SUBS, sub, steps), jnp.bfloat16),
            pltpu.VMEM((points // zs, tail.shape[1]), jnp.bfloat16),
            pltpu.VMEM((SUBS, tail_table.shape[0] // 2, sub), jnp.bfloat16),
            pltpu.VMEM(const.shape, jnp.bfloat16),
            pltpu.VMEM((zs, SUBS, 2 * width, sub), jnp.bfloat16),
            pltpu.VMEM((zs, 2 * pieces, LANES), jnp.bfloat16),
            pltpu.VMEM((zs, SUBS, 2 * width, sub), jnp.bfloat16),
            pltpu.VMEM((zs, 2 * pieces, LANES), jnp.bfloat16),
            pltpu.VMEM((zs, nb, LANES), jnp.float32),
            pltpu.VMEM((zs, nb, LANES), jnp.float32),
            pltpu.VMEM((ns, nb, LANES), jnp.float32),
            dma((zs, SUBS)), dma((4,)),
            dma((zs, SUBS)), dma((zs, SUBS)), dma((zs,)), dma((zs,)),
            dma((zs,)), dma((zs,)), dma((ns,)), dma((ns,)),
        ],
        compiler_params=pltpu.CompilerParams(
            collective_id=0, has_side_effects=True, vmem_limit_bytes=55040 * 1024
        ),
        cost_estimate=pl.CostEstimate(
            flops=flops, bytes_accessed=points * steps * 2, transcendentals=0
        ),
    )(snapshots, tail, jnp.asarray(const))
    return gram[:, :nb].reshape(FREQ_DEV, 2, 1, nb), values[0, :FREQ_DEV]


def power_of_two(count):
    return count > 1 and count & (count - 1) == 0


def shards(snapshots, tail):
    zs, ns = lax.axis_size("freq"), lax.axis_size("space")
    points, steps = snapshots.shape
    nb = zs * steps // (NFFT // 2)
    packs = FREQ_DEV * zs * nb == LANES and steps == NFFT and nb == ns == 8
    whole = points % (zs * SUBS * LANES) == 0
    if packs and whole and power_of_two(zs) and power_of_two(ns):
        return shards_kernel(zs, ns, snapshots, tail)
    return shards_general(snapshots, tail)


def solution(mesh):
    in_specs = (P("space", "freq"), P("space", None))
    out_specs = (P("freq", None, "space", None), P("freq"))
    return jax.shard_map(shards, mesh=mesh, in_specs=in_specs, out_specs=out_specs, check_vma=False)
```

```python
import functools
import math

import jax
import jax.numpy as jnp
import ml_dtypes
import numpy as np
from jax import lax
from jax.experimental import pallas as pl
from jax.experimental.pallas import tpu as pltpu
from jax.sharding import PartitionSpec as P

FREQ_DEV = 4
NFFT = 256
POWER = 4
LANES = 128
SUBS = 4
MESH = pl.DeviceIdType.MESH


def shifted(value, axis, steps):
    count = lax.axis_size(axis)
    initial, last = (max(0, -steps), min(count, count - steps))
    return lax.ppermute(value, axis, [(source, source + steps) for source in range(initial, last)])


def build_table(count):
    steps = jnp.arange(NFFT, dtype=jnp.int32)
    freqs = jnp.arange(count, dtype=jnp.int32)
    window = 0.5 - 0.5 * jnp.cos(2.0 * math.pi * steps.astype(jnp.float32) / NFFT)
    phase = 2.0 * math.pi * (steps[:, None] * freqs[None, :] % NFFT).astype(jnp.float32) / NFFT
    table = jnp.concatenate(
        [window[:, None] * jnp.cos(phase), -window[:, None] * jnp.sin(phase)], 1
    )
    return (table.astype(jnp.bfloat16), jnp.sum(window * window))


def transform(extended, table):
    points, width = extended.shape
    half = NFFT // 2
    count = width // half - 1
    halves = extended.reshape(points, count + 1, half)
    blocks = jnp.concatenate([halves[:, :-1], halves[:, 1:]], 2)
    coef = jnp.einsum("pbt,tk->bkp", blocks, table, preferred_element_type=jnp.float32)
    return coef.reshape(count, 2, table.shape[1] // 2, points).astype(jnp.bfloat16)


def gram_terms(coef, scale):
    big = jnp.einsum("bcfp,gdfp->fcbdg", coef, coef, preferred_element_type=jnp.float32)
    real = big[:, 0, :, 0, :] + big[:, 1, :, 1, :]
    imag = big[:, 0, :, 1, :] - big[:, 1, :, 0, :]
    return jnp.stack([real, imag], 1) * scale


def apply_matrix(matrix, vector):
    high = lax.Precision.HIGHEST
    m_real, m_imag = (matrix[:, 0], matrix[:, 1])
    v_real, v_imag = (vector[:, 0], vector[:, 1])
    u_real = jnp.einsum("fjk,fk->fj", m_real, v_real, precision=high) - jnp.einsum(
        "fjk,fk->fj", m_imag, v_imag, precision=high
    )
    u_imag = jnp.einsum("fjk,fk->fj", m_real, v_imag, precision=high) + jnp.einsum(
        "fjk,fk->fj", m_imag, v_real, precision=high
    )
    return jnp.stack([u_real, u_imag], 1)


def rescale(product):
    return product / jnp.sqrt(jnp.mean(product * product, axis=(1, 2), keepdims=True) + 1e-06)


def rayleigh(vector, product):
    return jnp.mean(vector * product, axis=(1, 2)) / (
        jnp.mean(vector * vector, axis=(1, 2)) + 1e-06
    )


def shards_general(snapshots, tail):
    points = snapshots.shape[0]
    freq_count = lax.axis_size("freq")
    half = NFFT // 2
    table, wsum = build_table(FREQ_DEV * freq_count)
    scale = 1.0 / (points * lax.axis_size("space") * wsum)
    following = shifted(snapshots[:, :half], "freq", -1)
    is_last = lax.axis_index("freq") == freq_count - 1
    following = jnp.where(is_last, tail, following)
    extended = jnp.concatenate([snapshots, following], 1)
    coef = transform(extended, table)
    regrouped = lax.all_to_all(coef, "freq", split_axis=2, concat_axis=0, tiled=True)
    partial_value = gram_terms(regrouped, scale)
    blocks_all = partial_value.shape[2]
    held = blocks_all // lax.axis_size("space")
    vector = jnp.stack(
        [
            jnp.ones((FREQ_DEV, blocks_all), jnp.float32),
            jnp.zeros((FREQ_DEV, blocks_all), jnp.float32),
        ],
        1,
    )
    total = lax.psum(partial_value, "space")
    for step in range(POWER):
        vector = rescale(apply_matrix(total, vector))
    spectrum = rayleigh(vector, apply_matrix(total, vector))
    gram_rows = lax.dynamic_slice_in_dim(total, lax.axis_index("space") * held, held, 2)
    return (gram_rows, spectrum)


def two_pieces(values):
    high = values.astype(ml_dtypes.bfloat16)
    low = (values - high.astype(np.float64)).astype(ml_dtypes.bfloat16)
    return np.concatenate([high, low], 0)


def half_rows(nf):
    steps = np.arange(NFFT // 2)
    phase = 2.0 * np.pi * (np.arange(nf + 1)[:, None] * steps[None, :] % NFFT) / NFFT
    real, imag = np.cos(phase), -np.sin(phase)
    main = np.concatenate([real[:nf], imag[:nf]], 0)
    main[nf] = real[nf]
    return main, imag[nf : nf + 1]


def make_tables(nf, pieces):
    main, extra = half_rows(nf)
    half = NFFT // 2
    width = 2 * nf
    both = np.zeros((2 * width, NFFT))
    extras = np.zeros((2 * pieces, NFFT))
    for h in range(2):
        both[h * width : (h + 1) * width, h * half : (h + 1) * half] = main
        extras[h::2, h * half : (h + 1) * half] = extra
    last = np.zeros((width + 16, half))
    last[:width] = main
    last[width] = extra[0]
    return two_pieces(both), two_pieces(extras), two_pieces(last)


def make_combine(nf, nb, pieces):
    width = 2 * nf
    main_rows = nb * width
    ext_rows = nb * pieces
    combine = np.zeros((2, nf, nb, main_rows + ext_rows + width + 16))

    def columns(m, f, part):
        if f == nf and part == 1:
            if m == nb:
                return [main_rows + ext_rows + width]
            first = main_rows + m // 2 * 2 * pieces + m % 2
            return [first + 2 * q for q in range(pieces)]
        start = main_rows + ext_rows if m == nb else m * width
        if f == nf:
            return [start + nf]
        if part == 1 and f == 0:
            return []
        return [start + part * nf + f]

    for f in range(nf):
        for b in range(nb):
            for m in (b, b + 1):
                second = m - b
                sign = (-1.0) ** f if second else 1.0
                side = 0.25 if second else -0.25
                for part in range(2):
                    for g, weight in ((f, 0.5), (f - 1, side), (f + 1, side)):
                        flip = -1.0 if g < 0 and part == 1 else 1.0
                        for column in columns(m, abs(g), part):
                            combine[part, f, b, column] += sign * flip * weight
    return combine.reshape(2 * nf * nb, -1).astype(ml_dtypes.bfloat16)


def xor_index(index, other, count):
    result = 0
    bit = 1
    while bit < count:
        digit = lax.rem(index // bit, 2)
        result = result + bit * ((1 - digit) if other & bit else digit)
        bit *= 2
    return result


def nt_dot(left, right):
    return lax.dot_general(
        left, right, (((1,), (1,)), ((), ())), preferred_element_type=jnp.float32
    )


def leading_value(g_re, g_im, nb):
    shape = g_re.shape
    row = lax.broadcasted_iota(jnp.int32, shape, 0)
    lane = lax.broadcasted_iota(jnp.int32, shape, 1)
    entries = 2.0 * nb

    def lane_sum(x):
        step = 1
        while step < nb:
            ahead = pltpu.roll(x, LANES - step, 1)
            behind = pltpu.roll(x, step, 1)
            x = x + jnp.where(lane % (2 * step) < step, ahead, behind)
            step *= 2
        return x

    def row_sum(x):
        return jnp.broadcast_to(jnp.sum(x, axis=0, keepdims=True), shape)

    def to_lanes(v_re, v_im):
        return row_sum(g_re * v_re + g_im * v_im), row_sum(g_re * v_im - g_im * v_re)

    def to_rows(v_re, v_im):
        return lane_sum(g_re * v_re - g_im * v_im), lane_sum(g_re * v_im + g_im * v_re)

    v_re, v_im = jnp.ones(shape, jnp.float32), jnp.zeros(shape, jnp.float32)
    for step in range(POWER):
        if step % 2 == 0:
            u_re, u_im = to_lanes(v_re, v_im)
            scale = lax.rsqrt(lane_sum(u_re * u_re + u_im * u_im) / entries + 1e-06)
            v_re, v_im = u_re, u_im
        else:
            u_re, u_im = to_rows(v_re, v_im)
            u_re, u_im = u_re * scale, u_im * scale
            scale = lax.rsqrt(row_sum(u_re * u_re + u_im * u_im) / entries + 1e-06)
            v_re, v_im = u_re * scale, u_im * scale
    u_re, u_im = to_lanes(v_re, v_im)
    here = lane % nb == row
    across_re = row_sum(jnp.where(here, v_re, 0.0))
    across_im = row_sum(jnp.where(here, v_im, 0.0))
    top = lane_sum(across_re * u_re + across_im * u_im) / entries
    return top / (row_sum(v_re * v_re + v_im * v_im) / entries + 1e-06)


def kernel(
    zs, ns, nf, nb, scale, spans, inner,
    snap_ref, tail_ref, const_ref, gram_ref, value_ref,
    x_buf, tail_buf, last_buf, const,
    send, send_ext, recv, recv_ext, z_part, z_recv, s_recv,
    x_sem, const_sem, send_sem, recv_sem, ext_send_sem, ext_recv_sem,
    z_send_sem, z_recv_sem, s_send_sem, s_recv_sem,
):
    my_s, my_z = lax.axis_index("space"), lax.axis_index("freq")
    quarter = snap_ref.shape[0] // zs
    sub = quarter // SUBS
    width = 2 * nf
    pieces = quarter // LANES
    here = sub // LANES
    order = list(range(zs // 2, zs)) + list(range(1, zs // 2))
    peers = {k: xor_index(my_z, k, zs) for k in order}
    peers[0] = my_z
    friends = {k: xor_index(my_s, k, ns) for k in range(1, ns)}

    barrier = pltpu.get_barrier_semaphore()
    for k in order:
        pl.semaphore_signal(barrier, inc=1, device_id=(my_s, peers[k]), device_id_type=MESH)
    for k in range(1, ns):
        pl.semaphore_signal(barrier, inc=1, device_id=(friends[k], my_z), device_id_type=MESH)

    loads = {}
    (t0, _), (e0, e1), (l0, l1), (c0, c1) = spans
    constants = [
        pltpu.make_async_copy(const_ref.at[a:b], const.at[a:b], const_sem.at[i])
        for i, (a, b) in enumerate([(t0, e1), (l0, l1), (c0, c1)])
    ] + [
        pltpu.make_async_copy(
            tail_ref.at[pl.ds(pl.multiple_of(my_z * quarter, quarter), quarter)],
            tail_buf, const_sem.at[3],
        ),
    ]
    constants[0].start()
    for s in range(SUBS):
        for k in order + [0]:
            first = pl.multiple_of(peers[k] * quarter + s * sub, sub)
            loads[k, s] = pltpu.make_async_copy(
                snap_ref.at[pl.ds(first, sub)], x_buf.at[k, s], x_sem.at[k, s]
            )
    for k in order:
        loads[k, 0].start()

    ext_row = lax.broadcasted_iota(jnp.int32, (2 * pieces, LANES), 0) // 2

    def folded(x):
        rows = x.shape[0] // 2
        return x[:rows] + x[rows:]

    def transform(k, s):
        return folded(nt_dot(const[t0:e0, : x_buf.shape[3]], x_buf[k, s])).astype(jnp.bfloat16)

    def extras_of(k):
        whole = x_buf[k].reshape(quarter, x_buf.shape[3])
        rows = folded(nt_dot(const[e0:e1, : x_buf.shape[3]], whole))
        extra = jnp.zeros((2 * pieces, LANES), jnp.float32)
        for q in range(pieces):
            extra = jnp.where(ext_row == q, rows[:, q * LANES : (q + 1) * LANES], extra)
        return extra.astype(jnp.bfloat16)

    def started(source, target, send_sems, recv_sems, k):
        copy = pltpu.make_async_remote_copy(
            source, target, send_sems, recv_sems,
            device_id=(my_s, peers[k]), device_id_type=MESH,
        )
        copy.start()
        return copy

    constants[0].wait()
    copies = {}
    for s in range(SUBS):
        for k in order:
            if s < 2:
                loads[k, s].wait()
            send[k, s] = transform(k, s)
            if s == 0 and k == order[0]:
                pl.semaphore_wait(barrier, zs - 1 + ns - 1)
            copies[k, s] = started(
                send.at[k, s], recv.at[my_z, s], send_sem.at[k, s], recv_sem.at[k, s], k
            )
            if s == 0 and k == order[0]:
                for later in range(1, SUBS):
                    for i in order:
                        loads[i, later].start()
                for i in range(SUBS):
                    loads[0, i].start()
                for copy in constants[1:]:
                    copy.start()
        if s == 1:
            for k in order:
                for later in range(2, SUBS):
                    loads[k, later].wait()
                send_ext[k] = extras_of(k)
                copies[k, "ext"] = started(
                    send_ext.at[k], recv_ext.at[my_z], ext_send_sem.at[k], ext_recv_sem.at[k], k
                )
    for s in range(SUBS):
        loads[0, s].wait()
        recv[my_z, s] = transform(0, s)
    recv_ext[my_z] = extras_of(0)
    for copy in constants[1:]:
        copy.wait()
    for s in range(SUBS):
        last = nt_dot(const[l0:l1, : tail_buf.shape[1]], tail_buf[s * sub : (s + 1) * sub])
        rows = last.shape[0] // 2
        last_buf[s] = (last[:rows] + last[rows:]).astype(jnp.bfloat16)

    main_rows = nb * width
    gram = jnp.zeros((width * nb, width * nb), jnp.float32)
    for s in range(SUBS):
        if s == 0:
            for k in order:
                copies[k, "ext"].wait_recv()
        extras = []
        for d in range(zs):
            extra = recv_ext[d]
            extras.append(
                jnp.concatenate(
                    [
                        jnp.where(ext_row == s * here + q, extra, jnp.zeros_like(extra))
                        for q in range(here)
                    ],
                    1,
                )
            )
        rest = jnp.dot(
            const[c0:c1, main_rows:inner],
            jnp.concatenate(extras + [last_buf[s]], 0),
            preferred_element_type=jnp.float32,
        )
        for k in order:
            copies[k, s].wait_recv()
        stacked = jnp.concatenate([recv[d, s] for d in range(zs)], 0)
        coef = rest + jnp.dot(
            const[c0:c1, :main_rows], stacked, preferred_element_type=jnp.float32
        )
        coef = coef.astype(jnp.bfloat16)
        gram = gram + nt_dot(coef, coef)

    side = nf * nb
    real = gram[:side, :side] + gram[side:, side:]
    imag = gram[:side, side:] - gram[side:, :side]
    lane_freq = lax.broadcasted_iota(jnp.int32, (nb, side), 1) // nb
    g_re = jnp.zeros((nb, side), jnp.float32)
    g_im = jnp.zeros((nb, side), jnp.float32)
    for f in range(nf):
        g_re = jnp.where(lane_freq == f, real[f * nb : (f + 1) * nb], g_re)
        g_im = jnp.where(lane_freq == f, imag[f * nb : (f + 1) * nb], g_im)
    group = FREQ_DEV * nb
    lane = lax.broadcasted_iota(jnp.int32, (nb, side), 1)
    packed = []
    for z in range(zs):
        re = pltpu.roll(g_re, (LANES - z * group) % LANES, 1) if z else g_re
        im = pltpu.roll(g_im, (LANES + group - z * group) % LANES, 1) if z != 1 else g_im
        packed.append(jnp.where(lane < group, re, jnp.where(lane < 2 * group, im, 0.0)) * scale)
        z_part[z] = packed[z]

    z_copies = []
    for k in order:
        copy = pltpu.make_async_remote_copy(
            z_part.at[peers[k]], z_recv.at[k], z_send_sem.at[k], z_recv_sem.at[k],
            device_id=(my_s, peers[k]), device_id_type=MESH,
        )
        copy.start()
        z_copies.append(copy)
    total = z_part[my_z]
    for k, copy in zip(order, z_copies):
        copy.wait_recv()
        total = total + z_recv[k]
    s_recv[my_s] = total
    s_copies = []
    for k in range(1, ns):
        copy = pltpu.make_async_remote_copy(
            s_recv.at[my_s], s_recv.at[my_s], s_send_sem.at[k], s_recv_sem.at[k],
            device_id=(friends[k], my_z), device_id_type=MESH,
        )
        copy.start()
        s_copies.append(copy)
    for copy in s_copies:
        copy.wait_recv()
    total = s_recv[0]
    for d in range(1, ns):
        total = total + s_recv[d]
    g_re = jnp.where(lane < group, total, 0.0)
    g_im = jnp.where(lane < group, pltpu.roll(total, LANES - group, 1), 0.0)

    value = leading_value(g_re, g_im, nb)
    row = lax.broadcasted_iota(jnp.int32, (nb, side), 0)
    mine = row == my_s
    row_re = jnp.sum(jnp.where(mine, g_re, 0.0), axis=0, keepdims=True)
    row_im = jnp.sum(jnp.where(mine, g_im, 0.0), axis=0, keepdims=True)
    result = jnp.where(row % 2 == 0, row_re, row_im)
    rows, values = result, value
    for f in range(1, FREQ_DEV):
        rows = jnp.where(row // 2 == f, pltpu.roll(result, LANES - f * nb, 1), rows)
        values = jnp.where(lane == f, pltpu.roll(value, LANES - f * (nb - 1), 1), values)
    gram_ref[...] = rows
    value_ref[...] = values

    for copy in copies.values():
        copy.wait_send()
    for copy in z_copies + s_copies:
        copy.wait_send()


def shards_kernel(zs, ns, snapshots, tail):
    points, steps = snapshots.shape
    nf = FREQ_DEV * zs
    nb = 2 * zs
    sub = points // zs // SUBS
    pieces = points // zs // LANES
    width = 2 * nf
    table, ext_table, tail_table = make_tables(nf, pieces)
    combine = make_combine(nf, nb, pieces)
    window = 0.5 - 0.5 * np.cos(2.0 * np.pi * np.arange(NFFT) / NFFT)
    scale = float(1.0 / (points * ns * np.sum(window * window)))
    parts = [table, ext_table, tail_table, combine]
    inner = combine.shape[1]
    padded = -(-inner // LANES) * LANES
    const = np.concatenate([np.pad(p, ((0, 0), (0, padded - p.shape[1]))) for p in parts], 0)
    ends = np.cumsum([p.shape[0] for p in parts]).tolist()
    spans = list(zip([0] + ends[:-1], ends))
    dma = pltpu.SemaphoreType.DMA
    flops = 2 * points * steps * table.shape[0]
    gram, values = pl.pallas_call(
        functools.partial(kernel, zs, ns, nf, nb, scale, spans, inner),
        out_shape=[jax.ShapeDtypeStruct((nb, LANES), jnp.float32)] * 2,
        in_specs=[pl.BlockSpec(memory_space=pltpu.HBM)] * 3,
        out_specs=[pl.BlockSpec(memory_space=pltpu.VMEM)] * 2,
        scratch_shapes=[
            pltpu.VMEM((zs, SUBS, sub, steps), jnp.bfloat16),
            pltpu.VMEM((points // zs, tail.shape[1]), jnp.bfloat16),
            pltpu.VMEM((SUBS, tail_table.shape[0] // 2, sub), jnp.bfloat16),
            pltpu.VMEM(const.shape, jnp.bfloat16),
            pltpu.VMEM((zs, SUBS, 2 * width, sub), jnp.bfloat16),
            pltpu.VMEM((zs, 2 * pieces, LANES), jnp.bfloat16),
            pltpu.VMEM((zs, SUBS, 2 * width, sub), jnp.bfloat16),
            pltpu.VMEM((zs, 2 * pieces, LANES), jnp.bfloat16),
            pltpu.VMEM((zs, nb, LANES), jnp.float32),
            pltpu.VMEM((zs, nb, LANES), jnp.float32),
            pltpu.VMEM((ns, nb, LANES), jnp.float32),
            dma((zs, SUBS)), dma((4,)),
            dma((zs, SUBS)), dma((zs, SUBS)), dma((zs,)), dma((zs,)),
            dma((zs,)), dma((zs,)), dma((ns,)), dma((ns,)),
        ],
        compiler_params=pltpu.CompilerParams(
            collective_id=0, has_side_effects=True, vmem_limit_bytes=55040 * 1024
        ),
        cost_estimate=pl.CostEstimate(
            flops=flops, bytes_accessed=points * steps * 2, transcendentals=0
        ),
    )(snapshots, tail, jnp.asarray(const))
    return gram[:, :nb].reshape(FREQ_DEV, 2, 1, nb), values[0, :FREQ_DEV]


def power_of_two(count):
    return count > 1 and count & (count - 1) == 0


def shards(snapshots, tail):
    zs, ns = lax.axis_size("freq"), lax.axis_size("space")
    points, steps = snapshots.shape
    nb = zs * steps // (NFFT // 2)
    packs = FREQ_DEV * zs * nb == LANES and steps == NFFT and nb == ns == 8
    whole = points % (zs * SUBS * LANES) == 0
    if packs and whole and power_of_two(zs) and power_of_two(ns):
        return shards_kernel(zs, ns, snapshots, tail)
    return shards_general(snapshots, tail)


def solution(mesh):
    in_specs = (P("space", "freq"), P("space", None))
    out_specs = (P("freq", None, "space", None), P("freq"))
    return jax.shard_map(shards, mesh=mesh, in_specs=in_specs, out_specs=out_specs, check_vma=False)
```

```python
import functools
import math

import jax
import jax.numpy as jnp
import ml_dtypes
import numpy as np
from jax import lax
from jax.experimental import pallas as pl
from jax.experimental.pallas import tpu as pltpu
from jax.sharding import PartitionSpec as P

FREQ_DEV = 4
NFFT = 256
POWER = 4
LANES = 128
SUBS = 4
MESH = pl.DeviceIdType.MESH


def shifted(value, axis, steps):
    count = lax.axis_size(axis)
    initial, last = (max(0, -steps), min(count, count - steps))
    return lax.ppermute(value, axis, [(source, source + steps) for source in range(initial, last)])


def build_table(count):
    steps = jnp.arange(NFFT, dtype=jnp.int32)
    freqs = jnp.arange(count, dtype=jnp.int32)
    window = 0.5 - 0.5 * jnp.cos(2.0 * math.pi * steps.astype(jnp.float32) / NFFT)
    phase = 2.0 * math.pi * (steps[:, None] * freqs[None, :] % NFFT).astype(jnp.float32) / NFFT
    table = jnp.concatenate(
        [window[:, None] * jnp.cos(phase), -window[:, None] * jnp.sin(phase)], 1
    )
    return (table.astype(jnp.bfloat16), jnp.sum(window * window))


def transform(extended, table):
    points, width = extended.shape
    half = NFFT // 2
    count = width // half - 1
    halves = extended.reshape(points, count + 1, half)
    blocks = jnp.concatenate([halves[:, :-1], halves[:, 1:]], 2)
    coef = jnp.einsum("pbt,tk->bkp", blocks, table, preferred_element_type=jnp.float32)
    return coef.reshape(count, 2, table.shape[1] // 2, points).astype(jnp.bfloat16)


def gram_terms(coef, scale):
    big = jnp.einsum("bcfp,gdfp->fcbdg", coef, coef, preferred_element_type=jnp.float32)
    real = big[:, 0, :, 0, :] + big[:, 1, :, 1, :]
    imag = big[:, 0, :, 1, :] - big[:, 1, :, 0, :]
    return jnp.stack([real, imag], 1) * scale


def apply_matrix(matrix, vector):
    high = lax.Precision.HIGHEST
    m_real, m_imag = (matrix[:, 0], matrix[:, 1])
    v_real, v_imag = (vector[:, 0], vector[:, 1])
    u_real = jnp.einsum("fjk,fk->fj", m_real, v_real, precision=high) - jnp.einsum(
        "fjk,fk->fj", m_imag, v_imag, precision=high
    )
    u_imag = jnp.einsum("fjk,fk->fj", m_real, v_imag, precision=high) + jnp.einsum(
        "fjk,fk->fj", m_imag, v_real, precision=high
    )
    return jnp.stack([u_real, u_imag], 1)


def rescale(product):
    return product / jnp.sqrt(jnp.mean(product * product, axis=(1, 2), keepdims=True) + 1e-06)


def rayleigh(vector, product):
    return jnp.mean(vector * product, axis=(1, 2)) / (
        jnp.mean(vector * vector, axis=(1, 2)) + 1e-06
    )


def shards_general(snapshots, tail):
    points = snapshots.shape[0]
    freq_count = lax.axis_size("freq")
    half = NFFT // 2
    table, wsum = build_table(FREQ_DEV * freq_count)
    scale = 1.0 / (points * lax.axis_size("space") * wsum)
    following = shifted(snapshots[:, :half], "freq", -1)
    is_last = lax.axis_index("freq") == freq_count - 1
    following = jnp.where(is_last, tail, following)
    extended = jnp.concatenate([snapshots, following], 1)
    coef = transform(extended, table)
    regrouped = lax.all_to_all(coef, "freq", split_axis=2, concat_axis=0, tiled=True)
    partial_value = gram_terms(regrouped, scale)
    blocks_all = partial_value.shape[2]
    held = blocks_all // lax.axis_size("space")
    vector = jnp.stack(
        [
            jnp.ones((FREQ_DEV, blocks_all), jnp.float32),
            jnp.zeros((FREQ_DEV, blocks_all), jnp.float32),
        ],
        1,
    )
    total = lax.psum(partial_value, "space")
    for step in range(POWER):
        vector = rescale(apply_matrix(total, vector))
    spectrum = rayleigh(vector, apply_matrix(total, vector))
    gram_rows = lax.dynamic_slice_in_dim(total, lax.axis_index("space") * held, held, 2)
    return (gram_rows, spectrum)


def two_pieces(values):
    high = values.astype(ml_dtypes.bfloat16)
    low = (values - high.astype(np.float64)).astype(ml_dtypes.bfloat16)
    return np.concatenate([high, low], 0)


def half_rows(nf):
    steps = np.arange(NFFT // 2)
    phase = 2.0 * np.pi * (np.arange(nf + 1)[:, None] * steps[None, :] % NFFT) / NFFT
    real, imag = np.cos(phase), -np.sin(phase)
    main = np.concatenate([real[:nf], imag[:nf]], 0)
    main[nf] = real[nf]
    return main, imag[nf : nf + 1]


def make_tables(nf, pieces):
    main, extra = half_rows(nf)
    half = NFFT // 2
    width = 2 * nf
    both = np.zeros((2 * width, NFFT))
    extras = np.zeros((2 * pieces, NFFT))
    for h in range(2):
        both[h * width : (h + 1) * width, h * half : (h + 1) * half] = main
        extras[h::2, h * half : (h + 1) * half] = extra
    last = np.zeros((width + 16, half))
    last[:width] = main
    last[width] = extra[0]
    return two_pieces(both), two_pieces(extras), two_pieces(last)


def make_combine(nf, nb, pieces):
    width = 2 * nf
    main_rows = nb * width
    ext_rows = nb * pieces
    combine = np.zeros((2, nf, nb, main_rows + ext_rows + width + 16))

    def columns(m, f, part):
        if f == nf and part == 1:
            if m == nb:
                return [main_rows + ext_rows + width]
            first = main_rows + m // 2 * 2 * pieces + m % 2
            return [first + 2 * q for q in range(pieces)]
        start = main_rows + ext_rows if m == nb else m * width
        if f == nf:
            return [start + nf]
        if part == 1 and f == 0:
            return []
        return [start + part * nf + f]

    for f in range(nf):
        for b in range(nb):
            for m in (b, b + 1):
                second = m - b
                sign = (-1.0) ** f if second else 1.0
                side = 0.25 if second else -0.25
                for part in range(2):
                    for g, weight in ((f, 0.5), (f - 1, side), (f + 1, side)):
                        flip = -1.0 if g < 0 and part == 1 else 1.0
                        for column in columns(m, abs(g), part):
                            combine[part, f, b, column] += sign * flip * weight
    return combine.reshape(2 * nf * nb, -1).astype(ml_dtypes.bfloat16)


def xor_index(index, other, count):
    result = 0
    bit = 1
    while bit < count:
        digit = lax.rem(index // bit, 2)
        result = result + bit * ((1 - digit) if other & bit else digit)
        bit *= 2
    return result


def nt_dot(left, right):
    return lax.dot_general(
        left, right, (((1,), (1,)), ((), ())), preferred_element_type=jnp.float32
    )


def leading_value(g_re, g_im, nb):
    shape = g_re.shape
    row = lax.broadcasted_iota(jnp.int32, shape, 0)
    lane = lax.broadcasted_iota(jnp.int32, shape, 1)
    entries = 2.0 * nb

    def lane_sum(x):
        step = 1
        while step < nb:
            ahead = pltpu.roll(x, LANES - step, 1)
            behind = pltpu.roll(x, step, 1)
            x = x + jnp.where(lane % (2 * step) < step, ahead, behind)
            step *= 2
        return x

    def row_sum(x):
        return jnp.broadcast_to(jnp.sum(x, axis=0, keepdims=True), shape)

    def to_lanes(v_re, v_im):
        return row_sum(g_re * v_re + g_im * v_im), row_sum(g_re * v_im - g_im * v_re)

    def to_rows(v_re, v_im):
        return lane_sum(g_re * v_re - g_im * v_im), lane_sum(g_re * v_im + g_im * v_re)

    v_re, v_im = jnp.ones(shape, jnp.float32), jnp.zeros(shape, jnp.float32)
    for step in range(POWER):
        if step % 2 == 0:
            u_re, u_im = to_lanes(v_re, v_im)
            scale = lax.rsqrt(lane_sum(u_re * u_re + u_im * u_im) / entries + 1e-06)
            v_re, v_im = u_re, u_im
        else:
            u_re, u_im = to_rows(v_re, v_im)
            u_re, u_im = u_re * scale, u_im * scale
            scale = lax.rsqrt(row_sum(u_re * u_re + u_im * u_im) / entries + 1e-06)
            v_re, v_im = u_re * scale, u_im * scale
    u_re, u_im = to_lanes(v_re, v_im)
    here = lane % nb == row
    across_re = row_sum(jnp.where(here, v_re, 0.0))
    across_im = row_sum(jnp.where(here, v_im, 0.0))
    top = lane_sum(across_re * u_re + across_im * u_im) / entries
    return top / (row_sum(v_re * v_re + v_im * v_im) / entries + 1e-06)


def kernel(
    zs, ns, nf, nb, scale, spans, inner,
    snap_ref, tail_ref, const_ref, gram_ref, value_ref,
    x_buf, tail_buf, last_buf, const,
    send, send_ext, recv, recv_ext, z_part, z_recv, s_recv,
    x_sem, const_sem, send_sem, recv_sem, ext_send_sem, ext_recv_sem,
    z_send_sem, z_recv_sem, s_send_sem, s_recv_sem,
):
    my_s, my_z = lax.axis_index("space"), lax.axis_index("freq")
    quarter = snap_ref.shape[0] // zs
    sub = quarter // SUBS
    width = 2 * nf
    pieces = quarter // LANES
    here = sub // LANES
    order = list(range(zs // 2, zs)) + list(range(1, zs // 2))
    peers = {k: xor_index(my_z, k, zs) for k in order}
    peers[0] = my_z
    friends = {k: xor_index(my_s, k, ns) for k in range(1, ns)}

    barrier = pltpu.get_barrier_semaphore()
    for k in order:
        pl.semaphore_signal(barrier, inc=1, device_id=(my_s, peers[k]), device_id_type=MESH)
    for k in range(1, ns):
        pl.semaphore_signal(barrier, inc=1, device_id=(friends[k], my_z), device_id_type=MESH)

    loads = {}
    (t0, _), (e0, e1), (l0, l1), (c0, c1) = spans
    constants = [
        pltpu.make_async_copy(const_ref.at[a:b], const.at[a:b], const_sem.at[i])
        for i, (a, b) in enumerate([(t0, e1), (l0, l1), (c0, c1)])
    ] + [
        pltpu.make_async_copy(
            tail_ref.at[pl.ds(pl.multiple_of(my_z * quarter, quarter), quarter)],
            tail_buf, const_sem.at[3],
        ),
    ]
    constants[0].start()
    for s in range(SUBS):
        for k in order + [0]:
            first = pl.multiple_of(peers[k] * quarter + s * sub, sub)
            loads[k, s] = pltpu.make_async_copy(
                snap_ref.at[pl.ds(first, sub)], x_buf.at[k, s], x_sem.at[k, s]
            )
    for k in order:
        loads[k, 0].start()

    ext_row = lax.broadcasted_iota(jnp.int32, (2 * pieces, LANES), 0) // 2

    def folded(x):
        rows = x.shape[0] // 2
        return x[:rows] + x[rows:]

    def transform(k, s):
        return folded(nt_dot(const[t0:e0, : x_buf.shape[3]], x_buf[k, s])).astype(jnp.bfloat16)

    def extras_of(k):
        whole = x_buf[k].reshape(quarter, x_buf.shape[3])
        rows = folded(nt_dot(const[e0:e1, : x_buf.shape[3]], whole))
        extra = jnp.zeros((2 * pieces, LANES), jnp.float32)
        for q in range(pieces):
            extra = jnp.where(ext_row == q, rows[:, q * LANES : (q + 1) * LANES], extra)
        return extra.astype(jnp.bfloat16)

    def started(source, target, send_sems, recv_sems, k):
        copy = pltpu.make_async_remote_copy(
            source, target, send_sems, recv_sems,
            device_id=(my_s, peers[k]), device_id_type=MESH,
        )
        copy.start()
        return copy

    constants[0].wait()
    copies = {}
    for s in range(SUBS):
        for k in order:
            if s < 2:
                loads[k, s].wait()
            send[k, s] = transform(k, s)
            if s == 0 and k == order[0]:
                pl.semaphore_wait(barrier, zs - 1 + ns - 1)
            copies[k, s] = started(
                send.at[k, s], recv.at[my_z, s], send_sem.at[k, s], recv_sem.at[k, s], k
            )
            if s == 0 and k == order[0]:
                for later in range(1, SUBS):
                    for i in order:
                        loads[i, later].start()
                for i in range(SUBS):
                    loads[0, i].start()
                for copy in constants[1:]:
                    copy.start()
        if s == 1:
            for k in order:
                for later in range(2, SUBS):
                    loads[k, later].wait()
                send_ext[k] = extras_of(k)
                copies[k, "ext"] = started(
                    send_ext.at[k], recv_ext.at[my_z], ext_send_sem.at[k], ext_recv_sem.at[k], k
                )
    for s in range(SUBS):
        loads[0, s].wait()
        recv[my_z, s] = transform(0, s)
    recv_ext[my_z] = extras_of(0)
    for copy in constants[1:]:
        copy.wait()
    for s in range(SUBS):
        last = nt_dot(const[l0:l1, : tail_buf.shape[1]], tail_buf[s * sub : (s + 1) * sub])
        rows = last.shape[0] // 2
        last_buf[s] = (last[:rows] + last[rows:]).astype(jnp.bfloat16)

    main_rows = nb * width
    gram = jnp.zeros((width * nb, width * nb), jnp.float32)
    for s in range(SUBS):
        if s == 0:
            for k in order:
                copies[k, "ext"].wait_recv()
        extras = []
        for d in range(zs):
            extra = recv_ext[d]
            extras.append(
                jnp.concatenate(
                    [
                        jnp.where(ext_row == s * here + q, extra, jnp.zeros_like(extra))
                        for q in range(here)
                    ],
                    1,
                )
            )
        rest = jnp.dot(
            const[c0:c1, main_rows:inner],
            jnp.concatenate(extras + [last_buf[s]], 0),
            preferred_element_type=jnp.float32,
        )
        for k in order:
            copies[k, s].wait_recv()
        stacked = jnp.concatenate([recv[d, s] for d in range(zs)], 0)
        coef = rest + jnp.dot(
            const[c0:c1, :main_rows], stacked, preferred_element_type=jnp.float32
        )
        coef = coef.astype(jnp.bfloat16)
        gram = gram + nt_dot(coef, coef)

    side = nf * nb
    real = gram[:side, :side] + gram[side:, side:]
    imag = gram[:side, side:] - gram[side:, :side]
    lane_freq = lax.broadcasted_iota(jnp.int32, (nb, side), 1) // nb
    g_re = jnp.zeros((nb, side), jnp.float32)
    g_im = jnp.zeros((nb, side), jnp.float32)
    for f in range(nf):
        g_re = jnp.where(lane_freq == f, real[f * nb : (f + 1) * nb], g_re)
        g_im = jnp.where(lane_freq == f, imag[f * nb : (f + 1) * nb], g_im)
    group = FREQ_DEV * nb
    lane = lax.broadcasted_iota(jnp.int32, (nb, side), 1)
    packed = []
    for z in range(zs):
        re = pltpu.roll(g_re, (LANES - z * group) % LANES, 1) if z else g_re
        im = pltpu.roll(g_im, (LANES + group - z * group) % LANES, 1) if z != 1 else g_im
        packed.append(jnp.where(lane < group, re, jnp.where(lane < 2 * group, im, 0.0)) * scale)
        z_part[z] = packed[z]

    z_copies = []
    for k in order:
        copy = pltpu.make_async_remote_copy(
            z_part.at[peers[k]], z_recv.at[k], z_send_sem.at[k], z_recv_sem.at[k],
            device_id=(my_s, peers[k]), device_id_type=MESH,
        )
        copy.start()
        z_copies.append(copy)
    total = z_part[my_z]
    for k, copy in zip(order, z_copies):
        copy.wait_recv()
        total = total + z_recv[k]
    s_recv[my_s] = total
    s_copies = []
    for k in range(1, ns):
        copy = pltpu.make_async_remote_copy(
            s_recv.at[my_s], s_recv.at[my_s], s_send_sem.at[k], s_recv_sem.at[k],
            device_id=(friends[k], my_z), device_id_type=MESH,
        )
        copy.start()
        s_copies.append(copy)
    for copy in s_copies:
        copy.wait_recv()
    total = s_recv[0]
    for d in range(1, ns):
        total = total + s_recv[d]
    g_re = jnp.where(lane < group, total, 0.0)
    g_im = jnp.where(lane < group, pltpu.roll(total, LANES - group, 1), 0.0)

    value = leading_value(g_re, g_im, nb)
    row = lax.broadcasted_iota(jnp.int32, (nb, side), 0)
    mine = row == my_s
    row_re = jnp.sum(jnp.where(mine, g_re, 0.0), axis=0, keepdims=True)
    row_im = jnp.sum(jnp.where(mine, g_im, 0.0), axis=0, keepdims=True)
    result = jnp.where(row % 2 == 0, row_re, row_im)
    rows, values = result, value
    for f in range(1, FREQ_DEV):
        rows = jnp.where(row // 2 == f, pltpu.roll(result, LANES - f * nb, 1), rows)
        values = jnp.where(lane == f, pltpu.roll(value, LANES - f * (nb - 1), 1), values)
    gram_ref[...] = rows
    value_ref[...] = values

    for copy in copies.values():
        copy.wait_send()
    for copy in z_copies + s_copies:
        copy.wait_send()


def place_results(gram_ref, value_ref, rows_ref, top_ref):
    rows_ref[...] = gram_ref[:, : rows_ref.shape[1]]
    top_ref[...] = value_ref[0:1, : top_ref.shape[1]]


def shards_kernel(zs, ns, snapshots, tail):
    points, steps = snapshots.shape
    nf = FREQ_DEV * zs
    nb = 2 * zs
    sub = points // zs // SUBS
    pieces = points // zs // LANES
    width = 2 * nf
    table, ext_table, tail_table = make_tables(nf, pieces)
    combine = make_combine(nf, nb, pieces)
    window = 0.5 - 0.5 * np.cos(2.0 * np.pi * np.arange(NFFT) / NFFT)
    scale = float(1.0 / (points * ns * np.sum(window * window)))
    parts = [table, ext_table, tail_table, combine]
    inner = combine.shape[1]
    padded = -(-inner // LANES) * LANES
    const = np.concatenate([np.pad(p, ((0, 0), (0, padded - p.shape[1]))) for p in parts], 0)
    ends = np.cumsum([p.shape[0] for p in parts]).tolist()
    spans = list(zip([0] + ends[:-1], ends))
    dma = pltpu.SemaphoreType.DMA
    flops = 2 * points * steps * table.shape[0]
    gram, values = pl.pallas_call(
        functools.partial(kernel, zs, ns, nf, nb, scale, spans, inner),
        out_shape=[jax.ShapeDtypeStruct((nb, LANES), jnp.float32)] * 2,
        in_specs=[pl.BlockSpec(memory_space=pltpu.HBM)] * 3,
        out_specs=[pl.BlockSpec(memory_space=pltpu.VMEM)] * 2,
        scratch_shapes=[
            pltpu.VMEM((zs, SUBS, sub, steps), jnp.bfloat16),
            pltpu.VMEM((points // zs, tail.shape[1]), jnp.bfloat16),
            pltpu.VMEM((SUBS, tail_table.shape[0] // 2, sub), jnp.bfloat16),
            pltpu.VMEM(const.shape, jnp.bfloat16),
            pltpu.VMEM((zs, SUBS, 2 * width, sub), jnp.bfloat16),
            pltpu.VMEM((zs, 2 * pieces, LANES), jnp.bfloat16),
            pltpu.VMEM((zs, SUBS, 2 * width, sub), jnp.bfloat16),
            pltpu.VMEM((zs, 2 * pieces, LANES), jnp.bfloat16),
            pltpu.VMEM((zs, nb, LANES), jnp.float32),
            pltpu.VMEM((zs, nb, LANES), jnp.float32),
            pltpu.VMEM((ns, nb, LANES), jnp.float32),
            dma((zs, SUBS)), dma((4,)),
            dma((zs, SUBS)), dma((zs, SUBS)), dma((zs,)), dma((zs,)),
            dma((zs,)), dma((zs,)), dma((ns,)), dma((ns,)),
        ],
        compiler_params=pltpu.CompilerParams(
            collective_id=0, has_side_effects=True, vmem_limit_bytes=55040 * 1024
        ),
        cost_estimate=pl.CostEstimate(
            flops=flops, bytes_accessed=points * steps * 2, transcendentals=0
        ),
    )(snapshots, tail, jnp.asarray(const))
    rows, top = pl.pallas_call(
        place_results,
        out_shape=[
            jax.ShapeDtypeStruct((2 * FREQ_DEV, nb), jnp.float32),
            jax.ShapeDtypeStruct((1, FREQ_DEV), jnp.float32),
        ],
        in_specs=[pl.BlockSpec(memory_space=pltpu.VMEM)] * 2,
        out_specs=[pl.BlockSpec(memory_space=pltpu.VMEM)] * 2,
    )(gram, values)
    return rows.reshape(FREQ_DEV, 2, 1, nb), top.reshape(FREQ_DEV)


def power_of_two(count):
    return count > 1 and count & (count - 1) == 0


def shards(snapshots, tail):
    zs, ns = lax.axis_size("freq"), lax.axis_size("space")
    points, steps = snapshots.shape
    nb = zs * steps // (NFFT // 2)
    packs = FREQ_DEV * zs * nb == LANES and steps == NFFT and nb == ns == 8
    whole = points % (zs * SUBS * LANES) == 0
    if packs and whole and power_of_two(zs) and power_of_two(ns):
        return shards_kernel(zs, ns, snapshots, tail)
    return shards_general(snapshots, tail)


def solution(mesh):
    in_specs = (P("space", "freq"), P("space", None))
    out_specs = (P("freq", None, "space", None), P("freq"))
    return jax.shard_map(shards, mesh=mesh, in_specs=in_specs, out_specs=out_specs, check_vma=False)
```

```python
import functools
import math

import jax
import jax.numpy as jnp
import ml_dtypes
import numpy as np
from jax import lax
from jax.experimental import pallas as pl
from jax.experimental.pallas import tpu as pltpu
from jax.sharding import PartitionSpec as P

FREQ_DEV = 4
NFFT = 256
POWER = 4
LANES = 128
SUBS = 8
MESH = pl.DeviceIdType.MESH


def shifted(value, axis, steps):
    count = lax.axis_size(axis)
    initial, last = (max(0, -steps), min(count, count - steps))
    return lax.ppermute(value, axis, [(source, source + steps) for source in range(initial, last)])


def build_table(count):
    steps = jnp.arange(NFFT, dtype=jnp.int32)
    freqs = jnp.arange(count, dtype=jnp.int32)
    window = 0.5 - 0.5 * jnp.cos(2.0 * math.pi * steps.astype(jnp.float32) / NFFT)
    phase = 2.0 * math.pi * (steps[:, None] * freqs[None, :] % NFFT).astype(jnp.float32) / NFFT
    table = jnp.concatenate(
        [window[:, None] * jnp.cos(phase), -window[:, None] * jnp.sin(phase)], 1
    )
    return (table.astype(jnp.bfloat16), jnp.sum(window * window))


def transform(extended, table):
    points, width = extended.shape
    half = NFFT // 2
    count = width // half - 1
    halves = extended.reshape(points, count + 1, half)
    blocks = jnp.concatenate([halves[:, :-1], halves[:, 1:]], 2)
    coef = jnp.einsum("pbt,tk->bkp", blocks, table, preferred_element_type=jnp.float32)
    return coef.reshape(count, 2, table.shape[1] // 2, points).astype(jnp.bfloat16)


def gram_terms(coef, scale):
    big = jnp.einsum("bcfp,gdfp->fcbdg", coef, coef, preferred_element_type=jnp.float32)
    real = big[:, 0, :, 0, :] + big[:, 1, :, 1, :]
    imag = big[:, 0, :, 1, :] - big[:, 1, :, 0, :]
    return jnp.stack([real, imag], 1) * scale


def apply_matrix(matrix, vector):
    high = lax.Precision.HIGHEST
    m_real, m_imag = (matrix[:, 0], matrix[:, 1])
    v_real, v_imag = (vector[:, 0], vector[:, 1])
    u_real = jnp.einsum("fjk,fk->fj", m_real, v_real, precision=high) - jnp.einsum(
        "fjk,fk->fj", m_imag, v_imag, precision=high
    )
    u_imag = jnp.einsum("fjk,fk->fj", m_real, v_imag, precision=high) + jnp.einsum(
        "fjk,fk->fj", m_imag, v_real, precision=high
    )
    return jnp.stack([u_real, u_imag], 1)


def rescale(product):
    return product / jnp.sqrt(jnp.mean(product * product, axis=(1, 2), keepdims=True) + 1e-06)


def rayleigh(vector, product):
    return jnp.mean(vector * product, axis=(1, 2)) / (
        jnp.mean(vector * vector, axis=(1, 2)) + 1e-06
    )


def shards_general(snapshots, tail):
    points = snapshots.shape[0]
    freq_count = lax.axis_size("freq")
    half = NFFT // 2
    table, wsum = build_table(FREQ_DEV * freq_count)
    scale = 1.0 / (points * lax.axis_size("space") * wsum)
    following = shifted(snapshots[:, :half], "freq", -1)
    is_last = lax.axis_index("freq") == freq_count - 1
    following = jnp.where(is_last, tail, following)
    extended = jnp.concatenate([snapshots, following], 1)
    coef = transform(extended, table)
    regrouped = lax.all_to_all(coef, "freq", split_axis=2, concat_axis=0, tiled=True)
    partial_value = gram_terms(regrouped, scale)
    blocks_all = partial_value.shape[2]
    held = blocks_all // lax.axis_size("space")
    vector = jnp.stack(
        [
            jnp.ones((FREQ_DEV, blocks_all), jnp.float32),
            jnp.zeros((FREQ_DEV, blocks_all), jnp.float32),
        ],
        1,
    )
    total = lax.psum(partial_value, "space")
    for step in range(POWER):
        vector = rescale(apply_matrix(total, vector))
    spectrum = rayleigh(vector, apply_matrix(total, vector))
    gram_rows = lax.dynamic_slice_in_dim(total, lax.axis_index("space") * held, held, 2)
    return (gram_rows, spectrum)


def two_pieces(values):
    high = values.astype(ml_dtypes.bfloat16)
    low = (values - high.astype(np.float64)).astype(ml_dtypes.bfloat16)
    return np.concatenate([high, low], 0)


def half_rows(nf):
    steps = np.arange(NFFT // 2)
    phase = 2.0 * np.pi * (np.arange(nf + 1)[:, None] * steps[None, :] % NFFT) / NFFT
    real, imag = np.cos(phase), -np.sin(phase)
    main = np.concatenate([real[:nf], imag[:nf]], 0)
    main[nf] = real[nf]
    return main, imag[nf : nf + 1]


def make_tables(nf, pieces):
    main, extra = half_rows(nf)
    half = NFFT // 2
    width = 2 * nf
    both = np.zeros((2 * width, NFFT))
    extras = np.zeros((2 * pieces, NFFT))
    for h in range(2):
        both[h * width : (h + 1) * width, h * half : (h + 1) * half] = main
        extras[h::2, h * half : (h + 1) * half] = extra
    last = np.zeros((width + 16, half))
    last[:width] = main
    last[width] = extra[0]
    return two_pieces(both), two_pieces(extras), two_pieces(last)


def make_combine(nf, nb, pieces):
    width = 2 * nf
    main_rows = nb * width
    ext_rows = nb * pieces
    combine = np.zeros((2, nf, nb, main_rows + ext_rows + width + 16))

    def columns(m, f, part):
        if f == nf and part == 1:
            if m == nb:
                return [main_rows + ext_rows + width]
            first = main_rows + m // 2 * 2 * pieces + m % 2
            return [first + 2 * q for q in range(pieces)]
        start = main_rows + ext_rows if m == nb else m * width
        if f == nf:
            return [start + nf]
        if part == 1 and f == 0:
            return []
        return [start + part * nf + f]

    for f in range(nf):
        for b in range(nb):
            for m in (b, b + 1):
                second = m - b
                sign = (-1.0) ** f if second else 1.0
                side = 0.25 if second else -0.25
                for part in range(2):
                    for g, weight in ((f, 0.5), (f - 1, side), (f + 1, side)):
                        flip = -1.0 if g < 0 and part == 1 else 1.0
                        for column in columns(m, abs(g), part):
                            combine[part, f, b, column] += sign * flip * weight
    return combine.reshape(2 * nf * nb, -1).astype(ml_dtypes.bfloat16)


def xor_index(index, other, count):
    result = 0
    bit = 1
    while bit < count:
        digit = lax.rem(index // bit, 2)
        result = result + bit * ((1 - digit) if other & bit else digit)
        bit *= 2
    return result


def nt_dot(left, right):
    return lax.dot_general(
        left, right, (((1,), (1,)), ((), ())), preferred_element_type=jnp.float32
    )


def leading_value(g_re, g_im, nb):
    shape = g_re.shape
    row = lax.broadcasted_iota(jnp.int32, shape, 0)
    lane = lax.broadcasted_iota(jnp.int32, shape, 1)
    entries = 2.0 * nb

    def lane_sum(x):
        step = 1
        while step < nb:
            ahead = pltpu.roll(x, LANES - step, 1)
            behind = pltpu.roll(x, step, 1)
            x = x + jnp.where(lane % (2 * step) < step, ahead, behind)
            step *= 2
        return x

    def row_sum(x):
        return jnp.broadcast_to(jnp.sum(x, axis=0, keepdims=True), shape)

    def to_lanes(v_re, v_im):
        return row_sum(g_re * v_re + g_im * v_im), row_sum(g_re * v_im - g_im * v_re)

    def to_rows(v_re, v_im):
        return lane_sum(g_re * v_re - g_im * v_im), lane_sum(g_re * v_im + g_im * v_re)

    v_re, v_im = jnp.ones(shape, jnp.float32), jnp.zeros(shape, jnp.float32)
    for step in range(POWER):
        if step % 2 == 0:
            u_re, u_im = to_lanes(v_re, v_im)
            scale = lax.rsqrt(lane_sum(u_re * u_re + u_im * u_im) / entries + 1e-06)
            v_re, v_im = u_re, u_im
        else:
            u_re, u_im = to_rows(v_re, v_im)
            u_re, u_im = u_re * scale, u_im * scale
            scale = lax.rsqrt(row_sum(u_re * u_re + u_im * u_im) / entries + 1e-06)
            v_re, v_im = u_re * scale, u_im * scale
    u_re, u_im = to_lanes(v_re, v_im)
    here = lane % nb == row
    across_re = row_sum(jnp.where(here, v_re, 0.0))
    across_im = row_sum(jnp.where(here, v_im, 0.0))
    top = lane_sum(across_re * u_re + across_im * u_im) / entries
    return top / (row_sum(v_re * v_re + v_im * v_im) / entries + 1e-06)


def kernel(
    zs, ns, nf, nb, scale, spans, inner,
    snap_ref, tail_ref, const_ref, gram_ref, value_ref,
    x_buf, tail_buf, last_buf, const,
    send, send_ext, recv, recv_ext, z_part, z_recv, s_recv,
    x_sem, const_sem, send_sem, recv_sem, ext_send_sem, ext_recv_sem,
    z_send_sem, z_recv_sem, s_send_sem, s_recv_sem,
):
    my_s, my_z = lax.axis_index("space"), lax.axis_index("freq")
    quarter = snap_ref.shape[0] // zs
    sub = quarter // SUBS
    width = 2 * nf
    pieces = quarter // LANES
    here = sub // LANES
    order = list(range(zs // 2, zs)) + list(range(1, zs // 2))
    peers = {k: xor_index(my_z, k, zs) for k in order}
    peers[0] = my_z
    friends = {k: xor_index(my_s, k, ns) for k in range(1, ns)}

    barrier = pltpu.get_barrier_semaphore()
    for k in order:
        pl.semaphore_signal(barrier, inc=1, device_id=(my_s, peers[k]), device_id_type=MESH)
    for k in range(1, ns):
        pl.semaphore_signal(barrier, inc=1, device_id=(friends[k], my_z), device_id_type=MESH)

    loads = {}
    (t0, _), (e0, e1), (l0, l1), (c0, c1) = spans
    constants = [
        pltpu.make_async_copy(const_ref.at[a:b], const.at[a:b], const_sem.at[i])
        for i, (a, b) in enumerate([(t0, e1), (l0, l1), (c0, c1)])
    ] + [
        pltpu.make_async_copy(
            tail_ref.at[pl.ds(pl.multiple_of(my_z * quarter, quarter), quarter)],
            tail_buf, const_sem.at[3],
        ),
    ]
    constants[0].start()
    for s in range(SUBS):
        for k in order + [0]:
            first = pl.multiple_of(peers[k] * quarter + s * sub, sub)
            loads[k, s] = pltpu.make_async_copy(
                snap_ref.at[pl.ds(first, sub)], x_buf.at[k, s], x_sem.at[k, s]
            )
    for k in order:
        loads[k, 0].start()

    ext_row = lax.broadcasted_iota(jnp.int32, (2 * pieces, LANES), 0) // 2

    def folded(x):
        rows = x.shape[0] // 2
        return x[:rows] + x[rows:]

    def transform(k, s):
        return folded(nt_dot(const[t0:e0, : x_buf.shape[3]], x_buf[k, s])).astype(jnp.bfloat16)

    def extras_of(k):
        whole = x_buf[k].reshape(quarter, x_buf.shape[3])
        rows = folded(nt_dot(const[e0:e1, : x_buf.shape[3]], whole))
        extra = jnp.zeros((2 * pieces, LANES), jnp.float32)
        for q in range(pieces):
            extra = jnp.where(ext_row == q, rows[:, q * LANES : (q + 1) * LANES], extra)
        return extra.astype(jnp.bfloat16)

    def started(source, target, send_sems, recv_sems, k):
        copy = pltpu.make_async_remote_copy(
            source, target, send_sems, recv_sems,
            device_id=(my_s, peers[k]), device_id_type=MESH,
        )
        copy.start()
        return copy

    constants[0].wait()
    copies = {}
    for s in range(SUBS):
        for k in order:
            if s < 2:
                loads[k, s].wait()
            send[k, s] = transform(k, s)
            if s == 0 and k == order[0]:
                pl.semaphore_wait(barrier, zs - 1 + ns - 1)
            copies[k, s] = started(
                send.at[k, s], recv.at[my_z, s], send_sem.at[k, s], recv_sem.at[k, s], k
            )
            if s == 0 and k == order[0]:
                for later in range(1, SUBS):
                    for i in order:
                        loads[i, later].start()
                for i in range(SUBS):
                    loads[0, i].start()
                for copy in constants[1:]:
                    copy.start()
        if s == 1:
            for k in order:
                for later in range(2, SUBS):
                    loads[k, later].wait()
                send_ext[k] = extras_of(k)
                copies[k, "ext"] = started(
                    send_ext.at[k], recv_ext.at[my_z], ext_send_sem.at[k], ext_recv_sem.at[k], k
                )
    for s in range(SUBS):
        loads[0, s].wait()
        recv[my_z, s] = transform(0, s)
    recv_ext[my_z] = extras_of(0)
    for copy in constants[1:]:
        copy.wait()
    for s in range(SUBS):
        last = nt_dot(const[l0:l1, : tail_buf.shape[1]], tail_buf[s * sub : (s + 1) * sub])
        rows = last.shape[0] // 2
        last_buf[s] = (last[:rows] + last[rows:]).astype(jnp.bfloat16)

    main_rows = nb * width
    gram = jnp.zeros((width * nb, width * nb), jnp.float32)
    for s in range(SUBS):
        if s == 0:
            for k in order:
                copies[k, "ext"].wait_recv()
        extras = []
        for d in range(zs):
            extra = recv_ext[d]
            extras.append(
                jnp.concatenate(
                    [
                        jnp.where(ext_row == s * here + q, extra, jnp.zeros_like(extra))
                        for q in range(here)
                    ],
                    1,
                )
            )
        rest = jnp.dot(
            const[c0:c1, main_rows:inner],
            jnp.concatenate(extras + [last_buf[s]], 0),
            preferred_element_type=jnp.float32,
        )
        for k in order:
            copies[k, s].wait_recv()
        stacked = jnp.concatenate([recv[d, s] for d in range(zs)], 0)
        coef = rest + jnp.dot(
            const[c0:c1, :main_rows], stacked, preferred_element_type=jnp.float32
        )
        coef = coef.astype(jnp.bfloat16)
        gram = gram + nt_dot(coef, coef)

    side = nf * nb
    real = gram[:side, :side] + gram[side:, side:]
    imag = gram[:side, side:] - gram[side:, :side]
    lane_freq = lax.broadcasted_iota(jnp.int32, (nb, side), 1) // nb
    g_re = jnp.zeros((nb, side), jnp.float32)
    g_im = jnp.zeros((nb, side), jnp.float32)
    for f in range(nf):
        g_re = jnp.where(lane_freq == f, real[f * nb : (f + 1) * nb], g_re)
        g_im = jnp.where(lane_freq == f, imag[f * nb : (f + 1) * nb], g_im)
    group = FREQ_DEV * nb
    lane = lax.broadcasted_iota(jnp.int32, (nb, side), 1)
    packed = []
    for z in range(zs):
        re = pltpu.roll(g_re, (LANES - z * group) % LANES, 1) if z else g_re
        im = pltpu.roll(g_im, (LANES + group - z * group) % LANES, 1) if z != 1 else g_im
        packed.append(jnp.where(lane < group, re, jnp.where(lane < 2 * group, im, 0.0)) * scale)
        z_part[z] = packed[z]

    z_copies = []
    for k in order:
        copy = pltpu.make_async_remote_copy(
            z_part.at[peers[k]], z_recv.at[k], z_send_sem.at[k], z_recv_sem.at[k],
            device_id=(my_s, peers[k]), device_id_type=MESH,
        )
        copy.start()
        z_copies.append(copy)
    total = z_part[my_z]
    for k, copy in zip(order, z_copies):
        copy.wait_recv()
        total = total + z_recv[k]
    s_recv[my_s] = total
    s_copies = []
    for k in range(1, ns):
        copy = pltpu.make_async_remote_copy(
            s_recv.at[my_s], s_recv.at[my_s], s_send_sem.at[k], s_recv_sem.at[k],
            device_id=(friends[k], my_z), device_id_type=MESH,
        )
        copy.start()
        s_copies.append(copy)
    for copy in s_copies:
        copy.wait_recv()
    total = s_recv[0]
    for d in range(1, ns):
        total = total + s_recv[d]
    g_re = jnp.where(lane < group, total, 0.0)
    g_im = jnp.where(lane < group, pltpu.roll(total, LANES - group, 1), 0.0)

    value = leading_value(g_re, g_im, nb)
    row = lax.broadcasted_iota(jnp.int32, (nb, side), 0)
    mine = row == my_s
    row_re = jnp.sum(jnp.where(mine, g_re, 0.0), axis=0, keepdims=True)
    row_im = jnp.sum(jnp.where(mine, g_im, 0.0), axis=0, keepdims=True)
    result = jnp.where(row % 2 == 0, row_re, row_im)
    rows, values = result, value
    for f in range(1, FREQ_DEV):
        rows = jnp.where(row // 2 == f, pltpu.roll(result, LANES - f * nb, 1), rows)
        values = jnp.where(lane == f, pltpu.roll(value, LANES - f * (nb - 1), 1), values)
    gram_ref[...] = rows
    value_ref[...] = values

    for copy in copies.values():
        copy.wait_send()
    for copy in z_copies + s_copies:
        copy.wait_send()


def shards_kernel(zs, ns, snapshots, tail):
    points, steps = snapshots.shape
    nf = FREQ_DEV * zs
    nb = 2 * zs
    sub = points // zs // SUBS
    pieces = points // zs // LANES
    width = 2 * nf
    table, ext_table, tail_table = make_tables(nf, pieces)
    combine = make_combine(nf, nb, pieces)
    window = 0.5 - 0.5 * np.cos(2.0 * np.pi * np.arange(NFFT) / NFFT)
    scale = float(1.0 / (points * ns * np.sum(window * window)))
    parts = [table, ext_table, tail_table, combine]
    inner = combine.shape[1]
    padded = -(-inner // LANES) * LANES
    const = np.concatenate([np.pad(p, ((0, 0), (0, padded - p.shape[1]))) for p in parts], 0)
    ends = np.cumsum([p.shape[0] for p in parts]).tolist()
    spans = list(zip([0] + ends[:-1], ends))
    dma = pltpu.SemaphoreType.DMA
    flops = 2 * points * steps * table.shape[0]
    gram, values = pl.pallas_call(
        functools.partial(kernel, zs, ns, nf, nb, scale, spans, inner),
        out_shape=[jax.ShapeDtypeStruct((nb, LANES), jnp.float32)] * 2,
        in_specs=[pl.BlockSpec(memory_space=pltpu.HBM)] * 3,
        out_specs=[pl.BlockSpec(memory_space=pltpu.VMEM)] * 2,
        scratch_shapes=[
            pltpu.VMEM((zs, SUBS, sub, steps), jnp.bfloat16),
            pltpu.VMEM((points // zs, tail.shape[1]), jnp.bfloat16),
            pltpu.VMEM((SUBS, tail_table.shape[0] // 2, sub), jnp.bfloat16),
            pltpu.VMEM(const.shape, jnp.bfloat16),
            pltpu.VMEM((zs, SUBS, 2 * width, sub), jnp.bfloat16),
            pltpu.VMEM((zs, 2 * pieces, LANES), jnp.bfloat16),
            pltpu.VMEM((zs, SUBS, 2 * width, sub), jnp.bfloat16),
            pltpu.VMEM((zs, 2 * pieces, LANES), jnp.bfloat16),
            pltpu.VMEM((zs, nb, LANES), jnp.float32),
            pltpu.VMEM((zs, nb, LANES), jnp.float32),
            pltpu.VMEM((ns, nb, LANES), jnp.float32),
            dma((zs, SUBS)), dma((4,)),
            dma((zs, SUBS)), dma((zs, SUBS)), dma((zs,)), dma((zs,)),
            dma((zs,)), dma((zs,)), dma((ns,)), dma((ns,)),
        ],
        compiler_params=pltpu.CompilerParams(
            collective_id=0, has_side_effects=True, vmem_limit_bytes=55040 * 1024
        ),
        cost_estimate=pl.CostEstimate(
            flops=flops, bytes_accessed=points * steps * 2, transcendentals=0
        ),
    )(snapshots, tail, jnp.asarray(const))
    return gram[:, :nb].reshape(FREQ_DEV, 2, 1, nb), values[0, :FREQ_DEV]


def power_of_two(count):
    return count > 1 and count & (count - 1) == 0


def shards(snapshots, tail):
    zs, ns = lax.axis_size("freq"), lax.axis_size("space")
    points, steps = snapshots.shape
    nb = zs * steps // (NFFT // 2)
    packs = FREQ_DEV * zs * nb == LANES and steps == NFFT and nb == ns == 8
    whole = points % (zs * SUBS * LANES) == 0
    if packs and whole and power_of_two(zs) and power_of_two(ns):
        return shards_kernel(zs, ns, snapshots, tail)
    return shards_general(snapshots, tail)


def solution(mesh):
    in_specs = (P("space", "freq"), P("space", None))
    out_specs = (P("freq", None, "space", None), P("freq"))
    return jax.shard_map(shards, mesh=mesh, in_specs=in_specs, out_specs=out_specs, check_vma=False)
```
